32 devices in a mesh: gx: 8 (over z, y), gy: 4 (over x, core).
Axes of the slice: x: 2, y: 2, z: 4, core: 2. Of those that a mesh axis runs over, the one named last changes fastest.
Arguments:
- mass_per_volume: float32 [1024, 2048], P('gy', 'gx'), may hold values from 0.5 to 2
- motion_speed: float32 [1024, 3, 2048], P('gy', None, 'gx'), may hold values from -3 to 3
- agitation_energy: float32 [1024, 2048], P('gy', 'gx'), may hold values from 0.5 to 2
- shear_deviatoric: float32 [1024, 5, 2048], P('gy', None, 'gx'), may hold values from -2.4 to 2.4
- thermal_current_array: float32 [1024, 3, 2048], P('gy', None, 'gx'), may hold values from -2.4 to 2.4
Outputs:
- rate: float32 [1024, 13, 2048], P('gy', None, 'gx')
The draws below stay inside these ranges and needn't reach their ends.
All inputs are finite; a program needn't handle non-finite values.
Results may differ from the reference program's by a relative error of at most 0.0043.
The reference program's roundings to bfloat16 on the way (of `grid`) count: a program that leaves them out, or rounds other values in their place, can miss the bound.
Values may be sent and summed in bfloat16 or wider, within the bound.
No kernel may reach another device: no remote copies, remote signals or barrier semaphores. Data moves between devices by JAX's collectives and lax.ppermute only.
A program may use at most 64 MiB of HBM per device.

```python
import math
import jax
import jax.numpy as jnp
from jax import lax

CROSS_NODES = 1024
DOWNFLOW_NODES = 2048


def block_scale(own_key, shape, split, low, top_value):
    def one(position, shards_of):
        heights = jax.random.uniform(jax.random.fold_in(jax.random.fold_in(own_key, 6), position), (shards_of,), jnp.float32, low / len(split), top_value / len(split))
        return jnp.repeat(jnp.exp(heights), shape[position] // shards_of).reshape((-1,) + (1,) * (len(shape) - position - 1))

    factor_of = one(*split[0])
    for cut in split[1:]:
        factor_of = factor_of * one(*cut)
    return factor_of


def gaussian(own_key, dims, scale, limit, cuts=(), held_as=jnp.bfloat16):
    drawn = scale * jax.random.normal(own_key, dims, jnp.float32)
    if cuts:
        drawn = drawn * block_scale(own_key, dims, cuts, -0.22, 0.18)
    return jnp.clip(drawn, -limit, limit).astype(held_as)


def setup_inputs(seed: int = 0) -> dict:
    streams_of = jax.random.split(jax.random.key(seed), 6)
    return {
        "mass_per_volume": jnp.clip(0.5 + 1.5 * jax.random.uniform(streams_of[0], (CROSS_NODES, DOWNFLOW_NODES), jnp.float32) ** block_scale(streams_of[0], (CROSS_NODES, DOWNFLOW_NODES), ((0, 4), (1, 8)), -0.2, 0.2), 0.5, 2.0),
        "motion_speed": gaussian(streams_of[1], (CROSS_NODES, 3, DOWNFLOW_NODES), 0.5, 3.0, ((0, 4), (2, 8)), jnp.float32),
        "agitation_energy": jnp.clip(0.5 + 1.5 * jax.random.uniform(streams_of[2], (CROSS_NODES, DOWNFLOW_NODES), jnp.float32) ** block_scale(streams_of[2], (CROSS_NODES, DOWNFLOW_NODES), ((0, 4), (1, 8)), -0.2, 0.2), 0.5, 2.0),
        "shear_deviatoric": gaussian(streams_of[3], (CROSS_NODES, 5, DOWNFLOW_NODES), 0.4, 2.4, ((0, 4), (2, 8)), jnp.float32),
        "thermal_current_array": gaussian(streams_of[4], (CROSS_NODES, 3, DOWNFLOW_NODES), 0.4, 2.4, ((0, 4), (2, 8)), jnp.float32),
    }


time_step = 0.05
enforcement_weight = 4.0
plate_speed = 0.5
dissipation_speed = 0.25

def derivative_rows(first, count, size):
    last = size - 1
    half = math.pi / (2.0 * last)
    rows = first + jnp.arange(count, dtype=jnp.int32)
    cols = jnp.arange(size, dtype=jnp.int32)
    summed = (rows[:, None] + cols[None, :]).astype(jnp.float32)
    differ = rows[:, None] - cols[None, :]
    same = differ == 0
    denom = -2.0 * jnp.sin(half * summed) * jnp.sin(half * differ.astype(jnp.float32))
    safe = jnp.where(same, jnp.float32(1.0), denom)

    def weights(index):
        edge = jnp.where((index == 0) | (index == last), jnp.float32(2.0), jnp.float32(1.0))
        parity = (1 - 2 * (index % 2)).astype(jnp.float32)
        return edge * parity
    ratio = weights(rows)[:, None] / weights(cols)[None, :]
    scale = math.pi / last * jnp.sin(2.0 * half * rows.astype(jnp.float32))
    offdiag = jnp.where(same, jnp.float32(0.0), scale[:, None] * ratio / safe)
    diagonal = -lax.optimization_barrier(jnp.sum(offdiag, axis=1))
    return (offdiag + jnp.where(same, diagonal[:, None], jnp.float32(0.0))).astype(jnp.bfloat16)

def fluxes(unknown_collection):
    agitation_energy = unknown_collection[:, 4]
    motion_speed = [unknown_collection[:, 1], unknown_collection[:, 2], unknown_collection[:, 3]]
    traction_matrix = [[unknown_collection[:, 5], unknown_collection[:, 6], unknown_collection[:, 8]], [unknown_collection[:, 6], unknown_collection[:, 7], unknown_collection[:, 9]], [unknown_collection[:, 8], unknown_collection[:, 9], -(unknown_collection[:, 5] + unknown_collection[:, 7])]]
    thermal_current_entry = [unknown_collection[:, 10], unknown_collection[:, 11], unknown_collection[:, 12]]
    pairs = [(0, 0), (0, 1), (1, 1), (0, 2), (1, 2)]
    result = []
    for spatial_axis_number in (0, 1):
        transported_quantity = motion_speed[spatial_axis_number]
        local_quantity = [unknown_collection[:, 0] * transported_quantity]
        for leading_subscript in range(3):
            local_quantity.append(motion_speed[leading_subscript] * transported_quantity + traction_matrix[leading_subscript][spatial_axis_number] + (agitation_energy if leading_subscript == spatial_axis_number else 0.0))
        local_quantity.append(transported_quantity * agitation_energy + 2.0 / 3.0 * thermal_current_entry[spatial_axis_number])
        for leading_subscript, trailing_subscript in pairs:
            production_entry = transported_quantity * traction_matrix[leading_subscript][trailing_subscript]
            production_entry = production_entry + 0.4 * ((thermal_current_entry[leading_subscript] if trailing_subscript == spatial_axis_number else 0.0) + (thermal_current_entry[trailing_subscript] if leading_subscript == spatial_axis_number else 0.0))
            production_entry = production_entry - (4.0 / 15.0 * thermal_current_entry[spatial_axis_number] if leading_subscript == trailing_subscript else 0.0)
            local_quantity.append(production_entry)
        for leading_subscript in range(3):
            local_quantity.append(transported_quantity * thermal_current_entry[leading_subscript] + agitation_energy * traction_matrix[leading_subscript][spatial_axis_number] + (2.5 * agitation_energy * agitation_energy if leading_subscript == spatial_axis_number else 0.0))
        result.append(jnp.stack(local_quantity, axis=1))
    return (result[0], result[1])

def source(unknown_collection, rows, size):
    mass_per_volume = unknown_collection[:, 0]
    agitation_energy = unknown_collection[:, 4]
    impact_often_measure = mass_per_volume * jnp.sqrt(agitation_energy * agitation_energy + 0.25)
    plate_condition = jnp.where(rows == 0, jnp.float32(1.0), jnp.where(rows == size - 1, jnp.float32(-1.0), jnp.float32(0.0)))[:, None]
    radial_distribution = jnp.abs(plate_condition)
    blank_quantity = jnp.zeros_like(mass_per_volume)
    production_entries = [blank_quantity, -enforcement_weight * radial_distribution * (unknown_collection[:, 1] - plate_speed * plate_condition), blank_quantity, blank_quantity, -dissipation_speed * impact_often_measure * agitation_energy - enforcement_weight * radial_distribution * (agitation_energy - 1.0)]
    production_entries = production_entries + [-0.8 * impact_often_measure * unknown_collection[:, k] for k in range(5, 10)]
    production_entries = production_entries + [-0.55 * impact_often_measure * unknown_collection[:, k] for k in range(10, 13)]
    return jnp.stack(production_entries, axis=1)

def section_rate(unknown_collection, grid, rows):
    flux_x, flux_y = fluxes(unknown_collection)
    coeffs = (0.75, -0.15, 1.0 / 60.0)
    along = jnp.zeros_like(flux_x)
    for k in range(3):
        along = along + coeffs[k] * (jnp.roll(flux_x, -(k + 1), axis=2) - jnp.roll(flux_x, k + 1, axis=2))
    lowered = flux_y.astype(jnp.bfloat16)
    across = jnp.dot(grid, lowered.reshape(lowered.shape[0], -1), preferred_element_type=jnp.float32).reshape(unknown_collection.shape)
    return -(along + across) + source(unknown_collection, rows, CROSS_NODES)

def reference(mass_per_volume, motion_speed, agitation_energy, shear_deviatoric, thermal_current_array):
    unknown_collection = jnp.concatenate([mass_per_volume[:, None], motion_speed, agitation_energy[:, None], shear_deviatoric, thermal_current_array], axis=1)
    grid = derivative_rows(0, CROSS_NODES, CROSS_NODES)
    rows = jnp.arange(CROSS_NODES, dtype=jnp.int32)
    first_rate = section_rate(unknown_collection, grid, rows)
    middle = unknown_collection + time_step * first_rate
    second_rate = section_rate(middle, grid, rows)
    return 0.5 * (first_rate + second_rate)
```

```python
import functools
import math

import jax
import jax.numpy as jnp
from jax import lax
from jax.experimental import pallas as pl
from jax.experimental.pallas import tpu as pltpu
from jax.sharding import PartitionSpec as P

time_step = 0.05
enforcement_weight = 4.0
plate_speed = 0.5
dissipation_speed = 0.25
coeffs = (0.75, -0.15, 1.0 / 60.0)

MOMENTS = 13
HALO = 8
RHO, TEMP = 0, 4
VMEM = pl.BlockSpec(memory_space=pltpu.VMEM)
SMEM = pl.BlockSpec(memory_space=pltpu.SMEM)


def params(mib=48):
    return pltpu.CompilerParams(vmem_limit_bytes=mib * 2**20)


def code(f, x):
    if f == RHO:
        return x - 1.25
    if f == TEMP:
        return jnp.exp2(160.0 * (x - 1.25))
    return x


def decode(f, y):
    if f == RHO:
        return y + 1.25
    if f == TEMP:
        return jnp.log2(y) * (1.0 / 160.0) + 1.25
    return y


def flux(u, d, f):
    v = u[1 + d]
    temperature = u[4]
    heat = u[10:13]
    s = [[u[5], u[6], u[8]], [u[6], u[7], u[9]], [u[8], u[9], None]]
    if f == 0:
        return u[0] * v
    if f < 4:
        i = f - 1
        out = u[1 + i] * v + s[i][d]
        return out + temperature if i == d else out
    if f == 4:
        return v * temperature + 2.0 / 3.0 * heat[d]
    if f < 10:
        i, j = ((0, 0), (0, 1), (1, 1), (0, 2), (1, 2))[f - 5]
        out = v * s[i][j]
        weight = {}
        if j == d:
            weight[i] = weight.get(i, 0.0) + 0.4
        if i == d:
            weight[j] = weight.get(j, 0.0) + 0.4
        if i == j:
            weight[d] = weight.get(d, 0.0) - 4.0 / 15.0
        for k, w in weight.items():
            out = out + w * heat[k]
        return out
    i = f - 10
    out = v * heat[i] + temperature * s[i][d]
    return out + 2.5 * temperature * temperature if i == d else out


def sources(u, wall):
    near = jnp.abs(wall)
    nu = u[0] * jnp.sqrt(u[4] * u[4] + 0.25)
    heavy, light = -0.8 * nu, -0.55 * nu
    out = [None] * MOMENTS
    out[1] = -enforcement_weight * near * (u[1] - plate_speed * wall)
    out[4] = -dissipation_speed * nu * u[4] - enforcement_weight * near * (u[4] - 1.0)
    for f in range(5, 10):
        out[f] = heavy * u[f]
    for f in range(10, 13):
        out[f] = light * u[f]
    return out


def along_of(fx):
    count = fx.shape[0]
    total = None
    for k in range(3):
        upper = pltpu.roll(fx, count - (k + 1), 0)
        lower = pltpu.roll(fx, k + 1, 0)
        term = coeffs[k] * (upper - lower)
        total = term if total is None else total + term
    return total


def pack_kernel(n, two, me_ref, rho, vel, temp, stress, heat, *refs):
    if two:
        firsts, (rest, left, right, tall) = refs[:n], refs[n:]
    else:
        firsts, (rest, left, right, tall) = (), refs
    rows, cols = rho.shape
    slab = cols // n
    wide = slab // 2 + 2 * HALO if two else slab + 2 * HALO
    me = me_ref[0]
    tall[0:HALO, :] = jnp.zeros((HALO, rows), jnp.float32)
    tall[HALO + cols :, :] = jnp.zeros((HALO, rows), jnp.float32)
    for f in range(MOMENTS):
        if f == 0:
            x = rho[...]
        elif f < 4:
            x = vel[f - 1]
        elif f == 4:
            x = temp[...]
        elif f < 10:
            x = stress[f - 5]
        else:
            x = heat[f - 10]
        tall[HALO : HALO + cols, :] = code(f, x).T
        left[f] = tall[0 : 2 * HALO, :].astype(jnp.bfloat16)
        right[f] = tall[cols : cols + 2 * HALO, :].astype(jnp.bfloat16)
        for d in range(n):
            start = d * slab
            if two:
                start += 0 if d < n // 2 else wide
                rest[d, f] = tall[start : start + slab // 2, :].astype(jnp.bfloat16)
            else:
                rest[d, f] = tall[start : start + wide, :].astype(jnp.bfloat16)
        for s in range(len(firsts)):
            to = jnp.bitwise_xor(me, s)
            start = to * slab + jnp.where(to < n // 2, slab // 2, 0)
            start = pl.multiple_of(start, 16)
            firsts[s][f] = tall[pl.ds(start, wide), :].astype(jnp.bfloat16)


def patch_kernel(n, me_ref, rest, before, after, *outs):
    me = me_ref[0]
    for s in range(n):
        to = jnp.bitwise_xor(me, s)
        outs[s][...] = rest[to]

        def merge(tile, halo, at_start):
            line = lax.broadcasted_iota(jnp.int32, halo.shape[1:], 0)
            keep = (line < HALO) == at_start
            for f in range(MOMENTS):
                new, old = halo[f].astype(jnp.float32), outs[s][f, tile, :].astype(jnp.float32)
                outs[s][f, tile, :] = jnp.where(keep, new, old).astype(jnp.bfloat16)

        @pl.when(to == 0)
        def _():
            merge(slice(0, 2 * HALO), before, True)

        @pl.when(to == n - 1)
        def _():
            count = outs[s].shape[1]
            merge(slice(count - 2 * HALO, count), after, False)


def grid_kernel(n, rows, me_ref, out, diag):
    size = n * rows
    last = size - 1
    half = math.pi / (2.0 * last)
    me = me_ref[0]
    step = 64 if rows % 64 == 0 else rows

    def weight(index):
        edge = jnp.where((index == 0) | (index == last), 2.0, 1.0)
        return edge * (1 - 2 * (index & 1)).astype(jnp.float32)

    for si in range(n):
        first_i = jnp.bitwise_xor(me, si) * rows
        lanes = pl.ds(si * rows, rows)
        row_i = first_i + lax.broadcasted_iota(jnp.int32, (8, rows), 1)
        angle = half * row_i.astype(jnp.float32)
        sin_i, cos_i = jnp.sin(angle)[0:1], jnp.cos(angle)[0:1]
        front = (-math.pi / last) * sin_i * cos_i * weight(row_i)[0:1]
        diag[...] = jnp.zeros_like(diag)
        for sj in range(n):
            first_j = jnp.bitwise_xor(me, sj) * rows

            def block(t, carry):
                at = t * step
                line = first_j + at
                row_j = line + lax.broadcasted_iota(jnp.int32, (step, 128), 0)
                angle_j = half * row_j.astype(jnp.float32)
                sin_j, cos_j = jnp.sin(angle_j)[:, 0:1], jnp.cos(angle_j)[:, 0:1]
                back = weight(row_j)[:, 0:1]
                back = jnp.where(jnp.abs(back) > 1.5, 0.25 * back, back)
                full_j = line + lax.broadcasted_iota(jnp.int32, (step, rows), 0)
                full_i = first_i + lax.broadcasted_iota(jnp.int32, (step, rows), 1)
                gap = full_i - full_j
                same = gap == 0
                x = half * gap.astype(jnp.float32)
                x2 = x * x
                poly = -1.0 / 39916800.0
                for c in (1 / 362880.0, -1 / 5040.0, 1 / 120.0, -1 / 6.0, 1.0):
                    poly = poly * x2 + c
                minus = x * poly
                plus = sin_i * cos_j + cos_i * sin_j
                denom = jnp.where(same, 1.0, plus * minus)
                off = jnp.where(same, 0.0, front * back / denom)
                diag[...] += jnp.sum(off.reshape(step // 8, 8, rows), axis=0)
                here = pl.ds(pl.multiple_of(sj * rows + at, 16), step)
                out[here, lanes] = off.astype(jnp.bfloat16)
                return carry

            lax.fori_loop(0, rows // step, block, 0)
        total = -jnp.sum(diag[...], axis=0, keepdims=True)
        own = pl.ds(si * rows, rows)
        ij = lax.broadcasted_iota(jnp.int32, (rows, rows), 0)
        ji = lax.broadcasted_iota(jnp.int32, (rows, rows), 1)
        tile = out[own, lanes].astype(jnp.float32)
        out[own, lanes] = jnp.where(ij == ji, total, tile).astype(jnp.bfloat16)


def section_kernel(n, two, second, me_ref, grid, *refs):
    firsts, refs = refs[:n], refs[n:]
    if second:
        rests, refs = refs[:n], refs[n:]
    outs, (u0, u1, r0, fy0, fy1, product) = refs[:n], refs[n:]
    wide, size = u0.shape[1:]
    rows = size // n
    core = wide - 2 * HALO
    me = me_ref[0]
    right_first = me < n // 2
    lane = rows if rows < 128 else 128
    parts = rows // lane

    for s in range(n):
        here = pl.ds(s * rows, rows)
        for f in range(MOMENTS):
            if not second:
                u0[f, :, here] = decode(f, firsts[s][f].astype(jnp.float32))
            else:
                new = rests[s][f].astype(jnp.float32)
                fresh = pl.ds(pl.multiple_of(jnp.where(right_first, 0, 2 * HALO), 16), core)
                u0[f, fresh, here] = decode(f, new)
                src = pl.ds(pl.multiple_of(jnp.where(right_first, 0, core), 16), 2 * HALO)
                dst = pl.ds(pl.multiple_of(jnp.where(right_first, core, 0), 16), 2 * HALO)
                old = firsts[s][f, src, :].astype(jnp.float32)
                u0[f, dst, here] = decode(f, old)

    def walls(s, p, count):
        line = jnp.bitwise_xor(me, s) * rows + p * lane
        line = line + lax.broadcasted_iota(jnp.int32, (count, lane), 1)
        return jnp.where(line == 0, 1.0, jnp.where(line == size - 1, -1.0, 0.0))

    for s in range(n):
        for p in range(parts):
            here = pl.ds(s * rows + p * lane, lane)
            u = [u0[f, :, here] for f in range(MOMENTS)]
            for f in range(MOMENTS):
                fy0[f * wide : (f + 1) * wide, here] = flux(u, 1, f).astype(jnp.bfloat16)

    middle = slice(HALO, HALO + core)
    for s in range(n):
        block = pl.ds(s * rows, rows)
        product[...] = jnp.dot(fy0[...], grid[:, block], preferred_element_type=jnp.float32)
        for p in range(parts):
            here = pl.ds(s * rows + p * lane, lane)
            there = pl.ds(p * lane, lane)
            u = [u0[f, :, here] for f in range(MOMENTS)]
            src = sources(u, walls(s, p, wide))
            new = []
            for f in range(MOMENTS):
                across = product[f * wide : (f + 1) * wide, there]
                rate = -(along_of(flux(u, 0, f)) + across)
                if src[f] is not None:
                    rate = rate + src[f]
                r0[f, :, here] = rate[middle]
                new.append(u[f] + time_step * rate)
                u1[f, :, here] = new[f]
            inner = [x[middle] for x in new]
            for f in range(MOMENTS):
                fy1[f * core : (f + 1) * core, here] = flux(inner, 1, f).astype(jnp.bfloat16)

    for s in range(n):
        block = pl.ds(s * rows, rows)
        product[0 : MOMENTS * core, :] = jnp.dot(
            fy1[...], grid[:, block], preferred_element_type=jnp.float32
        )
        for p in range(parts):
            here = pl.ds(s * rows + p * lane, lane)
            there = pl.ds(p * lane, lane)
            u = [u1[f, :, here] for f in range(MOMENTS)]
            inner = [x[middle] for x in u]
            src = sources(inner, walls(s, p, core))
            for f in range(MOMENTS):
                across = product[f * core : (f + 1) * core, there]
                rate = -(along_of(flux(u, 0, f))[middle] + across)
                if src[f] is not None:
                    rate = rate + src[f]
                rate = 0.5 * (r0[f, :, here] + rate)
                outs[s][f, :, there] = rate.astype(outs[s].dtype)


def unpack_kernel(n, two, me_ref, *refs):
    chunks = [refs[:n], refs[n : 2 * n]] if two else [refs[:n]]
    out, tall = refs[-2:]
    cols = tall.shape[0]
    slab = cols // n
    width = slab // len(chunks)
    me = me_ref[0]
    for f in range(MOMENTS):
        for s in range(n):
            of = jnp.bitwise_xor(me, s)
            for c, arrays in enumerate(chunks):
                start = of * slab
                if two:
                    start += jnp.where(of < n // 2, width * (1 - c), width * c)
                here = pl.ds(pl.multiple_of(start, 16), width)
                tall[here, :] = arrays[s][f].astype(jnp.float32)
        out[f] = tall[...].T


def exchange(arrays, n):
    got = [arrays[0]]
    for s in range(1, n):
        got.append(lax.ppermute(arrays[s], "gy", [(i, i ^ s) for i in range(n)]))
    return got


def on_device(rho, vel, temp, stress, heat):
    rows, cols = rho.shape
    n = lax.axis_size("gy")
    ring = lax.axis_size("gx")
    size, slab = n * rows, cols // n
    two = slab % 32 == 0
    core = slab // 2 if two else slab
    wide = core + 2 * HALO
    half = jnp.bfloat16
    me = lax.axis_index("gy").astype(jnp.int32).reshape(1)
    vel, stress, heat = (jnp.swapaxes(a, 0, 1) for a in (vel, stress, heat))

    def message(width, kind=half):
        return jax.ShapeDtypeStruct((MOMENTS, width, rows), kind)

    spare = core if two else wide
    shapes = [message(wide)] * (n if two else 0)
    shapes += [jax.ShapeDtypeStruct((n, MOMENTS, spare, rows), half)] + [message(2 * HALO)] * 2
    packed = pl.pallas_call(
        functools.partial(pack_kernel, n, two),
        out_shape=shapes,
        in_specs=[SMEM] + [VMEM] * 5,
        out_specs=[VMEM] * len(shapes),
        scratch_shapes=[pltpu.VMEM((cols + 2 * HALO, rows), jnp.float32)],
        compiler_params=params(),
        name="pack",
    )(me, rho, vel, temp, stress, heat)
    rest, left, right = packed[-3:]
    up = [(i, (i + 1) % ring) for i in range(ring)]
    before = lax.ppermute(right, "gx", up)
    after = lax.ppermute(left, "gx", [(j, i) for i, j in up])
    firsts = exchange(packed[:n], n) if two else None

    grid = pl.pallas_call(
        functools.partial(grid_kernel, n, rows),
        out_shape=jax.ShapeDtypeStruct((size, size), half),
        in_specs=[SMEM],
        out_specs=VMEM,
        scratch_shapes=[pltpu.VMEM((8, rows), jnp.float32)],
        compiler_params=params(),
        name="grid",
    )(me)
    rests = pl.pallas_call(
        functools.partial(patch_kernel, n),
        out_shape=[message(spare)] * n,
        in_specs=[SMEM] + [VMEM] * 3,
        out_specs=[VMEM] * n,
        compiler_params=params(),
        name="patch",
    )(me, rest, before, after)
    rests = exchange(rests, n)

    def sections(second, *arrays):
        return pl.pallas_call(
            functools.partial(section_kernel, n, two, second),
            out_shape=[message(core, jnp.float32)] + [message(core)] * (n - 1),
            in_specs=[SMEM] + [VMEM] * (1 + len(arrays)),
            out_specs=[VMEM] * n,
            scratch_shapes=[
                pltpu.VMEM((MOMENTS, wide, size), jnp.float32),
                pltpu.VMEM((MOMENTS, wide, size), jnp.float32),
                pltpu.VMEM((MOMENTS, core, size), jnp.float32),
                pltpu.VMEM((MOMENTS * wide, size), half),
                pltpu.VMEM((MOMENTS * core, size), half),
                pltpu.VMEM((MOMENTS * wide, rows), jnp.float32),
            ],
            compiler_params=params(),
            name="sections",
        )(me, grid, *arrays)

    if two:
        back = exchange(sections(False, *firsts), n)
        back += exchange(sections(True, *firsts, *rests), n)
    else:
        back = exchange(sections(False, *rests), n)
    out = pl.pallas_call(
        functools.partial(unpack_kernel, n, two),
        out_shape=jax.ShapeDtypeStruct((MOMENTS, rows, cols), jnp.float32),
        in_specs=[SMEM] + [VMEM] * len(back),
        out_specs=VMEM,
        scratch_shapes=[pltpu.VMEM((cols, rows), jnp.float32)],
        compiler_params=params(),
        name="unpack",
    )(me, *back)
    return jnp.swapaxes(out, 0, 1)


def solution(mesh):
    return jax.shard_map(
        on_device,
        mesh=mesh,
        in_specs=(
            P("gy", "gx"),
            P("gy", None, "gx"),
            P("gy", "gx"),
            P("gy", None, "gx"),
            P("gy", None, "gx"),
        ),
        out_specs=P("gy", None, "gx"),
        check_vma=False,
    )
```

```python
import functools
import math

import jax
import jax.numpy as jnp
from jax import lax
from jax.experimental import pallas as pl
from jax.experimental.pallas import tpu as pltpu
from jax.sharding import PartitionSpec as P

time_step = 0.05
enforcement_weight = 4.0
plate_speed = 0.5
dissipation_speed = 0.25
coeffs = (0.75, -0.15, 1.0 / 60.0)

MOMENTS = 13
HALO = 8
RHO, TEMP = 0, 4
VMEM = pl.BlockSpec(memory_space=pltpu.VMEM)
HBM = pl.BlockSpec(memory_space=pltpu.HBM)
SMEM = pl.BlockSpec(memory_space=pltpu.SMEM)


def cost(micros):
    return pl.CostEstimate(
        flops=int(micros * 1e9), bytes_accessed=int(micros * 3e6), transcendentals=0
    )


def params(mib=48):
    return pltpu.CompilerParams(vmem_limit_bytes=mib * 2**20)


def code(f, x):
    if f == RHO:
        return x - 1.25
    if f == TEMP:
        return jnp.exp2(160.0 * (x - 1.25))
    return x


def decode(f, y):
    if f == RHO:
        return y + 1.25
    if f == TEMP:
        return jnp.log2(y) * (1.0 / 160.0) + 1.25
    return y


def flux(u, d, f):
    v = u[1 + d]
    temperature = u[4]
    heat = u[10:13]
    s = [[u[5], u[6], u[8]], [u[6], u[7], u[9]], [u[8], u[9], None]]
    if f == 0:
        return u[0] * v
    if f < 4:
        i = f - 1
        out = u[1 + i] * v + s[i][d]
        return out + temperature if i == d else out
    if f == 4:
        return v * temperature + 2.0 / 3.0 * heat[d]
    if f < 10:
        i, j = ((0, 0), (0, 1), (1, 1), (0, 2), (1, 2))[f - 5]
        out = v * s[i][j]
        weight = {}
        if j == d:
            weight[i] = weight.get(i, 0.0) + 0.4
        if i == d:
            weight[j] = weight.get(j, 0.0) + 0.4
        if i == j:
            weight[d] = weight.get(d, 0.0) - 4.0 / 15.0
        for k, w in weight.items():
            out = out + w * heat[k]
        return out
    i = f - 10
    out = v * heat[i] + temperature * s[i][d]
    return out + 2.5 * temperature * temperature if i == d else out


def sources(u, wall):
    near = jnp.abs(wall)
    nu = u[0] * jnp.sqrt(u[4] * u[4] + 0.25)
    heavy, light = -0.8 * nu, -0.55 * nu
    out = [None] * MOMENTS
    out[1] = -enforcement_weight * near * (u[1] - plate_speed * wall)
    out[4] = -dissipation_speed * nu * u[4] - enforcement_weight * near * (u[4] - 1.0)
    for f in range(5, 10):
        out[f] = heavy * u[f]
    for f in range(10, 13):
        out[f] = light * u[f]
    return out


def along_of(fx):
    count = fx.shape[0]
    total = None
    for k in range(3):
        upper = pltpu.roll(fx, count - (k + 1), 0)
        lower = pltpu.roll(fx, k + 1, 0)
        term = coeffs[k] * (upper - lower)
        total = term if total is None else total + term
    return total


def pack_kernel(n, two, me_ref, rho, vel, temp, stress, heat, *refs):
    if two:
        firsts, refs = refs[:n], refs[n:]
    tall, given, strip, arrived = refs
    rows, cols = rho.shape
    slab = cols // n
    wide = slab // 2 + 2 * HALO
    me = me_ref[0]
    copies = []
    for f in range(MOMENTS):
        if f == 0:
            src = rho
        elif f < 4:
            src = vel.at[f - 1]
        elif f == 4:
            src = temp
        elif f < 10:
            src = stress.at[f - 5]
        else:
            src = heat.at[f - 10]
        copies.append(pltpu.make_async_copy(src, given.at[f], arrived.at[f]))
        copies[f].start()
    strip[0:HALO, :] = jnp.zeros((HALO, rows), jnp.float32)
    strip[HALO + cols :, :] = jnp.zeros((HALO, rows), jnp.float32)
    for f in range(MOMENTS):
        copies[f].wait()
        strip[HALO : HALO + cols, :] = code(f, given[f]).T
        tall[f] = strip[...].astype(jnp.bfloat16)
        if two:
            for s in range(n):
                to = jnp.bitwise_xor(me, s)
                start = to * slab + jnp.where(to < n // 2, slab // 2, 0)
                start = pl.multiple_of(start, 16)
                firsts[s][f] = strip[pl.ds(start, wide), :].astype(jnp.bfloat16)


def edge_kernel(tall, left, right):
    cols = tall.shape[1] - 2 * HALO
    left[...] = tall[:, 0 : 2 * HALO, :]
    right[...] = tall[:, cols : cols + 2 * HALO, :]


def rest_kernel(n, two, me_ref, tall, before, after, *outs):
    me = me_ref[0]
    slab = (tall.shape[1] - 2 * HALO) // n
    count = outs[0].shape[1]
    for s in range(n):
        to = jnp.bitwise_xor(me, s)
        start = to * slab
        if two:
            start += jnp.where(to < n // 2, 0, slab // 2 + 2 * HALO)
        start = pl.multiple_of(start, 16)
        for f in range(MOMENTS):
            outs[s][f] = tall[f, pl.ds(start, count), :]

        def merge(tile, halo, at_start):
            line = lax.broadcasted_iota(jnp.int32, halo.shape[1:], 0)
            keep = (line < HALO) == at_start
            for f in range(MOMENTS):
                new, old = halo[f].astype(jnp.float32), outs[s][f, tile, :].astype(jnp.float32)
                outs[s][f, tile, :] = jnp.where(keep, new, old).astype(jnp.bfloat16)

        @pl.when(to == 0)
        def _():
            merge(slice(0, 2 * HALO), before, True)

        @pl.when(to == n - 1)
        def _():
            merge(slice(count - 2 * HALO, count), after, False)


def grid_kernel(n, rows, me_ref, out, sin_col, cos_col, back_col, line_col, total):
    size = n * rows
    last = size - 1
    half = math.pi / (2.0 * last)
    me = me_ref[0]
    step = 64
    lane = min(rows, 128)

    def table(s):
        line = jnp.bitwise_xor(me, s) * rows + lax.broadcasted_iota(jnp.int32, (8, rows), 1)
        angle = half * line.astype(jnp.float32)
        edge = (line == 0) | (line == last)
        sign = (1 - 2 * (line & 1)).astype(jnp.float32)
        return line.astype(jnp.float32), jnp.sin(angle), jnp.cos(angle), edge, sign

    def column(x):
        return jnp.broadcast_to(x[0:1], (lane, rows)).T

    for s in range(n):
        line, sine, cosine, edge, sign = table(s)
        here = pl.ds(s * rows, rows)
        line_col[here, :] = column(line)
        sin_col[here, :] = column(sine)
        cos_col[here, :] = column(cosine)
        back_col[here, :] = column(jnp.where(edge, 0.5 * sign, sign))

    for s in range(n):
        line, sine, cosine, edge, sign = table(s)
        front = (-math.pi / last) * sine * cosine * jnp.where(edge, 2.0 * sign, sign)
        for p in range(rows // lane):
            here = pl.ds(s * rows + p * lane, lane)
            line_i, sin_i, cos_i, front_i = (
                x[0:1, p * lane : (p + 1) * lane] for x in (line, sine, cosine, front)
            )
            total[...] = jnp.zeros_like(total)

            def block(t, carry):
                down = pl.ds(pl.multiple_of(t * step, step), step)
                gap = line_i - line_col[down, :]
                same = gap == 0.0
                x = half * gap
                x2 = x * x
                poly = -1.0 / 39916800.0
                for c in (1 / 362880.0, -1 / 5040.0, 1 / 120.0, -1 / 6.0, 1.0):
                    poly = poly * x2 + c
                plus = sin_i * cos_col[down, :] + cos_i * sin_col[down, :]
                denom = jnp.where(same, 1.0, plus * (x * poly))
                off = jnp.where(same, 0.0, front_i * back_col[down, :] / denom)
                total[...] += jnp.sum(off.reshape(step // 8, 8, lane), axis=0)
                out[down, here] = off.astype(jnp.bfloat16)
                return carry

            lax.fori_loop(0, size // step, block, 0)
            diagonal = -jnp.sum(total[...], axis=0, keepdims=True)
            same = lax.broadcasted_iota(jnp.int32, (lane, lane), 0) == (
                lax.broadcasted_iota(jnp.int32, (lane, lane), 1)
            )
            tile = out[here, here].astype(jnp.float32)
            out[here, here] = jnp.where(same, diagonal, tile).astype(jnp.bfloat16)


def section_kernel(n, two, second, me_ref, grid, *refs):
    firsts, refs = refs[:n], refs[n:]
    if second:
        rests, refs = refs[:n], refs[n + 1 :]
    outs, (u0, u1, r0, fy0, fy1, product) = refs[:n], refs[n:]
    wide, size = u0.shape[1:]
    rows = size // n
    core = wide - 2 * HALO
    me = me_ref[0]
    right_first = me < n // 2
    lane = rows if rows < 128 else 128
    parts = rows // lane

    for s in range(n):
        here = pl.ds(s * rows, rows)
        for f in range(MOMENTS):
            if not second:
                u0[f, :, here] = decode(f, firsts[s][f].astype(jnp.float32))
            else:
                new = rests[s][f].astype(jnp.float32)
                fresh = pl.ds(pl.multiple_of(jnp.where(right_first, 0, 2 * HALO), 16), core)
                u0[f, fresh, here] = decode(f, new)
                src = pl.ds(pl.multiple_of(jnp.where(right_first, 0, core), 16), 2 * HALO)
                dst = pl.ds(pl.multiple_of(jnp.where(right_first, core, 0), 16), 2 * HALO)
                old = firsts[s][f, src, :].astype(jnp.float32)
                u0[f, dst, here] = decode(f, old)

    def walls(s, p, count):
        line = jnp.bitwise_xor(me, s) * rows + p * lane
        line = line + lax.broadcasted_iota(jnp.int32, (count, lane), 1)
        return jnp.where(line == 0, 1.0, jnp.where(line == size - 1, -1.0, 0.0))

    for s in range(n):
        for p in range(parts):
            here = pl.ds(s * rows + p * lane, lane)
            u = [u0[f, :, here] for f in range(MOMENTS)]
            for f in range(MOMENTS):
                fy0[f * wide : (f + 1) * wide, here] = flux(u, 1, f).astype(jnp.bfloat16)

    middle = slice(HALO, HALO + core)
    for s in range(n):
        block = pl.ds(s * rows, rows)
        product[...] = jnp.dot(fy0[...], grid[:, block], preferred_element_type=jnp.float32)
        for p in range(parts):
            here = pl.ds(s * rows + p * lane, lane)
            there = pl.ds(p * lane, lane)
            u = [u0[f, :, here] for f in range(MOMENTS)]
            src = sources(u, walls(s, p, wide))
            new = []
            for f in range(MOMENTS):
                across = product[f * wide : (f + 1) * wide, there]
                rate = -(along_of(flux(u, 0, f)) + across)
                if src[f] is not None:
                    rate = rate + src[f]
                r0[f, :, here] = rate[middle]
                new.append(u[f] + time_step * rate)
                u1[f, :, here] = new[f]
            inner = [x[middle] for x in new]
            for f in range(MOMENTS):
                fy1[f * core : (f + 1) * core, here] = flux(inner, 1, f).astype(jnp.bfloat16)

    for s in range(n):
        block = pl.ds(s * rows, rows)
        product[0 : MOMENTS * core, :] = jnp.dot(
            fy1[...], grid[:, block], preferred_element_type=jnp.float32
        )
        for p in range(parts):
            here = pl.ds(s * rows + p * lane, lane)
            there = pl.ds(p * lane, lane)
            u = [u1[f, :, here] for f in range(MOMENTS)]
            inner = [x[middle] for x in u]
            src = sources(inner, walls(s, p, core))
            for f in range(MOMENTS):
                across = product[f * core : (f + 1) * core, there]
                rate = -(along_of(flux(u, 0, f))[middle] + across)
                if src[f] is not None:
                    rate = rate + src[f]
                rate = 0.5 * (r0[f, :, here] + rate)
                outs[s][f, :, there] = rate.astype(outs[s].dtype)


def unpack_kernel(n, two, me_ref, *refs):
    chunks = [refs[:n], refs[n : 2 * n]] if two else [refs[:n]]
    out, tall = refs[-2:]
    cols = tall.shape[0]
    slab = cols // n
    width = slab // len(chunks)
    me = me_ref[0]
    for f in range(MOMENTS):
        for s in range(n):
            of = jnp.bitwise_xor(me, s)
            for c, arrays in enumerate(chunks):
                start = of * slab
                if two:
                    start += jnp.where(of < n // 2, width * (1 - c), width * c)
                here = pl.ds(pl.multiple_of(start, 16), width)
                tall[here, :] = arrays[s][f].astype(jnp.float32)
        out[f] = tall[...].T


def exchange(arrays, n):
    got = [arrays[0]]
    for s in range(1, n):
        got.append(lax.ppermute(arrays[s], "gy", [(i, i ^ s) for i in range(n)]))
    return got


def on_device(rho, vel, temp, stress, heat):
    rows, cols = rho.shape
    n = lax.axis_size("gy")
    ring = lax.axis_size("gx")
    size, slab = n * rows, cols // n
    two = slab % 32 == 0
    core = slab // 2 if two else slab
    wide = core + 2 * HALO
    half = jnp.bfloat16
    me = lax.axis_index("gy").astype(jnp.int32).reshape(1)
    vel, stress, heat = (jnp.swapaxes(a, 0, 1) for a in (vel, stress, heat))

    def message(width, kind=half):
        return jax.ShapeDtypeStruct((MOMENTS, width, rows), kind)

    count = n if two else 0
    *firsts, tall = pl.pallas_call(
        functools.partial(pack_kernel, n, two),
        out_shape=[message(wide)] * count + [message(cols + 2 * HALO)],
        in_specs=[SMEM] + [HBM] * 5,
        out_specs=[VMEM] * (count + 1),
        scratch_shapes=[
            pltpu.VMEM((MOMENTS, rows, cols), jnp.float32),
            pltpu.VMEM((cols + 2 * HALO, rows), jnp.float32),
            pltpu.SemaphoreType.DMA((MOMENTS,)),
        ],
        compiler_params=params(56),
        cost_estimate=cost(2),
        name="pack",
    )(me, rho, vel, temp, stress, heat)
    if two:
        firsts = exchange(firsts, n)
    left, right = pl.pallas_call(
        edge_kernel,
        out_shape=[message(2 * HALO)] * 2,
        in_specs=[VMEM],
        out_specs=[VMEM] * 2,
        compiler_params=params(),
        cost_estimate=cost(0.2),
        name="edges",
    )(tall)
    up = [(i, (i + 1) % ring) for i in range(ring)]
    before = lax.ppermute(right, "gx", up)
    after = lax.ppermute(left, "gx", [(j, i) for i, j in up])

    lane = min(rows, 128)
    grid = pl.pallas_call(
        functools.partial(grid_kernel, n, rows),
        out_shape=jax.ShapeDtypeStruct((size, size), half),
        in_specs=[SMEM],
        out_specs=VMEM,
        scratch_shapes=[pltpu.VMEM((size, lane), jnp.float32)] * 4
        + [pltpu.VMEM((8, lane), jnp.float32)],
        compiler_params=params(),
        cost_estimate=cost(5),
        name="grid",
    )(me)
    rests = pl.pallas_call(
        functools.partial(rest_kernel, n, two),
        out_shape=[message(core if two else wide)] * n,
        in_specs=[SMEM] + [VMEM] * 3,
        out_specs=[VMEM] * n,
        compiler_params=params(),
        cost_estimate=cost(0.2),
        name="rest",
    )(me, tall, before, after)
    rests = exchange(rests, n)

    def sections(second, *arrays):
        return pl.pallas_call(
            functools.partial(section_kernel, n, two, second),
            out_shape=[message(core, jnp.float32)] + [message(core)] * (n - 1),
            in_specs=[SMEM] + [VMEM] * (2 * n + 1 if second else n + 1) + [HBM] * second,
            out_specs=[VMEM] * n,
            scratch_shapes=[
                pltpu.VMEM((MOMENTS, wide, size), jnp.float32),
                pltpu.VMEM((MOMENTS, wide, size), jnp.float32),
                pltpu.VMEM((MOMENTS, core, size), jnp.float32),
                pltpu.VMEM((MOMENTS * wide, size), half),
                pltpu.VMEM((MOMENTS * core, size), half),
                pltpu.VMEM((MOMENTS * wide, rows), jnp.float32),
            ],
            compiler_params=params(),
            cost_estimate=cost(7),
            name="sections",
        )(me, grid, *arrays)

    if two:
        first = sections(False, *firsts)
        back = exchange(first, n)
        back += exchange(sections(True, *firsts, *rests, first[1]), n)
    else:
        back = exchange(sections(False, *rests), n)
    out = pl.pallas_call(
        functools.partial(unpack_kernel, n, two),
        out_shape=jax.ShapeDtypeStruct((MOMENTS, rows, cols), jnp.float32),
        in_specs=[SMEM] + [VMEM] * len(back),
        out_specs=VMEM,
        scratch_shapes=[pltpu.VMEM((cols, rows), jnp.float32)],
        compiler_params=params(),
        cost_estimate=cost(3),
        name="unpack",
    )(me, *back)
    return jnp.swapaxes(out, 0, 1)


def solution(mesh):
    return jax.shard_map(
        on_device,
        mesh=mesh,
        in_specs=(
            P("gy", "gx"),
            P("gy", None, "gx"),
            P("gy", "gx"),
            P("gy", None, "gx"),
            P("gy", None, "gx"),
        ),
        out_specs=P("gy", None, "gx"),
        check_vma=False,
    )
```

```python
import functools
import math

import jax
import jax.numpy as jnp
from jax import lax
from jax.experimental import pallas as pl
from jax.experimental.pallas import tpu as pltpu
from jax.sharding import PartitionSpec as P

time_step = 0.05
enforcement_weight = 4.0
plate_speed = 0.5
dissipation_speed = 0.25
coeffs = (0.75, -0.15, 1.0 / 60.0)

MOMENTS = 13
HALO = 8
RHO, TEMP = 0, 4
VMEM = pl.BlockSpec(memory_space=pltpu.VMEM)
ANY = pl.BlockSpec(memory_space=pl.ANY)
HBM = pl.BlockSpec(memory_space=pltpu.HBM)
SMEM = pl.BlockSpec(memory_space=pltpu.SMEM)


def cost(micros):
    return pl.CostEstimate(
        flops=int(micros * 1e9), bytes_accessed=int(micros * 3e6), transcendentals=0
    )


def params(mib=48):
    return pltpu.CompilerParams(vmem_limit_bytes=mib * 2**20)


def code(f, x):
    if f == RHO:
        return x - 1.25
    if f == TEMP:
        return jnp.exp2(160.0 * (x - 1.25))
    return x


def decode(f, y):
    if f == RHO:
        return y + 1.25
    if f == TEMP:
        return jnp.log2(y) * (1.0 / 160.0) + 1.25
    return y


def flux(u, d, f):
    v = u[1 + d]
    temperature = u[4]
    heat = u[10:13]
    s = [[u[5], u[6], u[8]], [u[6], u[7], u[9]], [u[8], u[9], None]]
    if f == 0:
        return u[0] * v
    if f < 4:
        i = f - 1
        out = u[1 + i] * v + s[i][d]
        return out + temperature if i == d else out
    if f == 4:
        return v * temperature + 2.0 / 3.0 * heat[d]
    if f < 10:
        i, j = ((0, 0), (0, 1), (1, 1), (0, 2), (1, 2))[f - 5]
        out = v * s[i][j]
        weight = {}
        if j == d:
            weight[i] = weight.get(i, 0.0) + 0.4
        if i == d:
            weight[j] = weight.get(j, 0.0) + 0.4
        if i == j:
            weight[d] = weight.get(d, 0.0) - 4.0 / 15.0
        for k, w in weight.items():
            out = out + w * heat[k]
        return out
    i = f - 10
    out = v * heat[i] + temperature * s[i][d]
    return out + 2.5 * temperature * temperature if i == d else out


def sources(u, wall):
    near = jnp.abs(wall)
    nu = u[0] * jnp.sqrt(u[4] * u[4] + 0.25)
    heavy, light = -0.8 * nu, -0.55 * nu
    out = [None] * MOMENTS
    out[1] = -enforcement_weight * near * (u[1] - plate_speed * wall)
    out[4] = -dissipation_speed * nu * u[4] - enforcement_weight * near * (u[4] - 1.0)
    for f in range(5, 10):
        out[f] = heavy * u[f]
    for f in range(10, 13):
        out[f] = light * u[f]
    return out


def along_of(fx):
    count = fx.shape[0]
    total = None
    for k in range(3):
        upper = pltpu.roll(fx, count - (k + 1), 0)
        lower = pltpu.roll(fx, k + 1, 0)
        term = coeffs[k] * (upper - lower)
        total = term if total is None else total + term
    return total


def pack_kernel(n, two, me_ref, rho, vel, temp, stress, heat, *refs):
    count = n if two else 0
    outs, (strip, given, arrived), refs = refs[: count + 3], refs[count + 3 : count + 6], refs[count + 6 :]
    held, left_at = refs[: count + 3], refs[-1]
    firsts, (tall, left, right) = held[:count], held[count:]
    rows, cols = rho.shape
    slab = cols // n
    wide = slab // 2 + 2 * HALO
    me = me_ref[0]
    copies = []
    for f in range(MOMENTS):
        if f == 0:
            src = rho
        elif f < 4:
            src = vel.at[f - 1]
        elif f == 4:
            src = temp
        elif f < 10:
            src = stress.at[f - 5]
        else:
            src = heat.at[f - 10]
        copies.append(pltpu.make_async_copy(src, given.at[f], arrived.at[f]))
        copies[f].start()
    strip[0:HALO, :] = jnp.zeros((HALO, rows), jnp.float32)
    strip[HALO + cols :, :] = jnp.zeros((HALO, rows), jnp.float32)
    leaving = []
    for f in range(MOMENTS):
        copies[f].wait()
        strip[HALO : HALO + cols, :] = code(f, given[f]).T
        for s in range(count):
            to = jnp.bitwise_xor(me, s)
            start = to * slab + jnp.where(to < n // 2, slab // 2, 0)
            start = pl.multiple_of(start, 16)
            firsts[s][f] = strip[pl.ds(start, wide), :].astype(jnp.bfloat16)
        tall[f] = strip[...].astype(jnp.bfloat16)
        left[f] = tall[f, 0 : 2 * HALO, :]
        right[f] = tall[f, cols : cols + 2 * HALO, :]
        for k, (mine, out) in enumerate(zip(held, outs)):
            copy = pltpu.make_async_copy(mine.at[f], out.at[f], left_at.at[k, f])
            copy.start()
            leaving.append(copy)
    for copy in leaving:
        copy.wait()


def edge_kernel(left, right, after, left_out, right_out):
    left_out[...] = left[...]
    right_out[...] = right[...]


def rest_kernel(n, two, me_ref, tall, before, after, *outs):
    me = me_ref[0]
    slab = (tall.shape[1] - 2 * HALO) // n
    count = outs[0].shape[1]
    for s in range(n):
        to = jnp.bitwise_xor(me, s)
        start = to * slab
        if two:
            start += jnp.where(to < n // 2, 0, slab // 2 + 2 * HALO)
        start = pl.multiple_of(start, 16)
        for f in range(MOMENTS):
            outs[s][f] = tall[f, pl.ds(start, count), :]

        def merge(tile, halo, at_start):
            line = lax.broadcasted_iota(jnp.int32, halo.shape[1:], 0)
            keep = (line < HALO) == at_start
            for f in range(MOMENTS):
                new, old = halo[f].astype(jnp.float32), outs[s][f, tile, :].astype(jnp.float32)
                outs[s][f, tile, :] = jnp.where(keep, new, old).astype(jnp.bfloat16)

        @pl.when(to == 0)
        def _():
            merge(slice(0, 2 * HALO), before, True)

        @pl.when(to == n - 1)
        def _():
            merge(slice(count - 2 * HALO, count), after, False)


def grid_kernel(n, rows, slots, me_ref, out, sin_col, cos_col, back_col, line_col, total):
    size = n * rows
    last = size - 1
    half = math.pi / (2.0 * last)
    me = me_ref[0]
    step = 64
    lane = min(rows, 128)

    def table(s):
        line = jnp.bitwise_xor(me, s) * rows + lax.broadcasted_iota(jnp.int32, (8, rows), 1)
        angle = half * line.astype(jnp.float32)
        edge = (line == 0) | (line == last)
        sign = (1 - 2 * (line & 1)).astype(jnp.float32)
        return line.astype(jnp.float32), jnp.sin(angle), jnp.cos(angle), edge, sign

    def column(x):
        return jnp.broadcast_to(x[0:1], (lane, rows)).T

    for s in range(n):
        line, sine, cosine, edge, sign = table(s)
        here = pl.ds(s * rows, rows)
        line_col[here, :] = column(line)
        sin_col[here, :] = column(sine)
        cos_col[here, :] = column(cosine)
        back_col[here, :] = column(jnp.where(edge, 0.5 * sign, sign))

    for index, s in enumerate(slots):
        line, sine, cosine, edge, sign = table(s)
        front = (-math.pi / last) * sine * cosine * jnp.where(edge, 2.0 * sign, sign)
        for p in range(rows // lane):
            here = pl.ds(index * rows + p * lane, lane)
            own = pl.ds(s * rows + p * lane, lane)
            line_i, sin_i, cos_i, front_i = (
                x[0:1, p * lane : (p + 1) * lane] for x in (line, sine, cosine, front)
            )
            total[...] = jnp.zeros_like(total)

            def block(t, carry):
                down = pl.ds(pl.multiple_of(t * step, step), step)
                gap = line_i - line_col[down, :]
                same = gap == 0.0
                x = half * gap
                x2 = x * x
                poly = -1.0 / 39916800.0
                for c in (1 / 362880.0, -1 / 5040.0, 1 / 120.0, -1 / 6.0, 1.0):
                    poly = poly * x2 + c
                plus = sin_i * cos_col[down, :] + cos_i * sin_col[down, :]
                denom = jnp.where(same, 1.0, plus * (x * poly))
                off = jnp.where(same, 0.0, front_i * back_col[down, :] / denom)
                total[...] += jnp.sum(off.reshape(step // 8, 8, lane), axis=0)
                out[down, here] = off.astype(jnp.bfloat16)
                return carry

            lax.fori_loop(0, size // step, block, 0)
            diagonal = -jnp.sum(total[...], axis=0, keepdims=True)
            same = lax.broadcasted_iota(jnp.int32, (lane, lane), 0) == (
                lax.broadcasted_iota(jnp.int32, (lane, lane), 1)
            )
            tile = out[own, here].astype(jnp.float32)
            out[own, here] = jnp.where(same, diagonal, tile).astype(jnp.bfloat16)


def section_kernel(n, two, second, far, near, me_ref, grid_far, grid_near, *refs):
    firsts, refs = refs[:n], refs[n:]
    if second:
        rests, refs = refs[:n], refs[n + 1 :]
    outs, refs = refs[: len(far)], refs[len(far) :]
    u1, r0, fy1, u0, fy0, product = refs
    wide, size = u0.shape[1:]
    rows = size // n
    core = wide - 2 * HALO
    me = me_ref[0]
    right_first = me < n // 2
    lane = min(rows, 128)
    parts = rows // lane

    for s in range(n):
        here = pl.ds(s * rows, rows)
        for f in range(MOMENTS):
            if not second:
                u0[f, :, here] = decode(f, firsts[s][f].astype(jnp.float32))
            else:
                new = rests[s][f].astype(jnp.float32)
                fresh = pl.ds(pl.multiple_of(jnp.where(right_first, 0, 2 * HALO), 16), core)
                u0[f, fresh, here] = decode(f, new)
                src = pl.ds(pl.multiple_of(jnp.where(right_first, 0, core), 16), 2 * HALO)
                dst = pl.ds(pl.multiple_of(jnp.where(right_first, core, 0), 16), 2 * HALO)
                old = firsts[s][f, src, :].astype(jnp.float32)
                u0[f, dst, here] = decode(f, old)

    for s in range(n):
        for p in range(parts):
            here = pl.ds(s * rows + p * lane, lane)
            u = [u0[f, :, here] for f in range(MOMENTS)]
            for f in range(MOMENTS):
                fy0[f * wide : (f + 1) * wide, here] = flux(u, 1, f).astype(jnp.bfloat16)

    middle = slice(HALO, HALO + core)
    for s in range(n):
        weights = (grid_far, far) if s in far else (grid_near, near)
        block = pl.ds(weights[1].index(s) * rows, rows)
        product[...] = jnp.dot(fy0[...], weights[0][:, block], preferred_element_type=jnp.float32)
        for p in range(parts):
            here = pl.ds(s * rows + p * lane, lane)
            there = pl.ds(p * lane, lane)
            u = [u0[f, :, here] for f in range(MOMENTS)]
            src = sources(u, walls(me, s, p, n, rows, wide))
            new = []
            for f in range(MOMENTS):
                across = product[f * wide : (f + 1) * wide, there]
                rate = -(along_of(flux(u, 0, f)) + across)
                if src[f] is not None:
                    rate = rate + src[f]
                r0[f, :, here] = rate[middle]
                new.append(u[f] + time_step * rate)
                u1[f, :, here] = new[f]
            inner = [x[middle] for x in new]
            for f in range(MOMENTS):
                fy1[f * core : (f + 1) * core, here] = flux(inner, 1, f).astype(jnp.bfloat16)

    finish(n, far, me_ref, grid_far, u1, r0, fy1, outs, product)


def finish_kernel(n, near, chunks, me_ref, grid_near, *refs):
    states, outs, product = refs[: 3 * chunks], refs[-1 - len(near) : -1], refs[-1]
    core = outs[0].shape[1] // chunks
    for c in range(chunks):
        part = [out.at[:, c * core : (c + 1) * core, :] for out in outs]
        finish(n, near, me_ref, grid_near, *states[3 * c : 3 * c + 3], part, product)


def walls(me, s, p, n, rows, count):
    lane = min(rows, 128)
    line = jnp.bitwise_xor(me, s) * rows + p * lane
    line = line + lax.broadcasted_iota(jnp.int32, (count, lane), 1)
    return jnp.where(line == 0, 1.0, jnp.where(line == n * rows - 1, -1.0, 0.0))


def finish(n, slots, me_ref, grid, u1, r0, fy1, outs, product):
    wide, size = u1.shape[1:]
    rows = size // n
    core = wide - 2 * HALO
    lane = min(rows, 128)
    me = me_ref[0]
    middle = slice(HALO, HALO + core)
    for k, s in enumerate(slots):
        block = pl.ds(k * rows, rows)
        product[0 : MOMENTS * core, :] = jnp.dot(
            fy1[...], grid[:, block], preferred_element_type=jnp.float32
        )
        for p in range(rows // lane):
            here = pl.ds(s * rows + p * lane, lane)
            there = pl.ds(p * lane, lane)
            u = [u1[f, :, here] for f in range(MOMENTS)]
            inner = [x[middle] for x in u]
            src = sources(inner, walls(me, s, p, n, rows, core))
            for f in range(MOMENTS):
                across = product[f * core : (f + 1) * core, there]
                rate = -(along_of(flux(u, 0, f))[middle] + across)
                if src[f] is not None:
                    rate = rate + src[f]
                rate = 0.5 * (r0[f, :, here] + rate)
                outs[k][f, :, there] = rate.astype(outs[k].dtype)


def arrived_kernel(*refs):
    refs[-1][...] = jnp.zeros_like(refs[-1])


def unpack_kernel(n, far, near, chunks, me_ref, *refs):
    staying, refs = refs[: len(near)], refs[len(near) :]
    out, tall, held, leaving = refs[-4:]
    cols = tall.shape[0]
    slab = cols // n
    width = slab // chunks
    me = me_ref[0]
    copies = []
    for f in range(MOMENTS):
        for s in near + far:
            of = jnp.bitwise_xor(me, s)
            for c in range(chunks):
                start = of * slab
                if chunks == 2:
                    start += jnp.where(of < n // 2, width * (1 - c), width * c)
                here = pl.ds(pl.multiple_of(start, 16), width)
                if s in near:
                    piece = staying[near.index(s)][f, c * width : (c + 1) * width, :]
                else:
                    piece = refs[c * len(far) + far.index(s)][f]
                tall[here, :] = piece.astype(jnp.float32)
        held[f] = tall[...].T
        copies.append(pltpu.make_async_copy(held.at[f], out.at[f], leaving.at[f]))
        copies[f].start()
    for copy in copies:
        copy.wait()


def to_partner(array, n, s):
    return array if s == 0 else lax.ppermute(array, "gy", [(i, i ^ s) for i in range(n)])


def exchange(arrays, n, slots):
    return [to_partner(array, n, s) for array, s in zip(arrays, slots)]


def on_device(rho, vel, temp, stress, heat):
    rows, cols = rho.shape
    n = lax.axis_size("gy")
    ring = lax.axis_size("gx")
    size, slab = n * rows, cols // n
    two = slab % 32 == 0
    core = slab // 2 if two else slab
    wide = core + 2 * HALO
    half = jnp.bfloat16
    me = lax.axis_index("gy").astype(jnp.int32).reshape(1)
    vel, stress, heat = (jnp.swapaxes(a, 0, 1) for a in (vel, stress, heat))

    def message(width, kind=half):
        return jax.ShapeDtypeStruct((MOMENTS, width, rows), kind)

    count = n if two else 0
    shapes = [message(wide)] * count + [message(cols + 2 * HALO)] + [message(2 * HALO)] * 2
    *firsts, tall, left, right = pl.pallas_call(
        functools.partial(pack_kernel, n, two),
        out_shape=shapes,
        in_specs=[SMEM] + [HBM] * 5,
        out_specs=[ANY] * len(shapes),
        scratch_shapes=[
            pltpu.VMEM((cols + 2 * HALO, rows), jnp.float32),
            pltpu.VMEM((MOMENTS, rows, cols), jnp.float32),
            pltpu.SemaphoreType.DMA((MOMENTS,)),
        ]
        + [pltpu.VMEM(x.shape, x.dtype) for x in shapes]
        + [pltpu.SemaphoreType.DMA((len(shapes), MOMENTS))],
        compiler_params=params(56),
        cost_estimate=cost(2),
        name="pack",
    )(me, rho, vel, temp, stress, heat)
    if two:
        firsts = exchange(firsts, n, range(n))

    lane = min(rows, 128)

    def grid_of(slots):
        return pl.pallas_call(
            functools.partial(grid_kernel, n, rows, slots),
            out_shape=jax.ShapeDtypeStruct((size, len(slots) * rows), half),
            in_specs=[SMEM],
            out_specs=VMEM,
            scratch_shapes=[pltpu.VMEM((size, lane), jnp.float32)] * 4
            + [pltpu.VMEM((8, lane), jnp.float32)],
            compiler_params=params(24),
            cost_estimate=cost(3),
            name="grid",
        )(me)

    far, near = (tuple(range(n // 2, n)), tuple(range(n // 2)))
    grid = {far: grid_of(far)}
    left, right = pl.pallas_call(
        edge_kernel,
        out_shape=[message(2 * HALO)] * 2,
        in_specs=[VMEM] * 2 + [ANY],
        out_specs=[VMEM] * 2,
        compiler_params=params(24),
        cost_estimate=cost(0.2),
        name="edges",
    )(left, right, grid[far])
    up = [(i, (i + 1) % ring) for i in range(ring)]
    before = lax.ppermute(right, "gx", up)
    after = lax.ppermute(left, "gx", [(j, i) for i, j in up])
    grid[near] = grid_of(near)
    rests = pl.pallas_call(
        functools.partial(rest_kernel, n, two),
        out_shape=[message(core if two else wide)] * n,
        in_specs=[SMEM] + [VMEM] * 3,
        out_specs=[VMEM] * n,
        compiler_params=params(),
        cost_estimate=cost(0.2),
        name="rest",
    )(me, tall, before, after)
    rests = exchange(rests, n, range(n))

    def sections(second, *arrays):
        state = [
            jax.ShapeDtypeStruct((MOMENTS, wide, size), jnp.float32),
            jax.ShapeDtypeStruct((MOMENTS, core, size), jnp.float32),
            jax.ShapeDtypeStruct((MOMENTS * core, size), half),
        ]
        *crossing, u1, r0, fy1 = pl.pallas_call(
            functools.partial(section_kernel, n, two, second, far, near),
            out_shape=[message(core)] * len(far) + state,
            in_specs=[SMEM] + [VMEM] * (2 * n + 2 if second else n + 2) + [ANY] * second,
            out_specs=[VMEM] * (len(far) + 3),
            scratch_shapes=[
                pltpu.VMEM((MOMENTS, wide, size), jnp.float32),
                pltpu.VMEM((MOMENTS * wide, size), half),
                pltpu.VMEM((MOMENTS * wide, rows), jnp.float32),
            ],
            compiler_params=params(24),
            cost_estimate=cost(6),
            name="sections",
        )(me, grid[far], grid[near], *arrays)
        return crossing, [u1, r0, fy1]

    def finished(states, *ties):
        return pl.pallas_call(
            functools.partial(finish_kernel, n, near, len(states) // 3),
            out_shape=[message(slab, jnp.float32)] + [message(slab)] * (len(near) - 1),
            in_specs=[SMEM] + [VMEM] * (len(states) + 1) + [ANY] * len(ties),
            out_specs=[VMEM] * len(near),
            scratch_shapes=[pltpu.VMEM((MOMENTS * core, rows), jnp.float32)],
            compiler_params=params(24),
            cost_estimate=cost(4),
            name="finish",
        )(me, grid[near], *states, *ties)

    if two:
        crossing, states = sections(False, *firsts)
        back = exchange(crossing, n, far)
        crossing, more = sections(True, *firsts, *rests, crossing[0])
        staying = finished(states + more, *back)
        back += exchange(crossing, n, far)
    else:
        crossing, states = sections(False, *rests)
        staying = finished(states)
        back = exchange(crossing, n, far)
    staying = exchange(staying, n, near)
    arrived = pl.pallas_call(
        arrived_kernel,
        out_shape=jax.ShapeDtypeStruct((8, 128), jnp.float32),
        in_specs=[ANY] * len(back),
        out_specs=VMEM,
        cost_estimate=cost(6),
        name="arrived",
    )(*back)
    out = pl.pallas_call(
        functools.partial(unpack_kernel, n, far, near, 2 if two else 1),
        out_shape=jax.ShapeDtypeStruct((MOMENTS, rows, cols), jnp.float32),
        in_specs=[SMEM] + [VMEM] * (len(staying) + len(back)) + [ANY],
        out_specs=ANY,
        scratch_shapes=[
            pltpu.VMEM((cols, rows), jnp.float32),
            pltpu.VMEM((MOMENTS, rows, cols), jnp.float32),
            pltpu.SemaphoreType.DMA((MOMENTS,)),
        ],
        compiler_params=params(24),
        cost_estimate=cost(3),
        name="unpack",
    )(me, *staying, *back, arrived)
    return jnp.swapaxes(out, 0, 1)


def solution(mesh):
    return jax.shard_map(
        on_device,
        mesh=mesh,
        in_specs=(
            P("gy", "gx"),
            P("gy", None, "gx"),
            P("gy", "gx"),
            P("gy", None, "gx"),
            P("gy", None, "gx"),
        ),
        out_specs=P("gy", None, "gx"),
        check_vma=False,
    )
```

```python
import functools
import math

import jax
import jax.numpy as jnp
from jax import lax
from jax.experimental import pallas as pl
from jax.experimental.pallas import tpu as pltpu
from jax.sharding import PartitionSpec as P

time_step = 0.05
enforcement_weight = 4.0
plate_speed = 0.5
dissipation_speed = 0.25
coeffs = (0.75, -0.15, 1.0 / 60.0)

MOMENTS = 13
HALO = 8
RHO, TEMP = 0, 4
VMEM = pl.BlockSpec(memory_space=pltpu.VMEM)
ANY = pl.BlockSpec(memory_space=pl.ANY)
HBM = pl.BlockSpec(memory_space=pltpu.HBM)
SMEM = pl.BlockSpec(memory_space=pltpu.SMEM)


def cost(micros):
    return pl.CostEstimate(
        flops=int(micros * 1e9), bytes_accessed=int(micros * 3e6), transcendentals=0
    )


def params(mib=48):
    return pltpu.CompilerParams(vmem_limit_bytes=mib * 2**20)


def code(f, x):
    if f == RHO:
        return x - 1.25
    if f == TEMP:
        return jnp.exp2(160.0 * (x - 1.25))
    return x


def decode(f, y):
    if f == RHO:
        return y + 1.25
    if f == TEMP:
        return jnp.log2(y) * (1.0 / 160.0) + 1.25
    return y


def flux(u, d, f):
    v = u[1 + d]
    temperature = u[4]
    heat = u[10:13]
    s = [[u[5], u[6], u[8]], [u[6], u[7], u[9]], [u[8], u[9], None]]
    if f == 0:
        return u[0] * v
    if f < 4:
        i = f - 1
        out = u[1 + i] * v + s[i][d]
        return out + temperature if i == d else out
    if f == 4:
        return v * temperature + 2.0 / 3.0 * heat[d]
    if f < 10:
        i, j = ((0, 0), (0, 1), (1, 1), (0, 2), (1, 2))[f - 5]
        out = v * s[i][j]
        weight = {}
        if j == d:
            weight[i] = weight.get(i, 0.0) + 0.4
        if i == d:
            weight[j] = weight.get(j, 0.0) + 0.4
        if i == j:
            weight[d] = weight.get(d, 0.0) - 4.0 / 15.0
        for k, w in weight.items():
            out = out + w * heat[k]
        return out
    i = f - 10
    out = v * heat[i] + temperature * s[i][d]
    return out + 2.5 * temperature * temperature if i == d else out


def sources(u, wall):
    near = jnp.abs(wall)
    nu = u[0] * jnp.sqrt(u[4] * u[4] + 0.25)
    heavy, light = -0.8 * nu, -0.55 * nu
    out = [None] * MOMENTS
    out[1] = -enforcement_weight * near * (u[1] - plate_speed * wall)
    out[4] = -dissipation_speed * nu * u[4] - enforcement_weight * near * (u[4] - 1.0)
    for f in range(5, 10):
        out[f] = heavy * u[f]
    for f in range(10, 13):
        out[f] = light * u[f]
    return out


def along_of(fx):
    count = fx.shape[0]
    total = None
    for k in range(3):
        upper = pltpu.roll(fx, count - (k + 1), 0)
        lower = pltpu.roll(fx, k + 1, 0)
        term = coeffs[k] * (upper - lower)
        total = term if total is None else total + term
    return total


GROUPS = ((0, 1), (1, 4), (4, 5), (5, 8), (8, 10), (10, 13))


def pack_kernel(n, two, me_ref, rho, vel, temp, stress, heat, *refs):
    count = n if two else 0
    total = count + 3
    outs, (strip, given, arrived), refs = refs[:total], refs[total : total + 3], refs[total + 3 :]
    held, left_at = refs[:total], refs[-1]
    tall, left, right = held[count:]
    rows, cols = rho.shape
    slab = cols // n
    wide = slab // 2 + 2 * HALO
    me = me_ref[0]
    parts = (rho, vel, temp, stress.at[0:3], stress.at[3:5], heat)
    copies = []
    for k, (first, end) in enumerate(GROUPS):
        dst = given.at[first] if k in (0, 2) else given.at[first:end]
        copies.append(pltpu.make_async_copy(parts[k], dst, arrived.at[k]))
        copies[k].start()
    strip[0:HALO, :] = jnp.zeros((HALO, rows), jnp.float32)
    strip[HALO + cols :, :] = jnp.zeros((HALO, rows), jnp.float32)
    leaving = []

    def leave(k, span, at):
        copy = pltpu.make_async_copy(held[k].at[span], outs[k].at[span], left_at.at[k, at])
        copy.start()
        leaving.append(copy)

    done = 0
    for k, (first, end) in enumerate(GROUPS):
        copies[k].wait()
        for f in range(first, end):
            strip[HALO : HALO + cols, :] = code(f, given[f]).T
            for s in range(count):
                to = jnp.bitwise_xor(me, s)
                start = to * slab + jnp.where(to < n // 2, slab // 2, 0)
                start = pl.multiple_of(start, 16)
                held[s][f] = strip[pl.ds(start, wide), :].astype(jnp.bfloat16)
            tall[f] = strip[...].astype(jnp.bfloat16)
            left[f] = tall[f, 0 : 2 * HALO, :]
            right[f] = tall[f, cols : cols + 2 * HALO, :]
        if k in (1, 3, 5):
            for s in range(count + 1):
                leave(s, slice(done, end), k // 2)
            done = end
    for s in (count + 1, count + 2):
        leave(s, slice(0, MOMENTS), 0)
    for copy in leaving:
        copy.wait()


def edge_kernel(left, right, after, left_out, right_out):
    left_out[...] = left[...]
    right_out[...] = right[...]


def rest_kernel(n, two, me_ref, tall, before, after, *outs):
    me = me_ref[0]
    slab = (tall.shape[1] - 2 * HALO) // n
    count = outs[0].shape[1]
    for s in range(n):
        to = jnp.bitwise_xor(me, s)
        start = to * slab
        if two:
            start += jnp.where(to < n // 2, 0, slab // 2 + 2 * HALO)
        start = pl.multiple_of(start, 16)
        for f in range(MOMENTS):
            outs[s][f] = tall[f, pl.ds(start, count), :]

        def merge(tile, halo, at_start):
            line = lax.broadcasted_iota(jnp.int32, halo.shape[1:], 0)
            keep = (line < HALO) == at_start
            for f in range(MOMENTS):
                new, old = halo[f].astype(jnp.float32), outs[s][f, tile, :].astype(jnp.float32)
                outs[s][f, tile, :] = jnp.where(keep, new, old).astype(jnp.bfloat16)

        @pl.when(to == 0)
        def _():
            merge(slice(0, 2 * HALO), before, True)

        @pl.when(to == n - 1)
        def _():
            merge(slice(count - 2 * HALO, count), after, False)


def grid_kernel(n, rows, slots, me_ref, out, sin_col, cos_col, back_col, line_col, total):
    size = n * rows
    last = size - 1
    half = math.pi / (2.0 * last)
    me = me_ref[0]
    step = 64
    lane = min(rows, 128)

    def table(s):
        line = jnp.bitwise_xor(me, s) * rows + lax.broadcasted_iota(jnp.int32, (8, rows), 1)
        angle = half * line.astype(jnp.float32)
        edge = (line == 0) | (line == last)
        sign = (1 - 2 * (line & 1)).astype(jnp.float32)
        return line.astype(jnp.float32), jnp.sin(angle), jnp.cos(angle), edge, sign

    def column(x):
        return jnp.broadcast_to(x[0:1], (lane, rows)).T

    for s in range(n):
        line, sine, cosine, edge, sign = table(s)
        here = pl.ds(s * rows, rows)
        line_col[here, :] = column(line)
        sin_col[here, :] = column(sine)
        cos_col[here, :] = column(cosine)
        back_col[here, :] = column(jnp.where(edge, 0.5 * sign, sign))

    for index, s in enumerate(slots):
        line, sine, cosine, edge, sign = table(s)
        front = (-math.pi / last) * sine * cosine * jnp.where(edge, 2.0 * sign, sign)
        for p in range(rows // lane):
            here = pl.ds(index * rows + p * lane, lane)
            own = pl.ds(s * rows + p * lane, lane)
            line_i, sin_i, cos_i, front_i = (
                x[0:1, p * lane : (p + 1) * lane] for x in (line, sine, cosine, front)
            )
            total[...] = jnp.zeros_like(total)

            def block(t, carry):
                down = pl.ds(pl.multiple_of(t * step, step), step)
                gap = line_i - line_col[down, :]
                same = gap == 0.0
                x = half * gap
                x2 = x * x
                poly = -1.0 / 39916800.0
                for c in (1 / 362880.0, -1 / 5040.0, 1 / 120.0, -1 / 6.0, 1.0):
                    poly = poly * x2 + c
                plus = sin_i * cos_col[down, :] + cos_i * sin_col[down, :]
                denom = jnp.where(same, 1.0, plus * (x * poly))
                off = jnp.where(same, 0.0, front_i * back_col[down, :] / denom)
                total[...] += jnp.sum(off.reshape(step // 8, 8, lane), axis=0)
                out[down, here] = off.astype(jnp.bfloat16)
                return carry

            lax.fori_loop(0, size // step, block, 0)
            diagonal = -jnp.sum(total[...], axis=0, keepdims=True)
            same = lax.broadcasted_iota(jnp.int32, (lane, lane), 0) == (
                lax.broadcasted_iota(jnp.int32, (lane, lane), 1)
            )
            tile = out[own, here].astype(jnp.float32)
            out[own, here] = jnp.where(same, diagonal, tile).astype(jnp.bfloat16)


def section_kernel(n, two, second, far, near, me_ref, grid_far, grid_near, *refs):
    firsts, refs = refs[:n], refs[n:]
    if second:
        rests, refs = refs[:n], refs[n + 1 :]
    outs, refs = refs[: len(far)], refs[len(far) :]
    u1, r0, fy1, u0, fy0, product = refs
    wide, size = u0.shape[1:]
    rows = size // n
    core = wide - 2 * HALO
    me = me_ref[0]
    right_first = me < n // 2
    lane = min(rows, 128)
    parts = rows // lane

    for s in range(n):
        here = pl.ds(s * rows, rows)
        for f in range(MOMENTS):
            if not second:
                u0[f, :, here] = decode(f, firsts[s][f].astype(jnp.float32))
            else:
                new = rests[s][f].astype(jnp.float32)
                fresh = pl.ds(pl.multiple_of(jnp.where(right_first, 0, 2 * HALO), 16), core)
                u0[f, fresh, here] = decode(f, new)
                src = pl.ds(pl.multiple_of(jnp.where(right_first, 0, core), 16), 2 * HALO)
                dst = pl.ds(pl.multiple_of(jnp.where(right_first, core, 0), 16), 2 * HALO)
                old = firsts[s][f, src, :].astype(jnp.float32)
                u0[f, dst, here] = decode(f, old)

    for s in range(n):
        for p in range(parts):
            here = pl.ds(s * rows + p * lane, lane)
            u = [u0[f, :, here] for f in range(MOMENTS)]
            for f in range(MOMENTS):
                fy0[f * wide : (f + 1) * wide, here] = flux(u, 1, f).astype(jnp.bfloat16)

    middle = slice(HALO, HALO + core)
    for s in range(n):
        weights = (grid_far, far) if s in far else (grid_near, near)
        block = pl.ds(weights[1].index(s) * rows, rows)
        product[...] = jnp.dot(fy0[...], weights[0][:, block], preferred_element_type=jnp.float32)
        for p in range(parts):
            here = pl.ds(s * rows + p * lane, lane)
            there = pl.ds(p * lane, lane)
            u = [u0[f, :, here] for f in range(MOMENTS)]
            src = sources(u, walls(me, s, p, n, rows, wide))
            new = []
            for f in range(MOMENTS):
                across = product[f * wide : (f + 1) * wide, there]
                rate = -(along_of(flux(u, 0, f)) + across)
                if src[f] is not None:
                    rate = rate + src[f]
                r0[f, :, here] = rate[middle]
                new.append(u[f] + time_step * rate)
                u1[f, :, here] = new[f]
            inner = [x[middle] for x in new]
            for f in range(MOMENTS):
                fy1[f * core : (f + 1) * core, here] = flux(inner, 1, f).astype(jnp.bfloat16)

    finish(n, far, me_ref, grid_far, u1, r0, fy1, outs, product)


def finish_kernel(n, near, chunks, me_ref, grid_near, *refs):
    states, outs, product = refs[: 3 * chunks], refs[-1 - len(near) : -1], refs[-1]
    core = outs[0].shape[1] // chunks
    for c in range(chunks):
        part = [out.at[:, c * core : (c + 1) * core, :] for out in outs]
        finish(n, near, me_ref, grid_near, *states[3 * c : 3 * c + 3], part, product)


def walls(me, s, p, n, rows, count):
    lane = min(rows, 128)
    line = jnp.bitwise_xor(me, s) * rows + p * lane
    line = line + lax.broadcasted_iota(jnp.int32, (count, lane), 1)
    return jnp.where(line == 0, 1.0, jnp.where(line == n * rows - 1, -1.0, 0.0))


def finish(n, slots, me_ref, grid, u1, r0, fy1, outs, product):
    wide, size = u1.shape[1:]
    rows = size // n
    core = wide - 2 * HALO
    lane = min(rows, 128)
    me = me_ref[0]
    middle = slice(HALO, HALO + core)
    for k, s in enumerate(slots):
        block = pl.ds(k * rows, rows)
        product[0 : MOMENTS * core, :] = jnp.dot(
            fy1[...], grid[:, block], preferred_element_type=jnp.float32
        )
        for p in range(rows // lane):
            here = pl.ds(s * rows + p * lane, lane)
            there = pl.ds(p * lane, lane)
            u = [u1[f, :, here] for f in range(MOMENTS)]
            inner = [x[middle] for x in u]
            src = sources(inner, walls(me, s, p, n, rows, core))
            for f in range(MOMENTS):
                across = product[f * core : (f + 1) * core, there]
                rate = -(along_of(flux(u, 0, f))[middle] + across)
                if src[f] is not None:
                    rate = rate + src[f]
                rate = 0.5 * (r0[f, :, here] + rate)
                outs[k][f, :, there] = rate.astype(outs[k].dtype)


def arrived_kernel(*refs):
    refs[-1][...] = jnp.zeros_like(refs[-1])


def unpack_kernel(n, far, near, chunks, me_ref, *refs):
    staying, refs = refs[: len(near)], refs[len(near) :]
    out, tall, held, leaving = refs[-4:]
    cols = tall.shape[0]
    slab = cols // n
    width = slab // chunks
    me = me_ref[0]
    copies = []
    for f in range(MOMENTS):
        for s in near + far:
            of = jnp.bitwise_xor(me, s)
            for c in range(chunks):
                start = of * slab
                if chunks == 2:
                    start += jnp.where(of < n // 2, width * (1 - c), width * c)
                here = pl.ds(pl.multiple_of(start, 16), width)
                if s in near:
                    piece = staying[near.index(s)][f, c * width : (c + 1) * width, :]
                else:
                    piece = refs[c * len(far) + far.index(s)][f]
                tall[here, :] = piece.astype(jnp.float32)
        held[f] = tall[...].T
        copies.append(pltpu.make_async_copy(held.at[f], out.at[f], leaving.at[f]))
        copies[f].start()
    for copy in copies:
        copy.wait()


def to_partner(array, n, s):
    return array if s == 0 else lax.ppermute(array, "gy", [(i, i ^ s) for i in range(n)])


def exchange(arrays, n, slots):
    return [to_partner(array, n, s) for array, s in zip(arrays, slots)]


def on_device(rho, vel, temp, stress, heat):
    rows, cols = rho.shape
    n = lax.axis_size("gy")
    ring = lax.axis_size("gx")
    size, slab = n * rows, cols // n
    two = slab % 32 == 0
    core = slab // 2 if two else slab
    wide = core + 2 * HALO
    half = jnp.bfloat16
    me = lax.axis_index("gy").astype(jnp.int32).reshape(1)
    vel, stress, heat = (jnp.swapaxes(a, 0, 1) for a in (vel, stress, heat))

    def message(width, kind=half):
        return jax.ShapeDtypeStruct((MOMENTS, width, rows), kind)

    shapes = [message(wide)] * n if two else []
    shapes += [message(cols + 2 * HALO)] + [message(2 * HALO)] * 2
    *firsts, tall, left, right = pl.pallas_call(
        functools.partial(pack_kernel, n, two),
        out_shape=shapes,
        in_specs=[SMEM] + [HBM] * 5,
        out_specs=[ANY] * len(shapes),
        scratch_shapes=[
            pltpu.VMEM((cols + 2 * HALO, rows), jnp.float32),
            pltpu.VMEM((MOMENTS, rows, cols), jnp.float32),
            pltpu.SemaphoreType.DMA((len(GROUPS),)),
        ]
        + [pltpu.VMEM(x.shape, x.dtype) for x in shapes]
        + [pltpu.SemaphoreType.DMA((len(shapes), 3))],
        compiler_params=params(56),
        cost_estimate=cost(2),
        name="pack",
    )(me, rho, vel, temp, stress, heat)
    if two:
        firsts = exchange(firsts, n, range(n))

    lane = min(rows, 128)

    def grid_of(slots):
        return pl.pallas_call(
            functools.partial(grid_kernel, n, rows, slots),
            out_shape=jax.ShapeDtypeStruct((size, len(slots) * rows), half),
            in_specs=[SMEM],
            out_specs=VMEM,
            scratch_shapes=[pltpu.VMEM((size, lane), jnp.float32)] * 4
            + [pltpu.VMEM((8, lane), jnp.float32)],
            compiler_params=params(24),
            cost_estimate=cost(3),
            name="grid",
        )(me)

    far, near = (tuple(range(n // 2, n)), tuple(range(n // 2)))
    grid = {far: grid_of(far)}
    left, right = pl.pallas_call(
        edge_kernel,
        out_shape=[message(2 * HALO)] * 2,
        in_specs=[VMEM] * 2 + [ANY],
        out_specs=[VMEM] * 2,
        compiler_params=params(24),
        cost_estimate=cost(0.2),
        name="edges",
    )(left, right, grid[far])
    up = [(i, (i + 1) % ring) for i in range(ring)]
    before = lax.ppermute(right, "gx", up)
    after = lax.ppermute(left, "gx", [(j, i) for i, j in up])
    grid[near] = grid_of(near)
    rests = pl.pallas_call(
        functools.partial(rest_kernel, n, two),
        out_shape=[message(core if two else wide)] * n,
        in_specs=[SMEM] + [VMEM] * 3,
        out_specs=[VMEM] * n,
        compiler_params=params(),
        cost_estimate=cost(0.2),
        name="rest",
    )(me, tall, before, after)
    rests = exchange(rests, n, range(n))

    def sections(second, *arrays):
        state = [
            jax.ShapeDtypeStruct((MOMENTS, wide, size), jnp.float32),
            jax.ShapeDtypeStruct((MOMENTS, core, size), jnp.float32),
            jax.ShapeDtypeStruct((MOMENTS * core, size), half),
        ]
        *crossing, u1, r0, fy1 = pl.pallas_call(
            functools.partial(section_kernel, n, two, second, far, near),
            out_shape=[message(core)] * len(far) + state,
            in_specs=[SMEM] + [VMEM] * (2 * n + 2 if second else n + 2) + [ANY] * second,
            out_specs=[VMEM] * (len(far) + 3),
            scratch_shapes=[
                pltpu.VMEM((MOMENTS, wide, size), jnp.float32),
                pltpu.VMEM((MOMENTS * wide, size), half),
                pltpu.VMEM((MOMENTS * wide, rows), jnp.float32),
            ],
            compiler_params=params(24),
            cost_estimate=cost(6),
            name="sections",
        )(me, grid[far], grid[near], *arrays)
        return crossing, [u1, r0, fy1]

    def finished(states, *ties):
        return pl.pallas_call(
            functools.partial(finish_kernel, n, near, len(states) // 3),
            out_shape=[message(slab, jnp.float32)] + [message(slab)] * (len(near) - 1),
            in_specs=[SMEM] + [VMEM] * (len(states) + 1) + [ANY] * len(ties),
            out_specs=[VMEM] * len(near),
            scratch_shapes=[pltpu.VMEM((MOMENTS * core, rows), jnp.float32)],
            compiler_params=params(24),
            cost_estimate=cost(4),
            name="finish",
        )(me, grid[near], *states, *ties)

    if two:
        crossing, states = sections(False, *firsts)
        back = exchange(crossing, n, far)
        crossing, more = sections(True, *firsts, *rests, crossing[0])
        staying = finished(states + more, *back)
        back += exchange(crossing, n, far)
    else:
        crossing, states = sections(False, *rests)
        staying = finished(states)
        back = exchange(crossing, n, far)
    staying = exchange(staying, n, near)
    arrived = pl.pallas_call(
        arrived_kernel,
        out_shape=jax.ShapeDtypeStruct((8, 128), jnp.float32),
        in_specs=[ANY] * len(back),
        out_specs=VMEM,
        compiler_params=params(1),
        cost_estimate=cost(6),
        name="arrived",
    )(*back)
    out = pl.pallas_call(
        functools.partial(unpack_kernel, n, far, near, 2 if two else 1),
        out_shape=jax.ShapeDtypeStruct((MOMENTS, rows, cols), jnp.float32),
        in_specs=[SMEM] + [VMEM] * (len(staying) + len(back)) + [ANY],
        out_specs=ANY,
        scratch_shapes=[
            pltpu.VMEM((cols, rows), jnp.float32),
            pltpu.VMEM((MOMENTS, rows, cols), jnp.float32),
            pltpu.SemaphoreType.DMA((MOMENTS,)),
        ],
        compiler_params=params(24),
        cost_estimate=cost(3),
        name="unpack",
    )(me, *staying, *back, arrived)
    return jnp.swapaxes(out, 0, 1)


def solution(mesh):
    return jax.shard_map(
        on_device,
        mesh=mesh,
        in_specs=(
            P("gy", "gx"),
            P("gy", None, "gx"),
            P("gy", "gx"),
            P("gy", None, "gx"),
            P("gy", None, "gx"),
        ),
        out_specs=P("gy", None, "gx"),
        check_vma=False,
    )
```

```python
import functools
import math

import jax
import jax.numpy as jnp
from jax import lax
from jax.experimental import pallas as pl
from jax.experimental.pallas import tpu as pltpu
from jax.sharding import PartitionSpec as P

time_step = 0.05
enforcement_weight = 4.0
plate_speed = 0.5
dissipation_speed = 0.25
coeffs = (0.75, -0.15, 1.0 / 60.0)

MOMENTS = 13
HALO = 8
RHO, TEMP = 0, 4
VMEM = pl.BlockSpec(memory_space=pltpu.VMEM)
ANY = pl.BlockSpec(memory_space=pl.ANY)
HBM = pl.BlockSpec(memory_space=pltpu.HBM)
SMEM = pl.BlockSpec(memory_space=pltpu.SMEM)


def cost(micros):
    return pl.CostEstimate(
        flops=int(micros * 1e9), bytes_accessed=int(micros * 3e6), transcendentals=0
    )


def params(mib=48):
    return pltpu.CompilerParams(vmem_limit_bytes=mib * 2**20)


def code(f, x):
    if f == RHO:
        return x - 1.25
    if f == TEMP:
        return jnp.exp2(160.0 * (x - 1.25))
    return x


def decode(f, y):
    if f == RHO:
        return y + 1.25
    if f == TEMP:
        return jnp.log2(y) * (1.0 / 160.0) + 1.25
    return y


def flux(u, d, f):
    v = u[1 + d]
    temperature = u[4]
    heat = u[10:13]
    s = [[u[5], u[6], u[8]], [u[6], u[7], u[9]], [u[8], u[9], None]]
    if f == 0:
        return u[0] * v
    if f < 4:
        i = f - 1
        out = u[1 + i] * v + s[i][d]
        return out + temperature if i == d else out
    if f == 4:
        return v * temperature + 2.0 / 3.0 * heat[d]
    if f < 10:
        i, j = ((0, 0), (0, 1), (1, 1), (0, 2), (1, 2))[f - 5]
        out = v * s[i][j]
        weight = {}
        if j == d:
            weight[i] = weight.get(i, 0.0) + 0.4
        if i == d:
            weight[j] = weight.get(j, 0.0) + 0.4
        if i == j:
            weight[d] = weight.get(d, 0.0) - 4.0 / 15.0
        for k, w in weight.items():
            out = out + w * heat[k]
        return out
    i = f - 10
    out = v * heat[i] + temperature * s[i][d]
    return out + 2.5 * temperature * temperature if i == d else out


def sources(u, wall):
    near = jnp.abs(wall)
    nu = u[0] * jnp.sqrt(u[4] * u[4] + 0.25)
    heavy, light = -0.8 * nu, -0.55 * nu
    out = [None] * MOMENTS
    out[1] = -enforcement_weight * near * (u[1] - plate_speed * wall)
    out[4] = -dissipation_speed * nu * u[4] - enforcement_weight * near * (u[4] - 1.0)
    for f in range(5, 10):
        out[f] = heavy * u[f]
    for f in range(10, 13):
        out[f] = light * u[f]
    return out


def along_of(fx):
    count = fx.shape[0]
    total = None
    for k in range(3):
        upper = pltpu.roll(fx, count - (k + 1), 0)
        lower = pltpu.roll(fx, k + 1, 0)
        term = coeffs[k] * (upper - lower)
        total = term if total is None else total + term
    return total


def message_start(me, s, slab):
    to = jnp.bitwise_xor(me, s)
    return pl.multiple_of(to * slab + jnp.where(to % 2 == 0, slab // 2, 0), 16)


def pack_kernel(n, moments, ranges, extra, me_ref, *refs):
    inputs, refs = refs[:moments], refs[moments:]
    total = len(ranges) + (3 if extra else 0)
    outs, refs = refs[-2 * total - 4 : -total - 4], refs[-total - 4 :]
    (strip, given, arrived), held, left_at = refs[:3], refs[3 : 3 + total], refs[-1]
    rows, cols = given.shape[1:]
    slab = cols // n
    me = me_ref[0]
    copies, end = [], 0
    for k, src in enumerate(inputs):
        first, end = end, end + (1 if len(src.shape) == 2 else src.shape[0])
        dst = given.at[first] if len(src.shape) == 2 else given.at[first:end]
        copies.append((first, end, pltpu.make_async_copy(src, dst, arrived.at[k])))
        copies[k][2].start()
    strip[0:HALO, :] = jnp.zeros((HALO, rows), jnp.float32)
    strip[HALO + cols :, :] = jnp.zeros((HALO, rows), jnp.float32)
    leaving = []

    def leave(k, first, last, at):
        span = pl.ds(first, last - first)
        copy = pltpu.make_async_copy(held[k].at[span], outs[k].at[span], left_at.at[k, at])
        copy.start()
        leaving.append(copy)

    for at, (first, end, copy) in enumerate(copies):
        copy.wait()
        for f in range(first, end):
            strip[HALO : HALO + cols, :] = code(f, given[f]).T
            for k, (s, low, high) in enumerate(ranges):
                if low <= f < high:
                    wide = held[k].shape[1]
                    here = pl.ds(message_start(me, s, slab), wide)
                    held[k][f - low] = strip[here, :].astype(jnp.bfloat16)
            if extra:
                tall, left, right = held[-3:]
                tall[f] = strip[...].astype(jnp.bfloat16)
                left[f] = tall[f, 0 : 2 * HALO, :]
                right[f] = tall[f, cols : cols + 2 * HALO, :]
        for k, (s, low, high) in enumerate(ranges):
            if max(first, low) < min(end, high):
                leave(k, max(first, low) - low, min(end, high) - low, at)
        if extra and at % 2 == 0:
            leave(total - 3, 0 if at == 0 else copies[at - 1][0], end, at)
    if extra:
        leave(total - 2, 0, MOMENTS, 0)
        leave(total - 1, 0, MOMENTS, 0)
    for copy in leaving:
        copy.wait()


def edge_kernel(left, right, tie, left_out, right_out):
    left_out[...] = left[...]
    right_out[...] = right[...]


def rest_kernel(n, two, me_ref, tall, before, after, *outs):
    me = me_ref[0]
    slab = (tall.shape[1] - 2 * HALO) // n
    count = outs[0].shape[1]
    for s in range(n):
        to = jnp.bitwise_xor(me, s)
        start = to * slab
        if two:
            start += jnp.where(to % 2 == 0, 0, slab // 2 + 2 * HALO)
        start = pl.multiple_of(start, 16)
        for f in range(MOMENTS):
            outs[s][f] = tall[f, pl.ds(start, count), :]

        def merge(tile, halo, at_start):
            line = lax.broadcasted_iota(jnp.int32, halo.shape[1:], 0)
            keep = (line < HALO) == at_start
            for f in range(MOMENTS):
                new, old = halo[f].astype(jnp.float32), outs[s][f, tile, :].astype(jnp.float32)
                outs[s][f, tile, :] = jnp.where(keep, new, old).astype(jnp.bfloat16)

        @pl.when(to == 0)
        def _():
            merge(slice(0, 2 * HALO), before, True)

        @pl.when(to == n - 1)
        def _():
            merge(slice(count - 2 * HALO, count), after, False)


def grid_kernel(n, rows, slots, me_ref, out, sin_col, cos_col, back_col, line_col, total):
    size = n * rows
    last = size - 1
    half = math.pi / (2.0 * last)
    me = me_ref[0]
    step = 64
    lane = min(rows, 128)

    def table(s):
        line = jnp.bitwise_xor(me, s) * rows + lax.broadcasted_iota(jnp.int32, (8, rows), 1)
        angle = half * line.astype(jnp.float32)
        edge = (line == 0) | (line == last)
        sign = (1 - 2 * (line & 1)).astype(jnp.float32)
        return line.astype(jnp.float32), jnp.sin(angle), jnp.cos(angle), edge, sign

    def column(x):
        return jnp.broadcast_to(x[0:1], (lane, rows)).T

    for s in range(n):
        line, sine, cosine, edge, sign = table(s)
        here = pl.ds(s * rows, rows)
        line_col[here, :] = column(line)
        sin_col[here, :] = column(sine)
        cos_col[here, :] = column(cosine)
        back_col[here, :] = column(jnp.where(edge, 0.5 * sign, sign))

    for index, s in enumerate(slots):
        line, sine, cosine, edge, sign = table(s)
        front = (-math.pi / last) * sine * cosine * jnp.where(edge, 2.0 * sign, sign)
        for p in range(rows // lane):
            here = pl.ds(index * rows + p * lane, lane)
            own = pl.ds(s * rows + p * lane, lane)
            line_i, sin_i, cos_i, front_i = (
                x[0:1, p * lane : (p + 1) * lane] for x in (line, sine, cosine, front)
            )
            total[...] = jnp.zeros_like(total)

            def block(t, carry):
                down = pl.ds(pl.multiple_of(t * step, step), step)
                gap = line_i - line_col[down, :]
                same = gap == 0.0
                x = half * gap
                x2 = x * x
                poly = -1.0 / 39916800.0
                for c in (1 / 362880.0, -1 / 5040.0, 1 / 120.0, -1 / 6.0, 1.0):
                    poly = poly * x2 + c
                plus = sin_i * cos_col[down, :] + cos_i * sin_col[down, :]
                denom = jnp.where(same, 1.0, plus * (x * poly))
                off = jnp.where(same, 0.0, front_i * back_col[down, :] / denom)
                total[...] += jnp.sum(off.reshape(step // 8, 8, lane), axis=0)
                out[down, here] = off.astype(jnp.bfloat16)
                return carry

            lax.fori_loop(0, size // step, block, 0)
            diagonal = -jnp.sum(total[...], axis=0, keepdims=True)
            same = lax.broadcasted_iota(jnp.int32, (lane, lane), 0) == (
                lax.broadcasted_iota(jnp.int32, (lane, lane), 1)
            )
            tile = out[own, here].astype(jnp.float32)
            out[own, here] = jnp.where(same, diagonal, tile).astype(jnp.bfloat16)


def weights_of(parts, grids, s, down=slice(None)):
    for part, grid in zip(parts, grids):
        if s in part:
            rows = grid.shape[1] // len(part)
            at = part.index(s) * rows
            return grid[down, at : at + rows]


def flip_kernel(n, parts, far, *refs):
    grids, out = refs[: len(parts)], refs[-1]
    rows = out.shape[0] // n
    line = lax.broadcasted_iota(jnp.int32, (rows, rows), 0)
    turn = line + lax.broadcasted_iota(jnp.int32, (rows, rows), 1) == rows - 1
    turn = jnp.where(turn, 1.0, 0.0).astype(jnp.bfloat16)
    for k, s in enumerate(far):
        for a in range(n):
            down = (a ^ (n - 1)) * rows
            tile = weights_of(parts, grids, s ^ (n - 1), slice(down, down + rows))
            tile = jnp.dot(turn, tile, preferred_element_type=jnp.float32).astype(jnp.bfloat16)
            tile = -jnp.dot(tile, turn, preferred_element_type=jnp.float32)
            out[a * rows : (a + 1) * rows, k * rows : (k + 1) * rows] = tile.astype(jnp.bfloat16)


def section_kernel(n, two, second, far, parts, me_ref, *refs):
    grids, refs = refs[: len(parts)], refs[len(parts) :]
    firsts, refs = refs[:n], refs[n:]
    if second:
        rests, refs = refs[:n], refs[n + 1 :]
    outs, refs = refs[: len(far)], refs[len(far) :]
    u1, r0, fy1, u0, fy0, product = refs
    wide, size = u0.shape[1:]
    rows = size // n
    core = wide - 2 * HALO
    me = me_ref[0]
    right_first = me % 2 == 0
    lane = min(rows, 128)
    strips = rows // lane

    for s in range(n):
        here = pl.ds(s * rows, rows)
        for f in range(MOMENTS):
            if not second:
                u0[f, :, here] = decode(f, firsts[s][f].astype(jnp.float32))
            else:
                new = rests[s][f].astype(jnp.float32)
                fresh = pl.ds(pl.multiple_of(jnp.where(right_first, 0, 2 * HALO), 16), core)
                u0[f, fresh, here] = decode(f, new)
                src = pl.ds(pl.multiple_of(jnp.where(right_first, 0, core), 16), 2 * HALO)
                dst = pl.ds(pl.multiple_of(jnp.where(right_first, core, 0), 16), 2 * HALO)
                old = firsts[s][f, src, :].astype(jnp.float32)
                u0[f, dst, here] = decode(f, old)

    for s in range(n):
        for p in range(strips):
            here = pl.ds(s * rows + p * lane, lane)
            u = [u0[f, :, here] for f in range(MOMENTS)]
            for f in range(MOMENTS):
                fy0[f * wide : (f + 1) * wide, here] = flux(u, 1, f).astype(jnp.bfloat16)

    middle = slice(HALO, HALO + core)
    for s in range(n):
        weights = weights_of(parts, grids, s)
        product[...] = jnp.dot(fy0[...], weights, preferred_element_type=jnp.float32)
        for p in range(strips):
            here = pl.ds(s * rows + p * lane, lane)
            there = pl.ds(p * lane, lane)
            u = [u0[f, :, here] for f in range(MOMENTS)]
            src = sources(u, walls(me, s, p, n, rows, wide))
            new = []
            for f in range(MOMENTS):
                across = product[f * wide : (f + 1) * wide, there]
                rate = -(along_of(flux(u, 0, f)) + across)
                if src[f] is not None:
                    rate = rate + src[f]
                r0[f, :, here] = rate[middle]
                new.append(u[f] + time_step * rate)
                u1[f, :, here] = new[f]
            inner = [x[middle] for x in new]
            for f in range(MOMENTS):
                fy1[f * core : (f + 1) * core, here] = flux(inner, 1, f).astype(jnp.bfloat16)

    finish(n, far, me_ref, parts, grids, u1, r0, fy1, outs, product)


def finish_kernel(n, near, parts, chunks, me_ref, *refs):
    grids, refs = refs[: len(parts)], refs[len(parts) :]
    states, outs, product = refs[: 3 * chunks], refs[-1 - len(near) : -1], refs[-1]
    core = outs[0].shape[1] // chunks
    for c in range(chunks):
        part = [out.at[:, c * core : (c + 1) * core, :] for out in outs]
        finish(n, near, me_ref, parts, grids, *states[3 * c : 3 * c + 3], part, product)


def walls(me, s, p, n, rows, count):
    lane = min(rows, 128)
    line = jnp.bitwise_xor(me, s) * rows + p * lane
    line = line + lax.broadcasted_iota(jnp.int32, (count, lane), 1)
    return jnp.where(line == 0, 1.0, jnp.where(line == n * rows - 1, -1.0, 0.0))


def finish(n, slots, me_ref, parts, grids, u1, r0, fy1, outs, product):
    wide, size = u1.shape[1:]
    rows = size // n
    core = wide - 2 * HALO
    lane = min(rows, 128)
    me = me_ref[0]
    middle = slice(HALO, HALO + core)
    for k, s in enumerate(slots):
        weights = weights_of(parts, grids, s)
        product[0 : MOMENTS * core, :] = jnp.dot(
            fy1[...], weights, preferred_element_type=jnp.float32
        )
        for p in range(rows // lane):
            here = pl.ds(s * rows + p * lane, lane)
            there = pl.ds(p * lane, lane)
            u = [u1[f, :, here] for f in range(MOMENTS)]
            inner = [x[middle] for x in u]
            src = sources(inner, walls(me, s, p, n, rows, core))
            for f in range(MOMENTS):
                across = product[f * core : (f + 1) * core, there]
                rate = -(along_of(flux(u, 0, f))[middle] + across)
                if src[f] is not None:
                    rate = rate + src[f]
                rate = 0.5 * (r0[f, :, here] + rate)
                outs[k][f, :, there] = rate.astype(outs[k].dtype)


def arrived_kernel(*refs):
    refs[-1][...] = jnp.zeros_like(refs[-1])


def unpack_kernel(n, far, near, chunks, me_ref, *refs):
    staying, refs = refs[: len(near)], refs[len(near) :]
    out, tall, held, leaving = refs[-4:]
    cols = tall.shape[0]
    slab = cols // n
    width = slab // chunks
    me = me_ref[0]
    copies = []
    for f in range(MOMENTS):
        for s in near + far:
            of = jnp.bitwise_xor(me, s)
            for c in range(chunks):
                start = of * slab
                if chunks == 2:
                    start += jnp.where(of % 2 == 0, width * (1 - c), width * c)
                here = pl.ds(pl.multiple_of(start, 16), width)
                if s in near:
                    piece = staying[near.index(s)][f, c * width : (c + 1) * width, :]
                else:
                    piece = refs[c * len(far) + far.index(s)][f]
                tall[here, :] = piece.astype(jnp.float32)
        held[f] = tall[...].T
        copies.append(pltpu.make_async_copy(held.at[f], out.at[f], leaving.at[f]))
        copies[f].start()
    for copy in copies:
        copy.wait()


def to_partner(array, n, s):
    return array if s == 0 else lax.ppermute(array, "gy", [(i, i ^ s) for i in range(n)])


def exchange(arrays, n, slots):
    pairs = list(zip(arrays, slots))[::-1]
    return [to_partner(array, n, s) for array, s in pairs][::-1]


def on_device(rho, vel, temp, stress, heat):
    rows, cols = rho.shape
    n = lax.axis_size("gy")
    ring = lax.axis_size("gx")
    size, slab = n * rows, cols // n
    two = slab % 32 == 0
    core = slab // 2 if two else slab
    wide = core + 2 * HALO
    half = jnp.bfloat16
    me = lax.axis_index("gy").astype(jnp.int32).reshape(1)
    vel, stress, heat = (jnp.swapaxes(a, 0, 1) for a in (vel, stress, heat))

    def message(width, kind=half):
        return jax.ShapeDtypeStruct((MOMENTS, width, rows), kind)

    far, near = (tuple(range(n // 2, n)), tuple(range(n // 2)))
    inputs = (rho, vel, temp, stress, heat)

    def pack(arrays, ranges, extra, *ties):
        shapes = [jax.ShapeDtypeStruct((high - low, wide, rows), half) for s, low, high in ranges]
        if extra:
            shapes += [message(cols + 2 * HALO)] + [message(2 * HALO)] * 2
        count = sum(1 if len(a.shape) == 2 else a.shape[0] for a in arrays)
        return pl.pallas_call(
            functools.partial(pack_kernel, n, len(arrays), ranges, extra),
            out_shape=shapes,
            in_specs=[SMEM] + [HBM] * len(arrays) + [ANY] * len(ties),
            out_specs=[ANY] * len(shapes),
            scratch_shapes=[
                pltpu.VMEM((cols + 2 * HALO, rows), jnp.float32),
                pltpu.VMEM((count, rows, cols), jnp.float32),
                pltpu.SemaphoreType.DMA((len(arrays),)),
            ]
            + [pltpu.VMEM(x.shape, x.dtype) for x in shapes]
            + [pltpu.SemaphoreType.DMA((len(shapes), len(arrays)))],
            compiler_params=params(56),
            cost_estimate=cost(0.05),
            name="pack",
        )(me, *arrays, *ties)

    firsts = []
    if two:
        firsts = pack(inputs, tuple((s, 0, MOMENTS) for s in range(n)), False)
        tall, left, right = pack(inputs, (), True, firsts[0])
        firsts = exchange(firsts, n, range(n))
    else:
        tall, left, right = pack(inputs, (), True)

    lane = min(rows, 128)

    def grid_of(slots):
        return pl.pallas_call(
            functools.partial(grid_kernel, n, rows, slots),
            out_shape=jax.ShapeDtypeStruct((size, len(slots) * rows), half),
            in_specs=[SMEM],
            out_specs=VMEM,
            scratch_shapes=[pltpu.VMEM((size, lane), jnp.float32)] * 4
            + [pltpu.VMEM((8, lane), jnp.float32)],
            compiler_params=params(24),
            cost_estimate=cost(0.05),
            name="grid",
        )(me)

    parts = (near[: n // 4], near[n // 4 :])
    grids = [grid_of(part) for part in parts]
    left, right = pl.pallas_call(
        edge_kernel,
        out_shape=[message(2 * HALO)] * 2,
        in_specs=[VMEM] * 2 + [ANY],
        out_specs=[VMEM] * 2,
        compiler_params=params(24),
        cost_estimate=cost(0.01),
        name="edges",
    )(left, right, grids[0])
    up = [(i, (i + 1) % ring) for i in range(ring)]
    before = lax.ppermute(right, "gx", up)
    after = lax.ppermute(left, "gx", [(j, i) for i, j in up])
    turned = pl.pallas_call(
        functools.partial(flip_kernel, n, parts, far),
        out_shape=jax.ShapeDtypeStruct((size, len(far) * rows), half),
        in_specs=[VMEM] * 2,
        out_specs=VMEM,
        compiler_params=params(24),
        cost_estimate=cost(0.02),
        name="flip",
    )(*grids)
    all_parts, all_grids = (*parts, far), (*grids, turned)
    rests = pl.pallas_call(
        functools.partial(rest_kernel, n, two),
        out_shape=[message(core if two else wide)] * n,
        in_specs=[SMEM] + [VMEM] * 3,
        out_specs=[VMEM] * n,
        compiler_params=params(),
        cost_estimate=cost(0.01),
        name="rest",
    )(me, tall, before, after)
    rests = exchange(rests, n, range(n))

    def sections(second, *arrays):
        state = [
            jax.ShapeDtypeStruct((MOMENTS, wide, size), jnp.float32),
            jax.ShapeDtypeStruct((MOMENTS, core, size), jnp.float32),
            jax.ShapeDtypeStruct((MOMENTS * core, size), half),
        ]
        *crossing, u1, r0, fy1 = pl.pallas_call(
            functools.partial(section_kernel, n, two, second, far, all_parts),
            out_shape=[message(core)] * len(far) + state,
            in_specs=[SMEM] + [VMEM] * (len(arrays) + 3 - second) + [ANY] * second,
            out_specs=[VMEM] * (len(far) + 3),
            scratch_shapes=[
                pltpu.VMEM((MOMENTS, wide, size), jnp.float32),
                pltpu.VMEM((MOMENTS * wide, size), half),
                pltpu.VMEM((MOMENTS * wide, rows), jnp.float32),
            ],
            compiler_params=params(24),
            cost_estimate=cost(6),
            name="sections",
        )(me, *all_grids, *arrays)
        return crossing, [u1, r0, fy1]

    def finished(states, *ties):
        return pl.pallas_call(
            functools.partial(finish_kernel, n, near, parts, len(states) // 3),
            out_shape=[message(slab, jnp.float32)] + [message(slab)] * (len(near) - 1),
            in_specs=[SMEM] + [VMEM] * (len(states) + 2) + [ANY] * len(ties),
            out_specs=[VMEM] * len(near),
            scratch_shapes=[pltpu.VMEM((MOMENTS * core, rows), jnp.float32)],
            compiler_params=params(24),
            cost_estimate=cost(4),
            name="finish",
        )(me, *grids, *states, *ties)

    if two:
        crossing, states = sections(False, *firsts)
        back = exchange(crossing, n, far)
        crossing, more = sections(True, *firsts, *rests, crossing[0])
        staying = finished(states + more, *back)
        back += exchange(crossing, n, far)
    else:
        crossing, states = sections(False, *rests)
        staying = finished(states)
        back = exchange(crossing, n, far)
    staying = exchange(staying, n, near)
    arrived = pl.pallas_call(
        arrived_kernel,
        out_shape=jax.ShapeDtypeStruct((8, 128), jnp.float32),
        in_specs=[ANY] * len(back),
        out_specs=VMEM,
        compiler_params=params(1),
        cost_estimate=cost(6),
        name="arrived",
    )(*back)
    out = pl.pallas_call(
        functools.partial(unpack_kernel, n, far, near, 2 if two else 1),
        out_shape=jax.ShapeDtypeStruct((MOMENTS, rows, cols), jnp.float32),
        in_specs=[SMEM] + [VMEM] * (len(staying) + len(back)) + [ANY],
        out_specs=ANY,
        scratch_shapes=[
            pltpu.VMEM((cols, rows), jnp.float32),
            pltpu.VMEM((MOMENTS, rows, cols), jnp.float32),
            pltpu.SemaphoreType.DMA((MOMENTS,)),
        ],
        compiler_params=params(24),
        cost_estimate=cost(3),
        name="unpack",
    )(me, *staying, *back, arrived)
    return jnp.swapaxes(out, 0, 1)


def solution(mesh):
    return jax.shard_map(
        on_device,
        mesh=mesh,
        in_specs=(
            P("gy", "gx"),
            P("gy", None, "gx"),
            P("gy", "gx"),
            P("gy", None, "gx"),
            P("gy", None, "gx"),
        ),
        out_specs=P("gy", None, "gx"),
        check_vma=False,
    )
```

```python
import functools
import math

import jax
import jax.numpy as jnp
from jax import lax
from jax.experimental import pallas as pl
from jax.experimental.pallas import tpu as pltpu
from jax.sharding import PartitionSpec as P

time_step = 0.05
enforcement_weight = 4.0
plate_speed = 0.5
dissipation_speed = 0.25
coeffs = (0.75, -0.15, 1.0 / 60.0)

MOMENTS = 13
HALO = 8
RHO, TEMP = 0, 4
VMEM = pl.BlockSpec(memory_space=pltpu.VMEM)
ANY = pl.BlockSpec(memory_space=pl.ANY)
HBM = pl.BlockSpec(memory_space=pltpu.HBM)
SMEM = pl.BlockSpec(memory_space=pltpu.SMEM)


def cost(micros):
    return pl.CostEstimate(
        flops=int(micros * 1e9), bytes_accessed=int(micros * 3e6), transcendentals=0
    )


def params(mib=48):
    return pltpu.CompilerParams(vmem_limit_bytes=mib * 2**20)


def code(f, x):
    if f == RHO:
        return x - 1.25
    if f == TEMP:
        return jnp.exp2(160.0 * (x - 1.25))
    return x


def decode(f, y):
    if f == RHO:
        return y + 1.25
    if f == TEMP:
        return jnp.log2(y) * (1.0 / 160.0) + 1.25
    return y


def flux(u, d, f):
    v = u[1 + d]
    temperature = u[4]
    heat = u[10:13]
    s = [[u[5], u[6], u[8]], [u[6], u[7], u[9]], [u[8], u[9], None]]
    if f == 0:
        return u[0] * v
    if f < 4:
        i = f - 1
        out = u[1 + i] * v + s[i][d]
        return out + temperature if i == d else out
    if f == 4:
        return v * temperature + 2.0 / 3.0 * heat[d]
    if f < 10:
        i, j = ((0, 0), (0, 1), (1, 1), (0, 2), (1, 2))[f - 5]
        out = v * s[i][j]
        weight = {}
        if j == d:
            weight[i] = weight.get(i, 0.0) + 0.4
        if i == d:
            weight[j] = weight.get(j, 0.0) + 0.4
        if i == j:
            weight[d] = weight.get(d, 0.0) - 4.0 / 15.0
        for k, w in weight.items():
            out = out + w * heat[k]
        return out
    i = f - 10
    out = v * heat[i] + temperature * s[i][d]
    return out + 2.5 * temperature * temperature if i == d else out


def sources(u, wall):
    near = jnp.abs(wall)
    nu = u[0] * jnp.sqrt(u[4] * u[4] + 0.25)
    heavy, light = -0.8 * nu, -0.55 * nu
    out = [None] * MOMENTS
    out[1] = -enforcement_weight * near * (u[1] - plate_speed * wall)
    out[4] = -dissipation_speed * nu * u[4] - enforcement_weight * near * (u[4] - 1.0)
    for f in range(5, 10):
        out[f] = heavy * u[f]
    for f in range(10, 13):
        out[f] = light * u[f]
    return out


def along_of(fx):
    count = fx.shape[0]
    total = None
    for k in range(3):
        upper = pltpu.roll(fx, count - (k + 1), 0)
        lower = pltpu.roll(fx, k + 1, 0)
        term = coeffs[k] * (upper - lower)
        total = term if total is None else total + term
    return total


def message_start(me, s, slab):
    to = jnp.bitwise_xor(me, s)
    return pl.multiple_of(to * slab + jnp.where(to % 2 == 0, slab // 2, 0), 16)


def pack_kernel(n, two, me_ref, *refs):
    inputs, refs = refs[:5], refs[5:]
    count = n if two else 0
    outs, (strip, given, arrived), refs = refs[: count + 1], refs[count + 1 : count + 4], refs[count + 4 :]
    held, left_at = refs[:-1], refs[-1]
    rows, cols = given.shape[1:]
    slab = cols // n
    me = me_ref[0]
    copies, end = [], 0
    for k, src in enumerate(inputs):
        first, end = end, end + (1 if len(src.shape) == 2 else src.shape[0])
        dst = given.at[first] if len(src.shape) == 2 else given.at[first:end]
        copies.append((first, end, pltpu.make_async_copy(src, dst, arrived.at[k])))
        copies[k][2].start()
    strip[0:HALO, :] = jnp.zeros((HALO, rows), jnp.float32)
    strip[HALO + cols :, :] = jnp.zeros((HALO, rows), jnp.float32)
    leaving = []
    done = 0
    for at, (first, end, copy) in enumerate(copies):
        copy.wait()
        for f in range(first, end):
            strip[HALO : HALO + cols, :] = code(f, given[f]).T
            for s in range(count):
                here = pl.ds(message_start(me, s, slab), held[s].shape[1])
                held[s][f] = strip[here, :].astype(jnp.bfloat16)
            held[count][f] = strip[...].astype(jnp.bfloat16)
        if at % 2 == 0:
            span = pl.ds(done, end - done)
            for k, out in enumerate(outs):
                copy = pltpu.make_async_copy(held[k].at[span], out.at[span], left_at.at[k, at // 2])
                copy.start()
                leaving.append(copy)
            done = end
    for copy in leaving:
        copy.wait()


def edge_kernel(tall, tie, left, right):
    cols = tall.shape[1] - 2 * HALO
    left[...] = tall[:, 0 : 2 * HALO, :]
    right[...] = tall[:, cols : cols + 2 * HALO, :]


def rest_kernel(n, two, me_ref, tall, before, after, *outs):
    me = me_ref[0]
    slab = (tall.shape[1] - 2 * HALO) // n
    count = outs[0].shape[1]
    for s in range(n):
        to = jnp.bitwise_xor(me, s)
        start = to * slab
        if two:
            start += jnp.where(to % 2 == 0, 0, slab // 2 + 2 * HALO)
        start = pl.multiple_of(start, 16)
        for f in range(MOMENTS):
            outs[s][f] = tall[f, pl.ds(start, count), :]

        def merge(tile, halo, at_start):
            line = lax.broadcasted_iota(jnp.int32, halo.shape[1:], 0)
            keep = (line < HALO) == at_start
            for f in range(MOMENTS):
                new, old = halo[f].astype(jnp.float32), outs[s][f, tile, :].astype(jnp.float32)
                outs[s][f, tile, :] = jnp.where(keep, new, old).astype(jnp.bfloat16)

        @pl.when(to == 0)
        def _():
            merge(slice(0, 2 * HALO), before, True)

        @pl.when(to == n - 1)
        def _():
            merge(slice(count - 2 * HALO, count), after, False)


def grid_kernel(n, rows, slots, me_ref, *refs):
    out, sin_col, cos_col, back_col, line_col, total = refs[-6:]
    size = n * rows
    last = size - 1
    half = math.pi / (2.0 * last)
    me = me_ref[0]
    step = 64
    lane = min(rows, 128)

    def table(s):
        line = jnp.bitwise_xor(me, s) * rows + lax.broadcasted_iota(jnp.int32, (8, rows), 1)
        angle = half * line.astype(jnp.float32)
        edge = (line == 0) | (line == last)
        sign = (1 - 2 * (line & 1)).astype(jnp.float32)
        return line.astype(jnp.float32), jnp.sin(angle), jnp.cos(angle), edge, sign

    def column(x):
        return jnp.broadcast_to(x[0:1], (lane, rows)).T

    for s in range(n):
        line, sine, cosine, edge, sign = table(s)
        here = pl.ds(s * rows, rows)
        line_col[here, :] = column(line)
        sin_col[here, :] = column(sine)
        cos_col[here, :] = column(cosine)
        back_col[here, :] = column(jnp.where(edge, 0.5 * sign, sign))

    for index, s in enumerate(slots):
        line, sine, cosine, edge, sign = table(s)
        front = (-math.pi / last) * sine * cosine * jnp.where(edge, 2.0 * sign, sign)
        for p in range(rows // lane):
            here = pl.ds(index * rows + p * lane, lane)
            own = pl.ds(s * rows + p * lane, lane)
            line_i, sin_i, cos_i, front_i = (
                x[0:1, p * lane : (p + 1) * lane] for x in (line, sine, cosine, front)
            )
            total[...] = jnp.zeros_like(total)

            def block(t, carry):
                down = pl.ds(pl.multiple_of(t * step, step), step)
                gap = line_i - line_col[down, :]
                same = gap == 0.0
                x = half * gap
                x2 = x * x
                poly = -1.0 / 39916800.0
                for c in (1 / 362880.0, -1 / 5040.0, 1 / 120.0, -1 / 6.0, 1.0):
                    poly = poly * x2 + c
                plus = sin_i * cos_col[down, :] + cos_i * sin_col[down, :]
                denom = jnp.where(same, 1.0, plus * (x * poly))
                off = jnp.where(same, 0.0, front_i * back_col[down, :] / denom)
                total[...] += jnp.sum(off.reshape(step // 8, 8, lane), axis=0)
                out[down, here] = off.astype(jnp.bfloat16)
                return carry

            lax.fori_loop(0, size // step, block, 0)
            diagonal = -jnp.sum(total[...], axis=0, keepdims=True)
            same = lax.broadcasted_iota(jnp.int32, (lane, lane), 0) == (
                lax.broadcasted_iota(jnp.int32, (lane, lane), 1)
            )
            tile = out[own, here].astype(jnp.float32)
            out[own, here] = jnp.where(same, diagonal, tile).astype(jnp.bfloat16)


def weights_of(parts, grids, s, down=slice(None)):
    for part, grid in zip(parts, grids):
        if s in part:
            rows = grid.shape[1] // len(part)
            at = part.index(s) * rows
            return grid[down, at : at + rows]


def flip_kernel(n, parts, far, *refs):
    grids, out = refs[: len(parts)], refs[-1]
    rows = out.shape[0] // n
    line = lax.broadcasted_iota(jnp.int32, (rows, rows), 0)
    turn = line + lax.broadcasted_iota(jnp.int32, (rows, rows), 1) == rows - 1
    turn = jnp.where(turn, 1.0, 0.0).astype(jnp.bfloat16)
    for k, s in enumerate(far):
        for a in range(n):
            down = (a ^ (n - 1)) * rows
            tile = weights_of(parts, grids, s ^ (n - 1), slice(down, down + rows))
            tile = jnp.dot(turn, tile, preferred_element_type=jnp.float32).astype(jnp.bfloat16)
            tile = -jnp.dot(tile, turn, preferred_element_type=jnp.float32)
            out[a * rows : (a + 1) * rows, k * rows : (k + 1) * rows] = tile.astype(jnp.bfloat16)


def far_first(arrays):
    half = len(arrays) // 2
    return [arrays[0], *arrays[half:], *arrays[1:half]]


def in_slots(arrays):
    half = len(arrays) // 2
    return [arrays[0], *arrays[half + 1 :], *arrays[1 : half + 1]]


def section_kernel(n, two, second, far, parts, me_ref, *refs):
    grids, refs = refs[: len(parts)], refs[len(parts) :]
    firsts, refs = in_slots(refs[:n]), refs[n:]
    if second:
        rests, refs = in_slots(refs[:n]), refs[n + 1 :]
    outs, refs = refs[: len(far)], refs[len(far) :]
    u1, r0, fy1, u0, fy0, product = refs
    wide, size = u0.shape[1:]
    rows = size // n
    core = wide - 2 * HALO
    me = me_ref[0]
    right_first = me % 2 == 0
    lane = min(rows, 128)
    strips = rows // lane

    for s in range(n):
        here = pl.ds(s * rows, rows)
        for f in range(MOMENTS):
            if not second:
                u0[f, :, here] = decode(f, firsts[s][f].astype(jnp.float32))
            else:
                new = rests[s][f].astype(jnp.float32)
                fresh = pl.ds(pl.multiple_of(jnp.where(right_first, 0, 2 * HALO), 16), core)
                u0[f, fresh, here] = decode(f, new)
                src = pl.ds(pl.multiple_of(jnp.where(right_first, 0, core), 16), 2 * HALO)
                dst = pl.ds(pl.multiple_of(jnp.where(right_first, core, 0), 16), 2 * HALO)
                old = firsts[s][f, src, :].astype(jnp.float32)
                u0[f, dst, here] = decode(f, old)

    for s in range(n):
        for p in range(strips):
            here = pl.ds(s * rows + p * lane, lane)
            u = [u0[f, :, here] for f in range(MOMENTS)]
            for f in range(MOMENTS):
                fy0[f * wide : (f + 1) * wide, here] = flux(u, 1, f).astype(jnp.bfloat16)

    middle = slice(HALO, HALO + core)
    for s in range(n):
        weights = weights_of(parts, grids, s)
        product[...] = jnp.dot(fy0[...], weights, preferred_element_type=jnp.float32)
        for p in range(strips):
            here = pl.ds(s * rows + p * lane, lane)
            there = pl.ds(p * lane, lane)
            u = [u0[f, :, here] for f in range(MOMENTS)]
            src = sources(u, walls(me, s, p, n, rows, wide))
            new = []
            for f in range(MOMENTS):
                across = product[f * wide : (f + 1) * wide, there]
                rate = -(along_of(flux(u, 0, f)) + across)
                if src[f] is not None:
                    rate = rate + src[f]
                r0[f, :, here] = rate[middle]
                new.append(u[f] + time_step * rate)
                u1[f, :, here] = new[f]
            inner = [x[middle] for x in new]
            for f in range(MOMENTS):
                fy1[f * core : (f + 1) * core, here] = flux(inner, 1, f).astype(jnp.bfloat16)

    finish(n, far, me_ref, parts, grids, u1, r0, fy1, outs, product)


def finish_kernel(n, near, parts, chunks, me_ref, *refs):
    grids, refs = refs[: len(parts)], refs[len(parts) :]
    states, outs, product = refs[: 3 * chunks], refs[-1 - len(near) : -1], refs[-1]
    core = outs[0].shape[1] // chunks
    for c in range(chunks):
        part = [out.at[:, c * core : (c + 1) * core, :] for out in outs]
        finish(n, near, me_ref, parts, grids, *states[3 * c : 3 * c + 3], part, product)


def walls(me, s, p, n, rows, count):
    lane = min(rows, 128)
    line = jnp.bitwise_xor(me, s) * rows + p * lane
    line = line + lax.broadcasted_iota(jnp.int32, (count, lane), 1)
    return jnp.where(line == 0, 1.0, jnp.where(line == n * rows - 1, -1.0, 0.0))


def finish(n, slots, me_ref, parts, grids, u1, r0, fy1, outs, product):
    wide, size = u1.shape[1:]
    rows = size // n
    core = wide - 2 * HALO
    lane = min(rows, 128)
    me = me_ref[0]
    middle = slice(HALO, HALO + core)
    for k, s in enumerate(slots):
        weights = weights_of(parts, grids, s)
        product[0 : MOMENTS * core, :] = jnp.dot(
            fy1[...], weights, preferred_element_type=jnp.float32
        )
        for p in range(rows // lane):
            here = pl.ds(s * rows + p * lane, lane)
            there = pl.ds(p * lane, lane)
            u = [u1[f, :, here] for f in range(MOMENTS)]
            inner = [x[middle] for x in u]
            src = sources(inner, walls(me, s, p, n, rows, core))
            for f in range(MOMENTS):
                across = product[f * core : (f + 1) * core, there]
                rate = -(along_of(flux(u, 0, f))[middle] + across)
                if src[f] is not None:
                    rate = rate + src[f]
                rate = 0.5 * (r0[f, :, here] + rate)
                outs[k][f, :, there] = rate.astype(outs[k].dtype)


def arrived_kernel(*refs):
    refs[-1][...] = jnp.zeros_like(refs[-1])


def unpack_kernel(n, far, near, chunks, me_ref, *refs):
    staying, refs = refs[: len(near)], refs[len(near) :]
    out, tall, held, leaving = refs[-4:]
    cols = tall.shape[0]
    slab = cols // n
    width = slab // chunks
    me = me_ref[0]
    copies = []
    for f in range(MOMENTS):
        for s in near + far:
            of = jnp.bitwise_xor(me, s)
            for c in range(chunks):
                start = of * slab
                if chunks == 2:
                    start += jnp.where(of % 2 == 0, width * (1 - c), width * c)
                here = pl.ds(pl.multiple_of(start, 16), width)
                if s in near:
                    piece = staying[near.index(s)][f, c * width : (c + 1) * width, :]
                else:
                    piece = refs[c * len(far) + far.index(s)][f]
                tall[here, :] = piece.astype(jnp.float32)
        held[f] = tall[...].T
        copies.append(pltpu.make_async_copy(held.at[f], out.at[f], leaving.at[f]))
        copies[f].start()
    for copy in copies:
        copy.wait()


def to_partner(array, n, s):
    return array if s == 0 else lax.ppermute(array, "gy", [(i, i ^ s) for i in range(n)])


def exchange(arrays, n, slots):
    pairs = list(zip(arrays, slots))[::-1]
    return [to_partner(array, n, s) for array, s in pairs][::-1]


def on_device(rho, vel, temp, stress, heat):
    rows, cols = rho.shape
    n = lax.axis_size("gy")
    ring = lax.axis_size("gx")
    size, slab = n * rows, cols // n
    two = slab % 32 == 0
    core = slab // 2 if two else slab
    wide = core + 2 * HALO
    half = jnp.bfloat16
    me = lax.axis_index("gy").astype(jnp.int32).reshape(1)
    vel, stress, heat = (jnp.swapaxes(a, 0, 1) for a in (vel, stress, heat))

    def message(width, kind=half):
        return jax.ShapeDtypeStruct((MOMENTS, width, rows), kind)

    far, near = (tuple(range(n // 2, n)), tuple(range(n // 2)))
    inputs = (rho, vel, temp, stress, heat)

    def pack(arrays):
        shapes = [message(wide)] * n if two else []
        shapes += [message(cols + 2 * HALO)]
        return pl.pallas_call(
            functools.partial(pack_kernel, n, two),
            out_shape=shapes,
            in_specs=[SMEM] + [HBM] * len(arrays),
            out_specs=[ANY] * len(shapes),
            scratch_shapes=[
                pltpu.VMEM((cols + 2 * HALO, rows), jnp.float32),
                pltpu.VMEM((MOMENTS, rows, cols), jnp.float32),
                pltpu.SemaphoreType.DMA((len(arrays),)),
            ]
            + [pltpu.VMEM(x.shape, x.dtype) for x in shapes]
            + [pltpu.SemaphoreType.DMA((len(shapes), 3))],
            compiler_params=params(56),
            cost_estimate=cost(2),
            name="pack",
        )(me, *arrays)

    firsts = []
    if two:
        *firsts, tall = pack(inputs)
        firsts = exchange(firsts, n, range(n))
    else:
        (tall,) = pack(inputs)

    lane = min(rows, 128)

    def grid_of(slots, *ties):
        return pl.pallas_call(
            functools.partial(grid_kernel, n, rows, slots),
            out_shape=jax.ShapeDtypeStruct((size, len(slots) * rows), half),
            in_specs=[SMEM] + [ANY] * len(ties),
            out_specs=VMEM,
            scratch_shapes=[pltpu.VMEM((size, lane), jnp.float32)] * 4
            + [pltpu.VMEM((8, lane), jnp.float32)],
            compiler_params=params(24),
            cost_estimate=cost(1),
            name="grid",
        )(me, *ties)

    parts = (near[: n // 4], near[n // 4 :])
    grids = [grid_of(part) for part in parts]
    left, right = pl.pallas_call(
        edge_kernel,
        out_shape=[message(2 * HALO)] * 2,
        in_specs=[VMEM, ANY],
        out_specs=[VMEM] * 2,
        compiler_params=params(24),
        cost_estimate=cost(0.2),
        name="edges",
    )(tall, grids[0])
    up = [(i, (i + 1) % ring) for i in range(ring)]
    before = lax.ppermute(right, "gx", up)
    after = lax.ppermute(left, "gx", [(j, i) for i, j in up])
    turned = pl.pallas_call(
        functools.partial(flip_kernel, n, parts, far),
        out_shape=jax.ShapeDtypeStruct((size, len(far) * rows), half),
        in_specs=[VMEM] * 2,
        out_specs=VMEM,
        compiler_params=params(24),
        cost_estimate=cost(0.3),
        name="flip",
    )(*grids)
    all_parts, all_grids = (*parts, far), (*grids, turned)
    rests = pl.pallas_call(
        functools.partial(rest_kernel, n, two),
        out_shape=[message(core if two else wide)] * n,
        in_specs=[SMEM] + [VMEM] * 3,
        out_specs=[VMEM] * n,
        compiler_params=params(),
        cost_estimate=cost(0.2),
        name="rest",
    )(me, tall, before, after)
    rests = exchange(rests, n, range(n))

    def sections(second, *arrays):
        state = [
            jax.ShapeDtypeStruct((MOMENTS, wide, size), jnp.float32),
            jax.ShapeDtypeStruct((MOMENTS, core, size), jnp.float32),
            jax.ShapeDtypeStruct((MOMENTS * core, size), half),
        ]
        *crossing, u1, r0, fy1 = pl.pallas_call(
            functools.partial(section_kernel, n, two, second, far, all_parts),
            out_shape=[message(core)] * len(far) + state,
            in_specs=[SMEM] + [VMEM] * (len(arrays) + 3 - second) + [ANY] * second,
            out_specs=[VMEM] * (len(far) + 3),
            scratch_shapes=[
                pltpu.VMEM((MOMENTS, wide, size), jnp.float32),
                pltpu.VMEM((MOMENTS * wide, size), half),
                pltpu.VMEM((MOMENTS * wide, rows), jnp.float32),
            ],
            compiler_params=params(24),
            cost_estimate=cost(6),
            name="sections",
        )(me, *all_grids, *arrays)
        return crossing, [u1, r0, fy1]

    def finished(states, *ties):
        return pl.pallas_call(
            functools.partial(finish_kernel, n, near, parts, len(states) // 3),
            out_shape=[message(slab, jnp.float32)] + [message(slab)] * (len(near) - 1),
            in_specs=[SMEM] + [VMEM] * (len(states) + 2) + [ANY] * len(ties),
            out_specs=[VMEM] * len(near),
            scratch_shapes=[pltpu.VMEM((MOMENTS * core, rows), jnp.float32)],
            compiler_params=params(24),
            cost_estimate=cost(4),
            name="finish",
        )(me, *grids, *states, *ties)

    if two:
        firsts, rests = far_first(firsts), far_first(rests)
        crossing, states = sections(False, *firsts)
        back = exchange(crossing, n, far)
        crossing, more = sections(True, *firsts, *rests, crossing[0])
        staying = finished(states + more, *back)
        back += exchange(crossing, n, far)
    else:
        crossing, states = sections(False, *far_first(rests))
        staying = finished(states)
        back = exchange(crossing, n, far)
    staying = exchange(staying, n, near)
    arrived = pl.pallas_call(
        arrived_kernel,
        out_shape=jax.ShapeDtypeStruct((8, 128), jnp.float32),
        in_specs=[ANY] * len(back),
        out_specs=VMEM,
        compiler_params=params(1),
        cost_estimate=cost(6),
        name="arrived",
    )(*back)
    out = pl.pallas_call(
        functools.partial(unpack_kernel, n, far, near, 2 if two else 1),
        out_shape=jax.ShapeDtypeStruct((MOMENTS, rows, cols), jnp.float32),
        in_specs=[SMEM] + [VMEM] * (len(staying) + len(back)) + [ANY],
        out_specs=ANY,
        scratch_shapes=[
            pltpu.VMEM((cols, rows), jnp.float32),
            pltpu.VMEM((MOMENTS, rows, cols), jnp.float32),
            pltpu.SemaphoreType.DMA((MOMENTS,)),
        ],
        compiler_params=params(24),
        cost_estimate=cost(3),
        name="unpack",
    )(me, *staying, *back, arrived)
    return jnp.swapaxes(out, 0, 1)


def solution(mesh):
    return jax.shard_map(
        on_device,
        mesh=mesh,
        in_specs=(
            P("gy", "gx"),
            P("gy", None, "gx"),
            P("gy", "gx"),
            P("gy", None, "gx"),
            P("gy", None, "gx"),
        ),
        out_specs=P("gy", None, "gx"),
        check_vma=False,
    )
```

```python
import functools
import math

import jax
import jax.numpy as jnp
from jax import lax
from jax.experimental import pallas as pl
from jax.experimental.pallas import tpu as pltpu
from jax.sharding import PartitionSpec as P

time_step = 0.05
enforcement_weight = 4.0
plate_speed = 0.5
dissipation_speed = 0.25
coeffs = (0.75, -0.15, 1.0 / 60.0)

MOMENTS = 13
HALO = 8
RHO, TEMP = 0, 4
VMEM = pl.BlockSpec(memory_space=pltpu.VMEM)
ANY = pl.BlockSpec(memory_space=pl.ANY)
HBM = pl.BlockSpec(memory_space=pltpu.HBM)
SMEM = pl.BlockSpec(memory_space=pltpu.SMEM)


def cost(micros):
    return pl.CostEstimate(
        flops=int(micros * 1e9), bytes_accessed=int(micros * 3e6), transcendentals=0
    )


def params(mib=48):
    return pltpu.CompilerParams(vmem_limit_bytes=mib * 2**20)


def code(f, x):
    if f == RHO:
        return x - 1.25
    if f == TEMP:
        return jnp.exp2(160.0 * (x - 1.25))
    return x


def decode(f, y):
    if f == RHO:
        return y + 1.25
    if f == TEMP:
        return jnp.log2(y) * (1.0 / 160.0) + 1.25
    return y


def flux(u, d, f):
    v = u[1 + d]
    temperature = u[4]
    heat = u[10:13]
    s = [[u[5], u[6], u[8]], [u[6], u[7], u[9]], [u[8], u[9], None]]
    if f == 0:
        return u[0] * v
    if f < 4:
        i = f - 1
        out = u[1 + i] * v + s[i][d]
        return out + temperature if i == d else out
    if f == 4:
        return v * temperature + 2.0 / 3.0 * heat[d]
    if f < 10:
        i, j = ((0, 0), (0, 1), (1, 1), (0, 2), (1, 2))[f - 5]
        out = v * s[i][j]
        weight = {}
        if j == d:
            weight[i] = weight.get(i, 0.0) + 0.4
        if i == d:
            weight[j] = weight.get(j, 0.0) + 0.4
        if i == j:
            weight[d] = weight.get(d, 0.0) - 4.0 / 15.0
        for k, w in weight.items():
            out = out + w * heat[k]
        return out
    i = f - 10
    out = v * heat[i] + temperature * s[i][d]
    return out + 2.5 * temperature * temperature if i == d else out


def sources(u, wall):
    near = jnp.abs(wall)
    nu = u[0] * jnp.sqrt(u[4] * u[4] + 0.25)
    heavy, light = -0.8 * nu, -0.55 * nu
    out = [None] * MOMENTS
    out[1] = -enforcement_weight * near * (u[1] - plate_speed * wall)
    out[4] = -dissipation_speed * nu * u[4] - enforcement_weight * near * (u[4] - 1.0)
    for f in range(5, 10):
        out[f] = heavy * u[f]
    for f in range(10, 13):
        out[f] = light * u[f]
    return out


def along_of(fx, turned, f):
    count = fx.shape[0] // 8
    turned[f] = fx
    x = [turned[f, pl.ds(v, 8, stride=count), :] for v in range(count)]
    x = [pltpu.roll(y, 1, 0) for y in x[-3:]] + x + [pltpu.roll(y, 7, 0) for y in x[:3]]
    for v in range(count):
        total = None
        for k in range(3):
            term = coeffs[k] * (x[3 + v + k + 1] - x[3 + v - k - 1])
            total = term if total is None else total + term
        turned[MOMENTS + f, pl.ds(v, 8, stride=count), :] = total
    return turned.at[MOMENTS + f]


def message_start(me, s, slab):
    to = jnp.bitwise_xor(me, s)
    return pl.multiple_of(to * slab + jnp.where(to % 2 == 0, slab // 2, 0), 16)


GROUPS = ((0, 1), (1, 4), (4, 5), (5, 8), (8, 10), (10, 13))


def pack_kernel(n, two, me_ref, *refs):
    (rho, vel, temp, stress, heat), refs = refs[:5], refs[5:]
    inputs = (rho, vel, temp, stress.at[0:3], stress.at[3:5], heat)
    count = n if two else 0
    outs, (strip, given, arrived), refs = refs[: count + 1], refs[count + 1 : count + 4], refs[count + 4 :]
    held, left_at = refs[:-1], refs[-1]
    rows, cols = given.shape[1:]
    slab = cols // n
    me = me_ref[0]
    copies = []
    for k, (first, end) in enumerate(GROUPS):
        dst = given.at[first] if len(inputs[k].shape) == 2 else given.at[first:end]
        copies.append(pltpu.make_async_copy(inputs[k], dst, arrived.at[k]))
        copies[k].start()
    strip[0:HALO, :] = jnp.zeros((HALO, rows), jnp.float32)
    strip[HALO + cols :, :] = jnp.zeros((HALO, rows), jnp.float32)
    leaving = []
    done = 0
    for at, (first, end) in enumerate(GROUPS):
        copies[at].wait()
        for f in range(first, end):
            strip[HALO : HALO + cols, :] = code(f, given[f]).T
            for s in range(count):
                here = pl.ds(message_start(me, s, slab), held[s].shape[1])
                held[s][f] = strip[here, :].astype(jnp.bfloat16)
            held[count][f] = strip[...].astype(jnp.bfloat16)
        if at in (1, 3, 4, 5):
            span = pl.ds(done, end - done)
            for k, out in enumerate(outs):
                copy = pltpu.make_async_copy(held[k].at[span], out.at[span], left_at.at[k, at - 1])
                copy.start()
                leaving.append(copy)
            done = end
    for copy in leaving:
        copy.wait()


def edge_kernel(tall, tie, left, right):
    cols = tall.shape[1] - 2 * HALO
    left[...] = tall[:, 0 : 2 * HALO, :]
    right[...] = tall[:, cols : cols + 2 * HALO, :]


def rest_kernel(n, two, me_ref, tall, before, after, *outs):
    me = me_ref[0]
    slab = (tall.shape[1] - 2 * HALO) // n
    count = outs[0].shape[1]
    for s in range(n):
        to = jnp.bitwise_xor(me, s)
        start = to * slab
        if two:
            start += jnp.where(to % 2 == 0, 0, slab // 2 + 2 * HALO)
        start = pl.multiple_of(start, 16)
        for f in range(MOMENTS):
            outs[s][f] = tall[f, pl.ds(start, count), :]

        def merge(tile, halo, at_start):
            line = lax.broadcasted_iota(jnp.int32, halo.shape[1:], 0)
            keep = (line < HALO) == at_start
            for f in range(MOMENTS):
                new, old = halo[f].astype(jnp.float32), outs[s][f, tile, :].astype(jnp.float32)
                outs[s][f, tile, :] = jnp.where(keep, new, old).astype(jnp.bfloat16)

        @pl.when(to == 0)
        def _():
            merge(slice(0, 2 * HALO), before, True)

        @pl.when(to == n - 1)
        def _():
            merge(slice(count - 2 * HALO, count), after, False)


def grid_kernel(n, rows, slots, me_ref, *refs):
    out, sin_col, cos_col, back_col, line_col, total = refs[-6:]
    size = n * rows
    last = size - 1
    half = math.pi / (2.0 * last)
    me = me_ref[0]
    step = 64
    lane = min(rows, 128)

    def table(s):
        line = jnp.bitwise_xor(me, s) * rows + lax.broadcasted_iota(jnp.int32, (8, rows), 1)
        angle = half * line.astype(jnp.float32)
        edge = (line == 0) | (line == last)
        sign = (1 - 2 * (line & 1)).astype(jnp.float32)
        return line.astype(jnp.float32), jnp.sin(angle), jnp.cos(angle), edge, sign

    def column(x):
        return jnp.broadcast_to(x[0:1], (lane, rows)).T

    for s in range(n):
        line, sine, cosine, edge, sign = table(s)
        here = pl.ds(s * rows, rows)
        line_col[here, :] = column(line)
        sin_col[here, :] = column(sine)
        cos_col[here, :] = column(cosine)
        back_col[here, :] = column(jnp.where(edge, 0.5 * sign, sign))

    for index, s in enumerate(slots):
        line, sine, cosine, edge, sign = table(s)
        front = (-math.pi / last) * sine * cosine * jnp.where(edge, 2.0 * sign, sign)
        for p in range(rows // lane):
            here = pl.ds(index * rows + p * lane, lane)
            own = pl.ds(s * rows + p * lane, lane)
            line_i, sin_i, cos_i, front_i = (
                x[0:1, p * lane : (p + 1) * lane] for x in (line, sine, cosine, front)
            )
            total[...] = jnp.zeros_like(total)

            def block(t, carry):
                down = pl.ds(pl.multiple_of(t * step, step), step)
                gap = line_i - line_col[down, :]
                same = gap == 0.0
                x = half * gap
                x2 = x * x
                poly = -1.0 / 39916800.0
                for c in (1 / 362880.0, -1 / 5040.0, 1 / 120.0, -1 / 6.0, 1.0):
                    poly = poly * x2 + c
                plus = sin_i * cos_col[down, :] + cos_i * sin_col[down, :]
                denom = jnp.where(same, 1.0, plus * (x * poly))
                off = jnp.where(same, 0.0, front_i * back_col[down, :] / denom)
                total[...] += jnp.sum(off.reshape(step // 8, 8, lane), axis=0)
                out[down, here] = off.astype(jnp.bfloat16)
                return carry

            lax.fori_loop(0, size // step, block, 0)
            diagonal = -jnp.sum(total[...], axis=0, keepdims=True)
            same = lax.broadcasted_iota(jnp.int32, (lane, lane), 0) == (
                lax.broadcasted_iota(jnp.int32, (lane, lane), 1)
            )
            tile = out[own, here].astype(jnp.float32)
            out[own, here] = jnp.where(same, diagonal, tile).astype(jnp.bfloat16)


def weights_of(parts, grids, s, down=slice(None)):
    for part, grid in zip(parts, grids):
        if s in part:
            rows = grid.shape[1] // len(part)
            at = part.index(s) * rows
            return grid[down, at : at + rows]


def flip_kernel(n, parts, far, *refs):
    grids, out = refs[: len(parts)], refs[-1]
    rows = out.shape[0] // n
    line = lax.broadcasted_iota(jnp.int32, (rows, rows), 0)
    turn = line + lax.broadcasted_iota(jnp.int32, (rows, rows), 1) == rows - 1
    turn = jnp.where(turn, 1.0, 0.0).astype(jnp.bfloat16)
    for k, s in enumerate(far):
        for a in range(n):
            down = (a ^ (n - 1)) * rows
            tile = weights_of(parts, grids, s ^ (n - 1), slice(down, down + rows))
            tile = jnp.dot(turn, tile, preferred_element_type=jnp.float32).astype(jnp.bfloat16)
            tile = -jnp.dot(tile, turn, preferred_element_type=jnp.float32)
            out[a * rows : (a + 1) * rows, k * rows : (k + 1) * rows] = tile.astype(jnp.bfloat16)


def far_first(arrays):
    half = len(arrays) // 2
    return [arrays[0], *arrays[half:], *arrays[1:half]]


def in_slots(arrays):
    half = len(arrays) // 2
    return [arrays[0], *arrays[half + 1 :], *arrays[1 : half + 1]]


def section_kernel(n, two, second, far, parts, me_ref, *refs):
    grids, refs = refs[: len(parts)], refs[len(parts) :]
    firsts, refs = in_slots(refs[:n]), refs[n:]
    if second:
        rests, refs = in_slots(refs[:n]), refs[n + 1 :]
    outs, refs = refs[: len(far)], refs[len(far) :]
    u1, r0, fy1, u0, fy0, product, turned = refs
    wide, size = u0.shape[1:]
    rows = size // n
    core = wide - 2 * HALO
    me = me_ref[0]
    right_first = me % 2 == 0
    lane = min(rows, 128)
    strips = rows // lane

    for s in range(n):
        here = pl.ds(s * rows, rows)
        for f in range(MOMENTS):
            if not second:
                u0[f, :, here] = decode(f, firsts[s][f].astype(jnp.float32))
            else:
                new = rests[s][f].astype(jnp.float32)
                fresh = pl.ds(pl.multiple_of(jnp.where(right_first, 0, 2 * HALO), 16), core)
                u0[f, fresh, here] = decode(f, new)
                src = pl.ds(pl.multiple_of(jnp.where(right_first, 0, core), 16), 2 * HALO)
                dst = pl.ds(pl.multiple_of(jnp.where(right_first, core, 0), 16), 2 * HALO)
                old = firsts[s][f, src, :].astype(jnp.float32)
                u0[f, dst, here] = decode(f, old)

    for s in range(n):
        for p in range(strips):
            here = pl.ds(s * rows + p * lane, lane)
            u = [u0[f, :, here] for f in range(MOMENTS)]
            for f in range(MOMENTS):
                fy0[f * wide : (f + 1) * wide, here] = flux(u, 1, f).astype(jnp.bfloat16)

    middle = slice(HALO, HALO + core)
    for s in range(n):
        weights = weights_of(parts, grids, s)
        product[...] = jnp.dot(fy0[...], weights, preferred_element_type=jnp.float32)
        for p in range(strips):
            here = pl.ds(s * rows + p * lane, lane)
            there = pl.ds(p * lane, lane)
            u = [u0[f, :, here] for f in range(MOMENTS)]
            src = sources(u, walls(me, s, p, n, rows, wide))
            new = []
            for f in range(MOMENTS):
                across = product[f * wide : (f + 1) * wide, there]
                rate = -(along_of(flux(u, 0, f), turned, f)[...] + across)
                if src[f] is not None:
                    rate = rate + src[f]
                r0[f, :, here] = rate[middle]
                new.append(u[f] + time_step * rate)
                u1[f, :, here] = new[f]
            inner = [x[middle] for x in new]
            for f in range(MOMENTS):
                fy1[f * core : (f + 1) * core, here] = flux(inner, 1, f).astype(jnp.bfloat16)

    finish(n, far, me_ref, parts, grids, u1, r0, fy1, outs, product, turned)


def finish_kernel(n, near, parts, chunks, me_ref, *refs):
    grids, refs = refs[: len(parts)], refs[len(parts) :]
    states, outs, product, turned = refs[: 3 * chunks], refs[-2 - len(near) : -2], *refs[-2:]
    core = outs[0].shape[1] // chunks
    for c in range(chunks):
        part = [out.at[:, c * core : (c + 1) * core, :] for out in outs]
        finish(n, near, me_ref, parts, grids, *states[3 * c : 3 * c + 3], part, product, turned)


def walls(me, s, p, n, rows, count):
    lane = min(rows, 128)
    line = jnp.bitwise_xor(me, s) * rows + p * lane
    line = line + lax.broadcasted_iota(jnp.int32, (count, lane), 1)
    return jnp.where(line == 0, 1.0, jnp.where(line == n * rows - 1, -1.0, 0.0))


def finish(n, slots, me_ref, parts, grids, u1, r0, fy1, outs, product, turned):
    wide, size = u1.shape[1:]
    rows = size // n
    core = wide - 2 * HALO
    lane = min(rows, 128)
    me = me_ref[0]
    middle = slice(HALO, HALO + core)
    for k, s in enumerate(slots):
        weights = weights_of(parts, grids, s)
        product[0 : MOMENTS * core, :] = jnp.dot(
            fy1[...], weights, preferred_element_type=jnp.float32
        )
        for p in range(rows // lane):
            here = pl.ds(s * rows + p * lane, lane)
            there = pl.ds(p * lane, lane)
            u = [u1[f, :, here] for f in range(MOMENTS)]
            inner = [x[middle] for x in u]
            src = sources(inner, walls(me, s, p, n, rows, core))
            for f in range(MOMENTS):
                across = product[f * core : (f + 1) * core, there]
                rate = -(along_of(flux(u, 0, f), turned, f)[middle, :] + across)
                if src[f] is not None:
                    rate = rate + src[f]
                rate = 0.5 * (r0[f, :, here] + rate)
                outs[k][f, :, there] = rate.astype(outs[k].dtype)


def arrived_kernel(*refs):
    refs[-1][...] = jnp.zeros_like(refs[-1])


def unpack_kernel(n, far, near, chunks, me_ref, *refs):
    staying, refs = refs[: len(near)], refs[len(near) :]
    out, tall, held, leaving = refs[-4:]
    cols = tall.shape[0]
    slab = cols // n
    width = slab // chunks
    me = me_ref[0]
    copies = []
    for f in range(MOMENTS):
        for s in near + far:
            of = jnp.bitwise_xor(me, s)
            for c in range(chunks):
                start = of * slab
                if chunks == 2:
                    start += jnp.where(of % 2 == 0, width * (1 - c), width * c)
                here = pl.ds(pl.multiple_of(start, 16), width)
                if s in near:
                    piece = staying[near.index(s)][f, c * width : (c + 1) * width, :]
                else:
                    piece = refs[c * len(far) + far.index(s)][f]
                tall[here, :] = piece.astype(jnp.float32)
        held[f] = tall[...].T
        copies.append(pltpu.make_async_copy(held.at[f], out.at[f], leaving.at[f]))
        copies[f].start()
    for copy in copies:
        copy.wait()


def to_partner(array, n, s):
    return array if s == 0 else lax.ppermute(array, "gy", [(i, i ^ s) for i in range(n)])


def exchange(arrays, n, slots):
    pairs = list(zip(arrays, slots))[::-1]
    return [to_partner(array, n, s) for array, s in pairs][::-1]


def on_device(rho, vel, temp, stress, heat):
    rows, cols = rho.shape
    n = lax.axis_size("gy")
    ring = lax.axis_size("gx")
    size, slab = n * rows, cols // n
    two = slab % 32 == 0
    core = slab // 2 if two else slab
    wide = core + 2 * HALO
    half = jnp.bfloat16
    me = lax.axis_index("gy").astype(jnp.int32).reshape(1)
    vel, stress, heat = (jnp.swapaxes(a, 0, 1) for a in (vel, stress, heat))

    def message(width, kind=half):
        return jax.ShapeDtypeStruct((MOMENTS, width, rows), kind)

    far, near = (tuple(range(n // 2, n)), tuple(range(n // 2)))
    inputs = (rho, vel, temp, stress, heat)

    def pack(arrays):
        shapes = [message(wide)] * n if two else []
        shapes += [message(cols + 2 * HALO)]
        return pl.pallas_call(
            functools.partial(pack_kernel, n, two),
            out_shape=shapes,
            in_specs=[SMEM] + [HBM] * len(arrays),
            out_specs=[ANY] * len(shapes),
            scratch_shapes=[
                pltpu.VMEM((cols + 2 * HALO, rows), jnp.float32),
                pltpu.VMEM((MOMENTS, rows, cols), jnp.float32),
                pltpu.SemaphoreType.DMA((len(GROUPS),)),
            ]
            + [pltpu.VMEM(x.shape, x.dtype) for x in shapes]
            + [pltpu.SemaphoreType.DMA((len(shapes), len(GROUPS)))],
            compiler_params=params(56),
            cost_estimate=cost(2),
            name="pack",
        )(me, *arrays)

    firsts = []
    if two:
        *firsts, tall = pack(inputs)
        firsts = exchange(firsts, n, range(n))
    else:
        (tall,) = pack(inputs)

    lane = min(rows, 128)

    def grid_of(slots, *ties):
        return pl.pallas_call(
            functools.partial(grid_kernel, n, rows, slots),
            out_shape=jax.ShapeDtypeStruct((size, len(slots) * rows), half),
            in_specs=[SMEM] + [ANY] * len(ties),
            out_specs=VMEM,
            scratch_shapes=[pltpu.VMEM((size, lane), jnp.float32)] * 4
            + [pltpu.VMEM((8, lane), jnp.float32)],
            compiler_params=params(24),
            cost_estimate=cost(1),
            name="grid",
        )(me, *ties)

    parts = (near[: n // 4], near[n // 4 :])
    grids = [grid_of(part) for part in parts]
    left, right = pl.pallas_call(
        edge_kernel,
        out_shape=[message(2 * HALO)] * 2,
        in_specs=[VMEM, ANY],
        out_specs=[VMEM] * 2,
        compiler_params=params(24),
        cost_estimate=cost(0.2),
        name="edges",
    )(tall, grids[0])
    up = [(i, (i + 1) % ring) for i in range(ring)]
    before = lax.ppermute(right, "gx", up)
    after = lax.ppermute(left, "gx", [(j, i) for i, j in up])
    turned = pl.pallas_call(
        functools.partial(flip_kernel, n, parts, far),
        out_shape=jax.ShapeDtypeStruct((size, len(far) * rows), half),
        in_specs=[VMEM] * 2,
        out_specs=VMEM,
        compiler_params=params(24),
        cost_estimate=cost(0.3),
        name="flip",
    )(*grids)
    all_parts, all_grids = (*parts, far), (*grids, turned)
    rests = pl.pallas_call(
        functools.partial(rest_kernel, n, two),
        out_shape=[message(core if two else wide)] * n,
        in_specs=[SMEM] + [VMEM] * 3,
        out_specs=[VMEM] * n,
        compiler_params=params(),
        cost_estimate=cost(0.2),
        name="rest",
    )(me, tall, before, after)
    rests = exchange(rests, n, range(n))

    def sections(second, *arrays):
        state = [
            jax.ShapeDtypeStruct((MOMENTS, wide, size), jnp.float32),
            jax.ShapeDtypeStruct((MOMENTS, core, size), jnp.float32),
            jax.ShapeDtypeStruct((MOMENTS * core, size), half),
        ]
        *crossing, u1, r0, fy1 = pl.pallas_call(
            functools.partial(section_kernel, n, two, second, far, all_parts),
            out_shape=[message(core)] * len(far) + state,
            in_specs=[SMEM] + [VMEM] * (len(arrays) + 3 - second) + [ANY] * second,
            out_specs=[VMEM] * (len(far) + 3),
            scratch_shapes=[
                pltpu.VMEM((MOMENTS, wide, size), jnp.float32),
                pltpu.VMEM((MOMENTS * wide, size), half),
                pltpu.VMEM((MOMENTS * wide, rows), jnp.float32),
                pltpu.VMEM((2 * MOMENTS, wide, lane), jnp.float32),
            ],
            compiler_params=params(24),
            cost_estimate=cost(6),
            name="sections",
        )(me, *all_grids, *arrays)
        return crossing, [u1, r0, fy1]

    def finished(states, *ties):
        return pl.pallas_call(
            functools.partial(finish_kernel, n, near, parts, len(states) // 3),
            out_shape=[message(slab, jnp.float32)] + [message(slab)] * (len(near) - 1),
            in_specs=[SMEM] + [VMEM] * (len(states) + 2) + [ANY] * len(ties),
            out_specs=[VMEM] * len(near),
            scratch_shapes=[
                pltpu.VMEM((MOMENTS * core, rows), jnp.float32),
                pltpu.VMEM((2 * MOMENTS, wide, lane), jnp.float32),
            ],
            compiler_params=params(24),
            cost_estimate=cost(4),
            name="finish",
        )(me, *grids, *states, *ties)

    if two:
        firsts, rests = far_first(firsts), far_first(rests)
        crossing, states = sections(False, *firsts)
        back = exchange(crossing, n, far)
        crossing, more = sections(True, *firsts, *rests, crossing[0])
        staying = finished(states + more, *back)
        back += exchange(crossing, n, far)
    else:
        crossing, states = sections(False, *far_first(rests))
        staying = finished(states)
        back = exchange(crossing, n, far)
    staying = exchange(staying, n, near)
    arrived = pl.pallas_call(
        arrived_kernel,
        out_shape=jax.ShapeDtypeStruct((8, 128), jnp.float32),
        in_specs=[ANY] * len(back),
        out_specs=VMEM,
        compiler_params=params(1),
        cost_estimate=cost(6),
        name="arrived",
    )(*back)
    out = pl.pallas_call(
        functools.partial(unpack_kernel, n, far, near, 2 if two else 1),
        out_shape=jax.ShapeDtypeStruct((MOMENTS, rows, cols), jnp.float32),
        in_specs=[SMEM] + [VMEM] * (len(staying) + len(back)) + [ANY],
        out_specs=ANY,
        scratch_shapes=[
            pltpu.VMEM((cols, rows), jnp.float32),
            pltpu.VMEM((MOMENTS, rows, cols), jnp.float32),
            pltpu.SemaphoreType.DMA((MOMENTS,)),
        ],
        compiler_params=params(24),
        cost_estimate=cost(3),
        name="unpack",
    )(me, *staying, *back, arrived)
    return jnp.swapaxes(out, 0, 1)


def solution(mesh):
    return jax.shard_map(
        on_device,
        mesh=mesh,
        in_specs=(
            P("gy", "gx"),
            P("gy", None, "gx"),
            P("gy", "gx"),
            P("gy", None, "gx"),
            P("gy", None, "gx"),
        ),
        out_specs=P("gy", None, "gx"),
        check_vma=False,
    )
```

```python
import functools
import math

import jax
import jax.numpy as jnp
from jax import lax
from jax.experimental import pallas as pl
from jax.experimental.pallas import tpu as pltpu
from jax.sharding import PartitionSpec as P

time_step = 0.05
enforcement_weight = 4.0
plate_speed = 0.5
dissipation_speed = 0.25
coeffs = (0.75, -0.15, 1.0 / 60.0)

MOMENTS = 13
HALO = 8
NEED = 6
SKIP = HALO - NEED
RHO, TEMP = 0, 4
VMEM = pl.BlockSpec(memory_space=pltpu.VMEM)
ANY = pl.BlockSpec(memory_space=pl.ANY)
HBM = pl.BlockSpec(memory_space=pltpu.HBM)
SMEM = pl.BlockSpec(memory_space=pltpu.SMEM)


def cost(micros):
    return pl.CostEstimate(
        flops=int(micros * 1e9), bytes_accessed=int(micros * 3e6), transcendentals=0
    )


def params(mib=48):
    return pltpu.CompilerParams(vmem_limit_bytes=mib * 2**20)


def code(f, x):
    if f == RHO:
        return x - 1.25
    if f == TEMP:
        return jnp.exp2(160.0 * (x - 1.25))
    return x


def decode(f, y):
    if f == RHO:
        return y + 1.25
    if f == TEMP:
        return jnp.log2(y) * (1.0 / 160.0) + 1.25
    return y


def flux(u, d, f):
    v = u[1 + d]
    temperature = u[4]
    heat = u[10:13]
    s = [[u[5], u[6], u[8]], [u[6], u[7], u[9]], [u[8], u[9], None]]
    if f == 0:
        return u[0] * v
    if f < 4:
        i = f - 1
        out = u[1 + i] * v + s[i][d]
        return out + temperature if i == d else out
    if f == 4:
        return v * temperature + 2.0 / 3.0 * heat[d]
    if f < 10:
        i, j = ((0, 0), (0, 1), (1, 1), (0, 2), (1, 2))[f - 5]
        out = v * s[i][j]
        weight = {}
        if j == d:
            weight[i] = weight.get(i, 0.0) + 0.4
        if i == d:
            weight[j] = weight.get(j, 0.0) + 0.4
        if i == j:
            weight[d] = weight.get(d, 0.0) - 4.0 / 15.0
        for k, w in weight.items():
            out = out + w * heat[k]
        return out
    i = f - 10
    out = v * heat[i] + temperature * s[i][d]
    return out + 2.5 * temperature * temperature if i == d else out


def sources(u, wall):
    near = jnp.abs(wall)
    nu = u[0] * jnp.sqrt(u[4] * u[4] + 0.25)
    heavy, light = -0.8 * nu, -0.55 * nu
    out = [None] * MOMENTS
    out[1] = -enforcement_weight * near * (u[1] - plate_speed * wall)
    out[4] = -dissipation_speed * nu * u[4] - enforcement_weight * near * (u[4] - 1.0)
    for f in range(5, 10):
        out[f] = heavy * u[f]
    for f in range(10, 13):
        out[f] = light * u[f]
    return out


def along_of(fx, turned, f):
    count = fx.shape[0] // 8
    turned[f] = fx
    x = [turned[f, pl.ds(v, 8, stride=count), :] for v in range(count)]
    x = [pltpu.roll(y, 1, 0) for y in x[-3:]] + x + [pltpu.roll(y, 7, 0) for y in x[:3]]
    for v in range(count):
        total = None
        for k in range(3):
            term = coeffs[k] * (x[3 + v + k + 1] - x[3 + v - k - 1])
            total = term if total is None else total + term
        turned[MOMENTS + f, pl.ds(v, 8, stride=count), :] = total
    return turned.at[MOMENTS + f]


def message_start(me, s, slab):
    to = jnp.bitwise_xor(me, s)
    return pl.multiple_of(to * slab + jnp.where(to % 2 == 0, slab // 2, 0), 16)


GROUPS = ((0, 1), (1, 4), (4, 5), (5, 8), (8, 10), (10, 13))


def pack_kernel(n, two, me_ref, *refs):
    (rho, vel, temp, stress, heat), refs = refs[:5], refs[5:]
    inputs = (rho, vel, temp, stress.at[0:3], stress.at[3:5], heat)
    count = n if two else 0
    outs, (strip, given, arrived), refs = refs[: count + 1], refs[count + 1 : count + 4], refs[count + 4 :]
    held, left_at = refs[:-1], refs[-1]
    rows, cols = given.shape[1:]
    slab = cols // n
    me = me_ref[0]
    copies = []
    for k, (first, end) in enumerate(GROUPS):
        dst = given.at[first] if len(inputs[k].shape) == 2 else given.at[first:end]
        copies.append(pltpu.make_async_copy(inputs[k], dst, arrived.at[k]))
        copies[k].start()
    wide = slab // 2 + 2 * HALO
    lane = min(rows, 128)
    leaving = []
    done = 0
    for at, (first, end) in enumerate(GROUPS):
        copies[at].wait()
        for f in range(first, end):
            strip[f, 0:HALO, :] = jnp.zeros((HALO, rows), jnp.float32)
            strip[f, HALO + cols :, :] = jnp.zeros((HALO, rows), jnp.float32)
            strip[f, HALO : HALO + cols, :] = code(f, given[f]).T
            for s in range(count):
                block = strip[f, pl.ds(message_start(me, s, slab), wide), :][SKIP : wide - SKIP]
                halves = [block[:, p : p + lane] for p in range(0, rows, lane)]
                held[s][f] = jnp.concatenate(halves, axis=0).astype(jnp.bfloat16)
            held[count][f] = strip[f].astype(jnp.bfloat16)
        if at in (1, 3, 4, 5):
            span = pl.ds(done, end - done)
            for k, out in enumerate(outs):
                copy = pltpu.make_async_copy(held[k].at[span], out.at[span], left_at.at[k, at - 1])
                copy.start()
                leaving.append(copy)
            done = end
    for copy in leaving:
        copy.wait()


def edge_kernel(tall, tie, left, right):
    cols = tall.shape[1] - 2 * HALO
    left[...] = tall[:, 0 : 2 * HALO, :]
    right[...] = tall[:, cols : cols + 2 * HALO, :]


def rest_kernel(n, two, me_ref, tall, before, after, *outs):
    me = me_ref[0]
    slab = (tall.shape[1] - 2 * HALO) // n
    count = outs[0].shape[1]
    wide = slab // 2 + 2 * HALO if two else count
    line = lax.broadcasted_iota(jnp.int32, before.shape[1:], 0)
    for s in range(n):
        to = jnp.bitwise_xor(me, s)
        even = to % 2 == 0
        start = to * slab
        if two:
            start += jnp.where(even, 0, slab // 2)
        start = pl.multiple_of(start, 16)
        for f in range(MOMENTS):
            block = tall[f, pl.ds(start, wide), :].astype(jnp.float32)
            first, last = block[: 2 * HALO], block[wide - 2 * HALO :]
            first = jnp.where((line < HALO) & (to == 0), before[f].astype(jnp.float32), first)
            last = jnp.where((line >= HALO) & (to == n - 1), after[f].astype(jnp.float32), last)
            between = [block[2 * HALO : wide - 2 * HALO]] if wide > 4 * HALO else []
            block = jnp.concatenate([first, *between, last], axis=0)
            if two:
                near_end = block[SKIP : SKIP + count]
                far_end = block[wide - SKIP - count : wide - SKIP]
                block = jnp.where(even, near_end, far_end)
            outs[s][f] = block.astype(jnp.bfloat16)


def grid_kernel(n, rows, slots, me_ref, *refs):
    out, sin_col, cos_col, back_col, line_col, total = refs[-6:]
    size = n * rows
    last = size - 1
    half = math.pi / (2.0 * last)
    me = me_ref[0]
    step = 64
    lane = min(rows, 128)

    def table(s):
        line = jnp.bitwise_xor(me, s) * rows + lax.broadcasted_iota(jnp.int32, (8, rows), 1)
        angle = half * line.astype(jnp.float32)
        edge = (line == 0) | (line == last)
        sign = (1 - 2 * (line & 1)).astype(jnp.float32)
        return line.astype(jnp.float32), jnp.sin(angle), jnp.cos(angle), edge, sign

    def column(x):
        return jnp.broadcast_to(x[0:1], (lane, rows)).T

    for s in range(n):
        line, sine, cosine, edge, sign = table(s)
        here = pl.ds(s * rows, rows)
        line_col[here, :] = column(line)
        sin_col[here, :] = column(sine)
        cos_col[here, :] = column(cosine)
        back_col[here, :] = column(jnp.where(edge, 0.5 * sign, sign))

    for index, s in enumerate(slots):
        line, sine, cosine, edge, sign = table(s)
        front = (-math.pi / last) * sine * cosine * jnp.where(edge, 2.0 * sign, sign)
        for p in range(rows // lane):
            here = pl.ds(index * rows + p * lane, lane)
            own = pl.ds(s * rows + p * lane, lane)
            line_i, sin_i, cos_i, front_i = (
                x[0:1, p * lane : (p + 1) * lane] for x in (line, sine, cosine, front)
            )
            total[...] = jnp.zeros_like(total)

            def block(t, carry):
                down = pl.ds(pl.multiple_of(t * step, step), step)
                gap = line_i - line_col[down, :]
                same = gap == 0.0
                x = half * gap
                x2 = x * x
                poly = -1.0 / 39916800.0
                for c in (1 / 362880.0, -1 / 5040.0, 1 / 120.0, -1 / 6.0, 1.0):
                    poly = poly * x2 + c
                plus = sin_i * cos_col[down, :] + cos_i * sin_col[down, :]
                denom = jnp.where(same, 1.0, plus * (x * poly))
                off = jnp.where(same, 0.0, front_i * back_col[down, :] / denom)
                total[...] += jnp.sum(off.reshape(step // 8, 8, lane), axis=0)
                out[down, here] = off.astype(jnp.bfloat16)
                return carry

            lax.fori_loop(0, size // step, block, 0)
            diagonal = -jnp.sum(total[...], axis=0, keepdims=True)
            same = lax.broadcasted_iota(jnp.int32, (lane, lane), 0) == (
                lax.broadcasted_iota(jnp.int32, (lane, lane), 1)
            )
            tile = out[own, here].astype(jnp.float32)
            out[own, here] = jnp.where(same, diagonal, tile).astype(jnp.bfloat16)


def weights_of(parts, grids, s, down=slice(None)):
    for part, grid in zip(parts, grids):
        if s in part:
            rows = grid.shape[1] // len(part)
            at = part.index(s) * rows
            return grid[down, at : at + rows]


def flip_kernel(n, parts, far, *refs):
    grids, out = refs[: len(parts)], refs[-1]
    rows = out.shape[0] // n
    line = lax.broadcasted_iota(jnp.int32, (rows, rows), 0)
    turn = line + lax.broadcasted_iota(jnp.int32, (rows, rows), 1) == rows - 1
    turn = jnp.where(turn, 1.0, 0.0).astype(jnp.bfloat16)
    for k, s in enumerate(far):
        for a in range(n):
            down = (a ^ (n - 1)) * rows
            tile = weights_of(parts, grids, s ^ (n - 1), slice(down, down + rows))
            tile = jnp.dot(turn, tile, preferred_element_type=jnp.float32).astype(jnp.bfloat16)
            tile = -jnp.dot(tile, turn, preferred_element_type=jnp.float32)
            out[a * rows : (a + 1) * rows, k * rows : (k + 1) * rows] = tile.astype(jnp.bfloat16)


def far_first(arrays):
    half = len(arrays) // 2
    return [arrays[0], *arrays[half:], *arrays[1:half]]


def in_slots(arrays):
    half = len(arrays) // 2
    return [arrays[0], *arrays[half + 1 :], *arrays[1 : half + 1]]


def section_kernel(n, two, second, far, parts, me_ref, *refs):
    grids, refs = refs[: len(parts)], refs[len(parts) :]
    firsts, refs = in_slots(refs[:n]), refs[n:]
    if second:
        rests, refs = in_slots(refs[:n]), refs[n + 1 :]
    outs, refs = refs[: len(far)], refs[len(far) :]
    u1, r0, fy1, u0, fy0, product, turned = refs
    wide, size = u0.shape[1:]
    rows = size // n
    core = wide - 2 * HALO
    me = me_ref[0]
    right_first = me % 2 == 0
    lane = min(rows, 128)
    strips = rows // lane

    part = wide - 2 * SKIP
    lap = 2 * NEED
    for s in range(n):
        for f in range(MOMENTS):
            if not two:
                u0[f, :, pl.ds(s * rows, rows)] = decode(f, firsts[s][f].astype(jnp.float32))
                continue
            whole = decode(f, firsts[s][f].astype(jnp.float32))
            for p in range(strips):
                here = pl.ds(s * rows + p * lane, lane)
                first = whole[p * part : (p + 1) * part]
                u0[f, 0:8, here] = jnp.zeros((8, lane), jnp.float32)
                u0[f, wide - 8 :, here] = jnp.zeros((8, lane), jnp.float32)
                if not second:
                    u0[f, SKIP : SKIP + part, here] = first
                    continue
                new = rests[s][f, :, p * lane : (p + 1) * lane].astype(jnp.float32)
                new = decode(f, new)
                left = jnp.concatenate([new, first[:lap]], axis=0)
                right = jnp.concatenate([first[part - lap :], new], axis=0)
                u0[f, SKIP : SKIP + part, here] = jnp.where(right_first, left, right)

    for s in range(n):
        for p in range(strips):
            here = pl.ds(s * rows + p * lane, lane)
            u = [u0[f, :, here] for f in range(MOMENTS)]
            for f in range(MOMENTS):
                fy0[f * wide : (f + 1) * wide, here] = flux(u, 1, f).astype(jnp.bfloat16)

    middle = slice(HALO, HALO + core)
    for s in range(n):
        weights = weights_of(parts, grids, s)
        product[...] = jnp.dot(fy0[...], weights, preferred_element_type=jnp.float32)
        for p in range(strips):
            here = pl.ds(s * rows + p * lane, lane)
            there = pl.ds(p * lane, lane)
            u = [u0[f, :, here] for f in range(MOMENTS)]
            src = sources(u, walls(me, s, p, n, rows, wide))
            new = []
            for f in range(MOMENTS):
                across = product[f * wide : (f + 1) * wide, there]
                rate = -(along_of(flux(u, 0, f), turned, f)[...] + across)
                if src[f] is not None:
                    rate = rate + src[f]
                r0[f, :, here] = rate[middle]
                new.append(u[f] + time_step * rate)
                u1[f, :, here] = new[f]
            inner = [x[middle] for x in new]
            for f in range(MOMENTS):
                fy1[f * core : (f + 1) * core, here] = flux(inner, 1, f).astype(jnp.bfloat16)

    finish(n, far, me_ref, parts, grids, u1, r0, fy1, outs, product, turned)


def finish_kernel(n, near, parts, chunks, me_ref, *refs):
    grids, refs = refs[: len(parts)], refs[len(parts) :]
    states, outs, product, turned = refs[: 3 * chunks], refs[-2 - len(near) : -2], *refs[-2:]
    core = outs[0].shape[1] // chunks
    for c in range(chunks):
        part = [out.at[:, c * core : (c + 1) * core, :] for out in outs]
        finish(n, near, me_ref, parts, grids, *states[3 * c : 3 * c + 3], part, product, turned)


def walls(me, s, p, n, rows, count):
    lane = min(rows, 128)
    line = jnp.bitwise_xor(me, s) * rows + p * lane
    line = line + lax.broadcasted_iota(jnp.int32, (count, lane), 1)
    return jnp.where(line == 0, 1.0, jnp.where(line == n * rows - 1, -1.0, 0.0))


def finish(n, slots, me_ref, parts, grids, u1, r0, fy1, outs, product, turned):
    wide, size = u1.shape[1:]
    rows = size // n
    core = wide - 2 * HALO
    lane = min(rows, 128)
    me = me_ref[0]
    middle = slice(HALO, HALO + core)
    for k, s in enumerate(slots):
        weights = weights_of(parts, grids, s)
        product[0 : MOMENTS * core, :] = jnp.dot(
            fy1[...], weights, preferred_element_type=jnp.float32
        )
        for p in range(rows // lane):
            here = pl.ds(s * rows + p * lane, lane)
            there = pl.ds(p * lane, lane)
            u = [u1[f, :, here] for f in range(MOMENTS)]
            inner = [x[middle] for x in u]
            src = sources(inner, walls(me, s, p, n, rows, core))
            for f in range(MOMENTS):
                across = product[f * core : (f + 1) * core, there]
                rate = -(along_of(flux(u, 0, f), turned, f)[middle, :] + across)
                if src[f] is not None:
                    rate = rate + src[f]
                rate = 0.5 * (r0[f, :, here] + rate)
                outs[k][f, :, there] = rate.astype(outs[k].dtype)


def arrived_kernel(*refs):
    refs[-1][...] = jnp.zeros_like(refs[-1])


def unpack_kernel(n, far, near, chunks, me_ref, *refs):
    staying, refs = refs[: len(near)], refs[len(near) :]
    out, tall, held, leaving = refs[-4:]
    cols = tall.shape[1]
    slab = cols // n
    width = slab // chunks
    me = me_ref[0]
    copies = []
    for f in range(MOMENTS):
        for s in near + far:
            of = jnp.bitwise_xor(me, s)
            for c in range(chunks):
                start = of * slab
                if chunks == 2:
                    start += jnp.where(of % 2 == 0, width * (1 - c), width * c)
                here = pl.ds(pl.multiple_of(start, 16), width)
                if s in near:
                    piece = staying[near.index(s)][f, c * width : (c + 1) * width, :]
                else:
                    piece = refs[c * len(far) + far.index(s)][f]
                tall[f, here, :] = piece.astype(jnp.float32)
        held[f] = tall[f].T
        copies.append(pltpu.make_async_copy(held.at[f], out.at[f], leaving.at[f]))
        copies[f].start()
    for copy in copies:
        copy.wait()


def to_partner(array, n, s):
    return array if s == 0 else lax.ppermute(array, "gy", [(i, i ^ s) for i in range(n)])


def exchange(arrays, n, slots):
    pairs = list(zip(arrays, slots))[::-1]
    return [to_partner(array, n, s) for array, s in pairs][::-1]


def on_device(rho, vel, temp, stress, heat):
    rows, cols = rho.shape
    n = lax.axis_size("gy")
    ring = lax.axis_size("gx")
    size, slab = n * rows, cols // n
    two = slab % 32 == 0
    core = slab // 2 if two else slab
    wide = core + 2 * HALO
    lane = min(rows, 128)
    half = jnp.bfloat16
    me = lax.axis_index("gy").astype(jnp.int32).reshape(1)
    vel, stress, heat = (jnp.swapaxes(a, 0, 1) for a in (vel, stress, heat))

    def message(width, kind=half):
        return jax.ShapeDtypeStruct((MOMENTS, width, rows), kind)

    far, near = (tuple(range(n // 2, n)), tuple(range(n // 2)))
    inputs = (rho, vel, temp, stress, heat)

    def pack(arrays):
        sent = (MOMENTS, (wide - 2 * SKIP) * (rows // lane), lane)
        shapes = [jax.ShapeDtypeStruct(sent, half)] * n if two else []
        shapes += [message(cols + 2 * HALO)]
        return pl.pallas_call(
            functools.partial(pack_kernel, n, two),
            out_shape=shapes,
            in_specs=[SMEM] + [HBM] * len(arrays),
            out_specs=[ANY] * len(shapes),
            scratch_shapes=[
                pltpu.VMEM((MOMENTS, cols + 2 * HALO, rows), jnp.float32),
                pltpu.VMEM((MOMENTS, rows, cols), jnp.float32),
                pltpu.SemaphoreType.DMA((len(GROUPS),)),
            ]
            + [pltpu.VMEM(x.shape, x.dtype) for x in shapes]
            + [pltpu.SemaphoreType.DMA((len(shapes), len(GROUPS)))],
            compiler_params=params(56),
            cost_estimate=cost(2),
            name="pack",
        )(me, *arrays)

    firsts = []
    if two:
        *firsts, tall = pack(inputs)
        firsts = exchange(firsts, n, range(n))
    else:
        (tall,) = pack(inputs)

    def grid_of(slots, *ties):
        return pl.pallas_call(
            functools.partial(grid_kernel, n, rows, slots),
            out_shape=jax.ShapeDtypeStruct((size, len(slots) * rows), half),
            in_specs=[SMEM] + [ANY] * len(ties),
            out_specs=VMEM,
            scratch_shapes=[pltpu.VMEM((size, lane), jnp.float32)] * 4
            + [pltpu.VMEM((8, lane), jnp.float32)],
            compiler_params=params(24),
            cost_estimate=cost(1),
            name="grid",
        )(me, *ties)

    parts = (near[: n // 4], near[n // 4 :])
    grids = [grid_of(part) for part in parts]
    left, right = pl.pallas_call(
        edge_kernel,
        out_shape=[message(2 * HALO)] * 2,
        in_specs=[VMEM, ANY],
        out_specs=[VMEM] * 2,
        compiler_params=params(24),
        cost_estimate=cost(0.2),
        name="edges",
    )(tall, grids[0])
    up = [(i, (i + 1) % ring) for i in range(ring)]
    before = lax.ppermute(right, "gx", up)
    after = lax.ppermute(left, "gx", [(j, i) for i, j in up])
    turned = pl.pallas_call(
        functools.partial(flip_kernel, n, parts, far),
        out_shape=jax.ShapeDtypeStruct((size, len(far) * rows), half),
        in_specs=[VMEM] * 2,
        out_specs=VMEM,
        compiler_params=params(24),
        cost_estimate=cost(0.3),
        name="flip",
    )(*grids)
    all_parts, all_grids = (*parts, far), (*grids, turned)
    rests = pl.pallas_call(
        functools.partial(rest_kernel, n, two),
        out_shape=[message(core if two else wide)] * n,
        in_specs=[SMEM] + [VMEM] * 3,
        out_specs=[VMEM] * n,
        compiler_params=params(),
        cost_estimate=cost(0.2),
        name="rest",
    )(me, tall, before, after)
    rests = exchange(rests, n, range(n))

    def sections(second, *arrays):
        state = [
            jax.ShapeDtypeStruct((MOMENTS, wide, size), jnp.float32),
            jax.ShapeDtypeStruct((MOMENTS, core, size), jnp.float32),
            jax.ShapeDtypeStruct((MOMENTS * core, size), half),
        ]
        *crossing, u1, r0, fy1 = pl.pallas_call(
            functools.partial(section_kernel, n, two, second, far, all_parts),
            out_shape=[message(core)] * len(far) + state,
            in_specs=[SMEM] + [VMEM] * (len(arrays) + 3 - second) + [ANY] * second,
            out_specs=[VMEM] * (len(far) + 3),
            scratch_shapes=[
                pltpu.VMEM((MOMENTS, wide, size), jnp.float32),
                pltpu.VMEM((MOMENTS * wide, size), half),
                pltpu.VMEM((MOMENTS * wide, rows), jnp.float32),
                pltpu.VMEM((2 * MOMENTS, wide, lane), jnp.float32),
            ],
            compiler_params=params(24),
            cost_estimate=cost(6),
            name="sections",
        )(me, *all_grids, *arrays)
        return crossing, [u1, r0, fy1]

    def finished(states, *ties):
        return pl.pallas_call(
            functools.partial(finish_kernel, n, near, parts, len(states) // 3),
            out_shape=[message(slab, jnp.float32)] + [message(slab)] * (len(near) - 1),
            in_specs=[SMEM] + [VMEM] * (len(states) + 2) + [ANY] * len(ties),
            out_specs=[VMEM] * len(near),
            scratch_shapes=[
                pltpu.VMEM((MOMENTS * core, rows), jnp.float32),
                pltpu.VMEM((2 * MOMENTS, wide, lane), jnp.float32),
            ],
            compiler_params=params(24),
            cost_estimate=cost(4),
            name="finish",
        )(me, *grids, *states, *ties)

    if two:
        firsts, rests = far_first(firsts), far_first(rests)
        crossing, states = sections(False, *firsts)
        back = exchange(crossing, n, far)
        crossing, more = sections(True, *firsts, *rests, crossing[0])
        staying = finished(states + more, *back)
        back += exchange(crossing, n, far)
    else:
        crossing, states = sections(False, *far_first(rests))
        staying = finished(states)
        back = exchange(crossing, n, far)
    staying = exchange(staying, n, near)
    arrived = pl.pallas_call(
        arrived_kernel,
        out_shape=jax.ShapeDtypeStruct((8, 128), jnp.float32),
        in_specs=[ANY] * len(back),
        out_specs=VMEM,
        compiler_params=params(1),
        cost_estimate=cost(6),
        name="arrived",
    )(*back)
    out = pl.pallas_call(
        functools.partial(unpack_kernel, n, far, near, 2 if two else 1),
        out_shape=jax.ShapeDtypeStruct((MOMENTS, rows, cols), jnp.float32),
        in_specs=[SMEM] + [VMEM] * (len(staying) + len(back)) + [ANY],
        out_specs=ANY,
        scratch_shapes=[
            pltpu.VMEM((MOMENTS, cols, rows), jnp.float32),
            pltpu.VMEM((MOMENTS, rows, cols), jnp.float32),
            pltpu.SemaphoreType.DMA((MOMENTS,)),
        ],
        compiler_params=params(24),
        cost_estimate=cost(3),
        name="unpack",
    )(me, *staying, *back, arrived)
    return jnp.swapaxes(out, 0, 1)


def solution(mesh):
    return jax.shard_map(
        on_device,
        mesh=mesh,
        in_specs=(
            P("gy", "gx"),
            P("gy", None, "gx"),
            P("gy", "gx"),
            P("gy", None, "gx"),
            P("gy", None, "gx"),
        ),
        out_specs=P("gy", None, "gx"),
        check_vma=False,
    )
```

```python
import functools
import math

import jax
import jax.numpy as jnp
from jax import lax
from jax.experimental import pallas as pl
from jax.experimental.pallas import tpu as pltpu
from jax.sharding import PartitionSpec as P

time_step = 0.05
enforcement_weight = 4.0
plate_speed = 0.5
dissipation_speed = 0.25
coeffs = (0.75, -0.15, 1.0 / 60.0)

MOMENTS = 13
HALO = 8
NEED = 6
SKIP = HALO - NEED
RHO, TEMP = 0, 4
VMEM = pl.BlockSpec(memory_space=pltpu.VMEM)
ANY = pl.BlockSpec(memory_space=pl.ANY)
HBM = pl.BlockSpec(memory_space=pltpu.HBM)
SMEM = pl.BlockSpec(memory_space=pltpu.SMEM)


def cost(micros):
    return pl.CostEstimate(
        flops=int(micros * 1e9), bytes_accessed=int(micros * 3e6), transcendentals=0
    )


def params(mib=48):
    return pltpu.CompilerParams(vmem_limit_bytes=mib * 2**20)


def code(f, x):
    if f == RHO:
        return x - 1.25
    if f == TEMP:
        return jnp.exp2(160.0 * (x - 1.25))
    return x


def decode(f, y):
    if f == RHO:
        return y + 1.25
    if f == TEMP:
        return jnp.log2(y) * (1.0 / 160.0) + 1.25
    return y


def flux(u, d, f):
    v = u[1 + d]
    temperature = u[4]
    heat = u[10:13]
    s = [[u[5], u[6], u[8]], [u[6], u[7], u[9]], [u[8], u[9], None]]
    if f == 0:
        return u[0] * v
    if f < 4:
        i = f - 1
        out = u[1 + i] * v + s[i][d]
        return out + temperature if i == d else out
    if f == 4:
        return v * temperature + 2.0 / 3.0 * heat[d]
    if f < 10:
        i, j = ((0, 0), (0, 1), (1, 1), (0, 2), (1, 2))[f - 5]
        out = v * s[i][j]
        weight = {}
        if j == d:
            weight[i] = weight.get(i, 0.0) + 0.4
        if i == d:
            weight[j] = weight.get(j, 0.0) + 0.4
        if i == j:
            weight[d] = weight.get(d, 0.0) - 4.0 / 15.0
        for k, w in weight.items():
            out = out + w * heat[k]
        return out
    i = f - 10
    out = v * heat[i] + temperature * s[i][d]
    return out + 2.5 * temperature * temperature if i == d else out


def sources(u, wall):
    near = jnp.abs(wall)
    nu = u[0] * jnp.sqrt(u[4] * u[4] + 0.25)
    heavy, light = -0.8 * nu, -0.55 * nu
    out = [None] * MOMENTS
    out[1] = -enforcement_weight * near * (u[1] - plate_speed * wall)
    out[4] = -dissipation_speed * nu * u[4] - enforcement_weight * near * (u[4] - 1.0)
    for f in range(5, 10):
        out[f] = heavy * u[f]
    for f in range(10, 13):
        out[f] = light * u[f]
    return out


def along_of(fx, turned, f):
    count = fx.shape[0] // 8
    turned[f] = fx
    x = [turned[f, pl.ds(v, 8, stride=count), :] for v in range(count)]
    x = [pltpu.roll(y, 1, 0) for y in x[-3:]] + x + [pltpu.roll(y, 7, 0) for y in x[:3]]
    for v in range(count):
        total = None
        for k in range(3):
            term = coeffs[k] * (x[3 + v + k + 1] - x[3 + v - k - 1])
            total = term if total is None else total + term
        turned[MOMENTS + f, pl.ds(v, 8, stride=count), :] = total
    return turned.at[MOMENTS + f]


def message_start(me, s, slab):
    to = jnp.bitwise_xor(me, s)
    return pl.multiple_of(to * slab + jnp.where(to % 2 == 0, slab // 2, 0), 16)


GROUPS = ((0, 1), (1, 4), (4, 5), (5, 8), (8, 10), (10, 13))


def pack_kernel(n, two, me_ref, *refs):
    (rho, vel, temp, stress, heat), refs = refs[:5], refs[5:]
    inputs = (rho, vel, temp, stress.at[0:3], stress.at[3:5], heat)
    count = n if two else 0
    outs, (strip, given, arrived), refs = refs[: count + 1], refs[count + 1 : count + 4], refs[count + 4 :]
    held, left_at = refs[:-1], refs[-1]
    rows, cols = given.shape[1:]
    slab = cols // n
    me = me_ref[0]
    copies = []
    for k, (first, end) in enumerate(GROUPS):
        dst = given.at[first] if len(inputs[k].shape) == 2 else given.at[first:end]
        copies.append(pltpu.make_async_copy(inputs[k], dst, arrived.at[k]))
        copies[k].start()
    wide = slab // 2 + 2 * HALO
    lane = min(rows, 128)
    leaving = []
    done = 0
    for at, (first, end) in enumerate(GROUPS):
        copies[at].wait()
        for f in range(first, end):
            strip[f, 0:HALO, :] = jnp.zeros((HALO, rows), jnp.float32)
            strip[f, HALO + cols :, :] = jnp.zeros((HALO, rows), jnp.float32)
            strip[f, HALO : HALO + cols, :] = code(f, given[f]).T
            for s in range(count):
                block = strip[f, pl.ds(message_start(me, s, slab), wide), :][SKIP : wide - SKIP]
                halves = [block[:, p : p + lane] for p in range(0, rows, lane)]
                held[s][f] = jnp.concatenate(halves, axis=0).astype(jnp.bfloat16)
            held[count][f] = strip[f].astype(jnp.bfloat16)
        if at in (1, 3, 4, 5):
            span = pl.ds(done, end - done)
            for k, out in enumerate(outs):
                copy = pltpu.make_async_copy(held[k].at[span], out.at[span], left_at.at[k, at - 1])
                copy.start()
                leaving.append(copy)
            done = end
    for copy in leaving:
        copy.wait()


def edge_kernel(tall, tie, left, right):
    cols = tall.shape[1] - 2 * HALO
    left[...] = tall[:, 0 : 2 * HALO, :]
    right[...] = tall[:, cols : cols + 2 * HALO, :]


def rest_kernel(n, two, me_ref, tall, before, after, *outs):
    me = me_ref[0]
    slab = (tall.shape[1] - 2 * HALO) // n
    count = outs[0].shape[1]
    wide = slab // 2 + 2 * HALO if two else count
    line = lax.broadcasted_iota(jnp.int32, before.shape[1:], 0)
    for s in range(n):
        to = jnp.bitwise_xor(me, s)
        even = to % 2 == 0
        start = to * slab
        if two:
            start += jnp.where(even, 0, slab // 2)
        start = pl.multiple_of(start, 16)
        for f in range(MOMENTS):
            block = tall[f, pl.ds(start, wide), :].astype(jnp.float32)
            first, last = block[: 2 * HALO], block[wide - 2 * HALO :]
            first = jnp.where((line < HALO) & (to == 0), before[f].astype(jnp.float32), first)
            last = jnp.where((line >= HALO) & (to == n - 1), after[f].astype(jnp.float32), last)
            between = [block[2 * HALO : wide - 2 * HALO]] if wide > 4 * HALO else []
            block = jnp.concatenate([first, *between, last], axis=0)
            if two:
                near_end = block[SKIP : SKIP + count]
                far_end = block[wide - SKIP - count : wide - SKIP]
                block = jnp.where(even, near_end, far_end)
            outs[s][f] = block.astype(jnp.bfloat16)


def grid_kernel(n, rows, slots, me_ref, *refs):
    out, sin_col, cos_col, back_col, line_col, total = refs[-6:]
    size = n * rows
    last = size - 1
    half = math.pi / (2.0 * last)
    me = me_ref[0]
    step = 64
    lane = min(rows, 128)

    def table(s):
        line = jnp.bitwise_xor(me, s) * rows + lax.broadcasted_iota(jnp.int32, (8, rows), 1)
        angle = half * line.astype(jnp.float32)
        edge = (line == 0) | (line == last)
        sign = (1 - 2 * (line & 1)).astype(jnp.float32)
        return line.astype(jnp.float32), jnp.sin(angle), jnp.cos(angle), edge, sign

    def column(x):
        return jnp.broadcast_to(x[0:1], (lane, rows)).T

    for s in range(n):
        line, sine, cosine, edge, sign = table(s)
        here = pl.ds(s * rows, rows)
        line_col[here, :] = column(line)
        sin_col[here, :] = column(sine)
        cos_col[here, :] = column(cosine)
        back_col[here, :] = column(jnp.where(edge, 0.5 * sign, sign))

    for index, s in enumerate(slots):
        line, sine, cosine, edge, sign = table(s)
        front = (-math.pi / last) * sine * cosine * jnp.where(edge, 2.0 * sign, sign)
        for p in range(rows // lane):
            here = pl.ds(index * rows + p * lane, lane)
            own = pl.ds(s * rows + p * lane, lane)
            line_i, sin_i, cos_i, front_i = (
                x[0:1, p * lane : (p + 1) * lane] for x in (line, sine, cosine, front)
            )
            total[...] = jnp.zeros_like(total)

            def block(t, carry):
                down = pl.ds(pl.multiple_of(t * step, step), step)
                gap = line_i - line_col[down, :]
                same = gap == 0.0
                x = half * gap
                x2 = x * x
                poly = -1.0 / 39916800.0
                for c in (1 / 362880.0, -1 / 5040.0, 1 / 120.0, -1 / 6.0, 1.0):
                    poly = poly * x2 + c
                plus = sin_i * cos_col[down, :] + cos_i * sin_col[down, :]
                denom = jnp.where(same, 1.0, plus * (x * poly))
                off = jnp.where(same, 0.0, front_i * back_col[down, :] / denom)
                total[...] += jnp.sum(off.reshape(step // 8, 8, lane), axis=0)
                out[down, here] = off.astype(jnp.bfloat16)
                return carry

            lax.fori_loop(0, size // step, block, 0)
            diagonal = -jnp.sum(total[...], axis=0, keepdims=True)
            same = lax.broadcasted_iota(jnp.int32, (lane, lane), 0) == (
                lax.broadcasted_iota(jnp.int32, (lane, lane), 1)
            )
            tile = out[own, here].astype(jnp.float32)
            out[own, here] = jnp.where(same, diagonal, tile).astype(jnp.bfloat16)


def weights_of(parts, grids, s, down=slice(None)):
    for part, grid in zip(parts, grids):
        if s in part:
            rows = grid.shape[1] // len(part)
            at = part.index(s) * rows
            return grid[down, at : at + rows]


def flip_kernel(n, parts, far, *refs):
    grids, out = refs[: len(parts)], refs[-1]
    rows = out.shape[0] // n
    line = lax.broadcasted_iota(jnp.int32, (rows, rows), 0)
    turn = line + lax.broadcasted_iota(jnp.int32, (rows, rows), 1) == rows - 1
    turn = jnp.where(turn, 1.0, 0.0).astype(jnp.bfloat16)
    for k, s in enumerate(far):
        for a in range(n):
            down = (a ^ (n - 1)) * rows
            tile = weights_of(parts, grids, s ^ (n - 1), slice(down, down + rows))
            tile = jnp.dot(turn, tile, preferred_element_type=jnp.float32).astype(jnp.bfloat16)
            tile = -jnp.dot(tile, turn, preferred_element_type=jnp.float32)
            out[a * rows : (a + 1) * rows, k * rows : (k + 1) * rows] = tile.astype(jnp.bfloat16)


def far_first(arrays):
    half = len(arrays) // 2
    return [arrays[0], *arrays[half:], *arrays[1:half]]


def in_slots(arrays):
    half = len(arrays) // 2
    return [arrays[0], *arrays[half + 1 :], *arrays[1 : half + 1]]


def section_kernel(n, two, second, far, parts, me_ref, *refs):
    grids, refs = refs[: len(parts)], refs[len(parts) :]
    firsts, refs = in_slots(refs[:n]), refs[n:]
    if second:
        rests, refs = in_slots(refs[:n]), refs[n + 1 :]
    outs, refs = refs[: len(far)], refs[len(far) :]
    u1, r0, fy1, u0, fy0, product, turned = refs
    wide, size = u0.shape[1:]
    rows = size // n
    core = wide - 2 * HALO
    me = me_ref[0]
    right_first = me % 2 == 0
    lane = min(rows, 128)
    strips = rows // lane

    part = wide - 2 * SKIP
    lap = 2 * NEED
    for s in range(n):
        for f in range(MOMENTS):
            if not two:
                u0[f, :, pl.ds(s * rows, rows)] = decode(f, firsts[s][f].astype(jnp.float32))
                continue
            whole = decode(f, firsts[s][f].astype(jnp.float32))
            for p in range(strips):
                here = pl.ds(s * rows + p * lane, lane)
                first = whole[p * part : (p + 1) * part]
                u0[f, 0:8, here] = jnp.zeros((8, lane), jnp.float32)
                u0[f, wide - 8 :, here] = jnp.zeros((8, lane), jnp.float32)
                if not second:
                    u0[f, SKIP : SKIP + part, here] = first
                    continue
                new = rests[s][f, :, p * lane : (p + 1) * lane].astype(jnp.float32)
                new = decode(f, new)
                left = jnp.concatenate([new, first[:lap]], axis=0)
                right = jnp.concatenate([first[part - lap :], new], axis=0)
                u0[f, SKIP : SKIP + part, here] = jnp.where(right_first, left, right)

    for s in range(n):
        for p in range(strips):
            here = pl.ds(s * rows + p * lane, lane)
            u = [u0[f, :, here] for f in range(MOMENTS)]
            for f in range(MOMENTS):
                fy0[f * wide : (f + 1) * wide, here] = flux(u, 1, f).astype(jnp.bfloat16)

    middle = slice(HALO, HALO + core)
    for s in range(n):
        weights = weights_of(parts, grids, s)
        product[...] = jnp.dot(fy0[...], weights, preferred_element_type=jnp.float32)
        for p in range(strips):
            here = pl.ds(s * rows + p * lane, lane)
            there = pl.ds(p * lane, lane)
            u = [u0[f, :, here] for f in range(MOMENTS)]
            src = sources(u, walls(me, s, p, n, rows, wide))
            new = []
            for f in range(MOMENTS):
                across = product[f * wide : (f + 1) * wide, there]
                rate = -(along_of(flux(u, 0, f), turned, f)[...] + across)
                if src[f] is not None:
                    rate = rate + src[f]
                r0[f, :, here] = rate[middle]
                new.append(u[f] + time_step * rate)
                u1[f, :, here] = new[f]
            inner = [x[middle] for x in new]
            for f in range(MOMENTS):
                fy1[f * core : (f + 1) * core, here] = flux(inner, 1, f).astype(jnp.bfloat16)

    def place(s, f):
        return outs[far.index(s)].at[f]

    finish(n, far, me_ref, parts, grids, u1, r0, fy1, place, product, turned)


THIRDS = ((0, 5), (5, 9), (9, MOMENTS))


def finish_kernel(n, near, parts, chunks, me_ref, *refs):
    grids, refs = refs[: len(parts)], refs[len(parts) :]
    states, product, turned = refs[: 3 * chunks], *refs[-2:]
    outs = refs[-2 - 1 - len(THIRDS) * (len(near) - 1) : -2]
    core = outs[0].shape[1] // chunks

    def place(c, s, f):
        span = slice(c * core, (c + 1) * core)
        if s == 0:
            return outs[0].at[f, span]
        third = [first <= f < end for first, end in THIRDS].index(True)
        return outs[1 + len(THIRDS) * (s - 1) + third].at[f - THIRDS[third][0], span]

    for c in range(chunks):
        part = functools.partial(place, c)
        finish(n, near, me_ref, parts, grids, *states[3 * c : 3 * c + 3], part, product, turned)


def walls(me, s, p, n, rows, count):
    lane = min(rows, 128)
    line = jnp.bitwise_xor(me, s) * rows + p * lane
    line = line + lax.broadcasted_iota(jnp.int32, (count, lane), 1)
    return jnp.where(line == 0, 1.0, jnp.where(line == n * rows - 1, -1.0, 0.0))


def finish(n, slots, me_ref, parts, grids, u1, r0, fy1, outs, product, turned):
    wide, size = u1.shape[1:]
    rows = size // n
    core = wide - 2 * HALO
    lane = min(rows, 128)
    me = me_ref[0]
    middle = slice(HALO, HALO + core)
    for k, s in enumerate(slots):
        weights = weights_of(parts, grids, s)
        product[0 : MOMENTS * core, :] = jnp.dot(
            fy1[...], weights, preferred_element_type=jnp.float32
        )
        for p in range(rows // lane):
            here = pl.ds(s * rows + p * lane, lane)
            there = pl.ds(p * lane, lane)
            u = [u1[f, :, here] for f in range(MOMENTS)]
            inner = [x[middle] for x in u]
            src = sources(inner, walls(me, s, p, n, rows, core))
            for f in range(MOMENTS):
                across = product[f * core : (f + 1) * core, there]
                rate = -(along_of(flux(u, 0, f), turned, f)[middle, :] + across)
                if src[f] is not None:
                    rate = rate + src[f]
                rate = 0.5 * (r0[f, :, here] + rate)
                target = outs(s, f)
                target[:, there] = rate.astype(target.dtype)


def arrived_kernel(*refs):
    refs[-1][...] = jnp.zeros_like(refs[-1])


def unpack_kernel(n, slots, chunks, pieces, me_ref, *refs):
    out, token, tall, held, leaving = refs[-5:]
    token[...] = jnp.zeros_like(token)
    rows, cols = held.shape[1:]
    slab = cols // len(slots)
    width = slab // chunks
    me = me_ref[0]
    copies = []
    for f in range(MOMENTS):
        for array, (s, c, first, end) in zip(refs, pieces):
            if not first <= f < end:
                continue
            of = jnp.bitwise_xor(me, s)
            for k in range(chunks) if c is None else (c,):
                start = of % len(slots) * slab
                if chunks == 2:
                    start += jnp.where(of % 2 == 0, width * (1 - k), width * k)
                here = pl.ds(pl.multiple_of(start, 16), width)
                piece = array[f - first, k * width : (k + 1) * width] if c is None else array[f]
                tall[f, here, :] = piece.astype(jnp.float32)
        held[f] = tall[f].T
        side = jnp.bitwise_xor(me, slots[0]) // len(slots) * cols
        there = out.at[f, :, pl.ds(pl.multiple_of(side, 128), cols)]
        copies.append(pltpu.make_async_copy(held.at[f], there, leaving.at[f]))
        copies[f].start()
    for copy in copies:
        copy.wait()


def to_partner(array, n, s):
    return array if s == 0 else lax.ppermute(array, "gy", [(i, i ^ s) for i in range(n)])


def exchange(arrays, n, slots):
    pairs = list(zip(arrays, slots))[::-1]
    return [to_partner(array, n, s) for array, s in pairs][::-1]


def on_device(rho, vel, temp, stress, heat):
    rows, cols = rho.shape
    n = lax.axis_size("gy")
    ring = lax.axis_size("gx")
    size, slab = n * rows, cols // n
    two = slab % 32 == 0
    core = slab // 2 if two else slab
    wide = core + 2 * HALO
    lane = min(rows, 128)
    half = jnp.bfloat16
    me = lax.axis_index("gy").astype(jnp.int32).reshape(1)
    vel, stress, heat = (jnp.swapaxes(a, 0, 1) for a in (vel, stress, heat))

    def message(width, kind=half):
        return jax.ShapeDtypeStruct((MOMENTS, width, rows), kind)

    far, near = (tuple(range(n // 2, n)), tuple(range(n // 2)))
    inputs = (rho, vel, temp, stress, heat)

    def pack(arrays):
        sent = (MOMENTS, (wide - 2 * SKIP) * (rows // lane), lane)
        shapes = [jax.ShapeDtypeStruct(sent, half)] * n if two else []
        shapes += [message(cols + 2 * HALO)]
        return pl.pallas_call(
            functools.partial(pack_kernel, n, two),
            out_shape=shapes,
            in_specs=[SMEM] + [HBM] * len(arrays),
            out_specs=[ANY] * len(shapes),
            scratch_shapes=[
                pltpu.VMEM((MOMENTS, cols + 2 * HALO, rows), jnp.float32),
                pltpu.VMEM((MOMENTS, rows, cols), jnp.float32),
                pltpu.SemaphoreType.DMA((len(GROUPS),)),
            ]
            + [pltpu.VMEM(x.shape, x.dtype) for x in shapes]
            + [pltpu.SemaphoreType.DMA((len(shapes), len(GROUPS)))],
            compiler_params=params(56),
            cost_estimate=cost(2),
            name="pack",
        )(me, *arrays)

    firsts = []
    if two:
        *firsts, tall = pack(inputs)
        firsts = exchange(firsts, n, range(n))
    else:
        (tall,) = pack(inputs)

    def grid_of(slots, *ties):
        return pl.pallas_call(
            functools.partial(grid_kernel, n, rows, slots),
            out_shape=jax.ShapeDtypeStruct((size, len(slots) * rows), half),
            in_specs=[SMEM] + [ANY] * len(ties),
            out_specs=VMEM,
            scratch_shapes=[pltpu.VMEM((size, lane), jnp.float32)] * 4
            + [pltpu.VMEM((8, lane), jnp.float32)],
            compiler_params=params(24),
            cost_estimate=cost(1),
            name="grid",
        )(me, *ties)

    parts = (near[: n // 4], near[n // 4 :])
    grids = [grid_of(part) for part in parts]
    left, right = pl.pallas_call(
        edge_kernel,
        out_shape=[message(2 * HALO)] * 2,
        in_specs=[VMEM, ANY],
        out_specs=[VMEM] * 2,
        compiler_params=params(24),
        cost_estimate=cost(0.2),
        name="edges",
    )(tall, grids[0])
    up = [(i, (i + 1) % ring) for i in range(ring)]
    before = lax.ppermute(right, "gx", up)
    after = lax.ppermute(left, "gx", [(j, i) for i, j in up])
    turned = pl.pallas_call(
        functools.partial(flip_kernel, n, parts, far),
        out_shape=jax.ShapeDtypeStruct((size, len(far) * rows), half),
        in_specs=[VMEM] * 2,
        out_specs=VMEM,
        compiler_params=params(24),
        cost_estimate=cost(0.3),
        name="flip",
    )(*grids)
    all_parts, all_grids = (*parts, far), (*grids, turned)
    rests = pl.pallas_call(
        functools.partial(rest_kernel, n, two),
        out_shape=[message(core if two else wide)] * n,
        in_specs=[SMEM] + [VMEM] * 3,
        out_specs=[VMEM] * n,
        compiler_params=params(),
        cost_estimate=cost(0.2),
        name="rest",
    )(me, tall, before, after)
    rests = exchange(rests, n, range(n))

    def sections(second, *arrays):
        state = [
            jax.ShapeDtypeStruct((MOMENTS, wide, size), jnp.float32),
            jax.ShapeDtypeStruct((MOMENTS, core, size), jnp.float32),
            jax.ShapeDtypeStruct((MOMENTS * core, size), half),
        ]
        *crossing, u1, r0, fy1 = pl.pallas_call(
            functools.partial(section_kernel, n, two, second, far, all_parts),
            out_shape=[message(core)] * len(far) + state,
            in_specs=[SMEM] + [VMEM] * (len(arrays) + 3 - second) + [ANY] * second,
            out_specs=[VMEM] * (len(far) + 3),
            scratch_shapes=[
                pltpu.VMEM((MOMENTS, wide, size), jnp.float32),
                pltpu.VMEM((MOMENTS * wide, size), half),
                pltpu.VMEM((MOMENTS * wide, rows), jnp.float32),
                pltpu.VMEM((2 * MOMENTS, wide, lane), jnp.float32),
            ],
            compiler_params=params(24),
            cost_estimate=cost(6),
            name="sections",
        )(me, *all_grids, *arrays)
        return crossing, [u1, r0, fy1]

    def finished(states, *ties):
        thirds = [jax.ShapeDtypeStruct((end - first, slab, rows), half) for first, end in THIRDS]
        shapes = [message(slab, jnp.float32)] + thirds * (len(near) - 1)
        own, *others = pl.pallas_call(
            functools.partial(finish_kernel, n, near, parts, len(states) // 3),
            out_shape=shapes,
            in_specs=[SMEM] + [VMEM] * (len(states) + 2) + [ANY] * len(ties),
            out_specs=[VMEM] * len(shapes),
            scratch_shapes=[
                pltpu.VMEM((MOMENTS * core, rows), jnp.float32),
                pltpu.VMEM((2 * MOMENTS, wide, lane), jnp.float32),
            ],
            compiler_params=params(24),
            cost_estimate=cost(4),
            name="finish",
        )(me, *grids, *states, *ties)
        slots = [s for s in near[1:] for _ in THIRDS]
        return [own, *exchange(others, n, slots)]

    if two:
        firsts, rests = far_first(firsts), far_first(rests)
        crossing, states = sections(False, *firsts)
        back = exchange(crossing, n, far)
        crossing, more = sections(True, *firsts, *rests, crossing[0])
        staying = finished(states + more, *back)
        back += exchange(crossing, n, far)
    else:
        crossing, states = sections(False, *far_first(rests))
        staying = finished(states)
        back = exchange(crossing, n, far)
    chunks = 2 if two else 1
    token = jax.ShapeDtypeStruct((8, 128), jnp.float32)

    def unpack(slots, arrays, pieces, *before):
        alias = {1 + len(arrays): 0} if before else {}
        return pl.pallas_call(
            functools.partial(unpack_kernel, n, slots, chunks, pieces),
            out_shape=[jax.ShapeDtypeStruct((MOMENTS, rows, cols), jnp.float32), token],
            in_specs=[SMEM] + [VMEM] * len(arrays) + [ANY] * len(before),
            out_specs=[ANY, VMEM],
            scratch_shapes=[
                pltpu.VMEM((MOMENTS, cols // 2, rows), jnp.float32),
                pltpu.VMEM((MOMENTS, rows, cols // 2), jnp.float32),
                pltpu.SemaphoreType.DMA((MOMENTS,)),
            ],
            input_output_aliases=alias,
            compiler_params=params(24),
            cost_estimate=cost(0.01),
            name="unpack",
        )(me, *arrays, *before)

    pieces = [(0, None, 0, MOMENTS)] + [(s, None, *span) for s in near[1:] for span in THIRDS]
    out, turned_near = unpack(near, staying, tuple(pieces))
    arrived = pl.pallas_call(
        arrived_kernel,
        out_shape=token,
        in_specs=[ANY] * (len(back) + 1),
        out_specs=VMEM,
        compiler_params=params(1),
        cost_estimate=cost(6),
        name="arrived",
    )(*back, turned_near)
    pieces = [(s, c, 0, MOMENTS) for c in range(chunks) for s in far]
    out, _ = unpack(far, back, tuple(pieces), out, arrived)
    return jnp.swapaxes(out, 0, 1)


def solution(mesh):
    return jax.shard_map(
        on_device,
        mesh=mesh,
        in_specs=(
            P("gy", "gx"),
            P("gy", None, "gx"),
            P("gy", "gx"),
            P("gy", None, "gx"),
            P("gy", None, "gx"),
        ),
        out_specs=P("gy", None, "gx"),
        check_vma=False,
    )
```

```python
import functools
import math

import jax
import jax.numpy as jnp
from jax import lax
from jax.experimental import pallas as pl
from jax.experimental.pallas import tpu as pltpu
from jax.sharding import PartitionSpec as P

time_step = 0.05
enforcement_weight = 4.0
plate_speed = 0.5
dissipation_speed = 0.25
coeffs = (0.75, -0.15, 1.0 / 60.0)

MOMENTS = 13
HALO = 8
NEED = 6
SKIP = HALO - NEED
RHO, TEMP = 0, 4
VMEM = pl.BlockSpec(memory_space=pltpu.VMEM)
ANY = pl.BlockSpec(memory_space=pl.ANY)
HBM = pl.BlockSpec(memory_space=pltpu.HBM)
SMEM = pl.BlockSpec(memory_space=pltpu.SMEM)


def cost(micros):
    return pl.CostEstimate(
        flops=int(micros * 1e9), bytes_accessed=int(micros * 3e6), transcendentals=0
    )


def params(mib=48):
    return pltpu.CompilerParams(vmem_limit_bytes=mib * 2**20)


def code(f, x):
    if f == RHO:
        return x - 1.25
    if f == TEMP:
        return jnp.exp2(160.0 * (x - 1.25))
    return x


def decode(f, y):
    if f == RHO:
        return y + 1.25
    if f == TEMP:
        return jnp.log2(y) * (1.0 / 160.0) + 1.25
    return y


def flux(u, d, f):
    v = u[1 + d]
    temperature = u[4]
    heat = u[10:13]
    s = [[u[5], u[6], u[8]], [u[6], u[7], u[9]], [u[8], u[9], None]]
    if f == 0:
        return u[0] * v
    if f < 4:
        i = f - 1
        out = u[1 + i] * v + s[i][d]
        return out + temperature if i == d else out
    if f == 4:
        return v * temperature + 2.0 / 3.0 * heat[d]
    if f < 10:
        i, j = ((0, 0), (0, 1), (1, 1), (0, 2), (1, 2))[f - 5]
        out = v * s[i][j]
        weight = {}
        if j == d:
            weight[i] = weight.get(i, 0.0) + 0.4
        if i == d:
            weight[j] = weight.get(j, 0.0) + 0.4
        if i == j:
            weight[d] = weight.get(d, 0.0) - 4.0 / 15.0
        for k, w in weight.items():
            out = out + w * heat[k]
        return out
    i = f - 10
    out = v * heat[i] + temperature * s[i][d]
    return out + 2.5 * temperature * temperature if i == d else out


def sources(u, wall):
    near = jnp.abs(wall)
    nu = u[0] * jnp.sqrt(u[4] * u[4] + 0.25)
    heavy, light = -0.8 * nu, -0.55 * nu
    out = [None] * MOMENTS
    out[1] = -enforcement_weight * near * (u[1] - plate_speed * wall)
    out[4] = -dissipation_speed * nu * u[4] - enforcement_weight * near * (u[4] - 1.0)
    for f in range(5, 10):
        out[f] = heavy * u[f]
    for f in range(10, 13):
        out[f] = light * u[f]
    return out


def along_of(fx, turned, f):
    count = fx.shape[0] // 8
    turned[f] = fx
    x = [turned[f, pl.ds(v, 8, stride=count), :] for v in range(count)]
    x = [pltpu.roll(y, 1, 0) for y in x[-3:]] + x + [pltpu.roll(y, 7, 0) for y in x[:3]]
    for v in range(count):
        total = None
        for k in range(3):
            term = coeffs[k] * (x[3 + v + k + 1] - x[3 + v - k - 1])
            total = term if total is None else total + term
        turned[MOMENTS + f, pl.ds(v, 8, stride=count), :] = total
    return turned.at[MOMENTS + f]


def message_start(me, s, slab):
    to = jnp.bitwise_xor(me, s)
    return pl.multiple_of(to * slab + jnp.where(to % 2 == 0, slab // 2, 0), 16)


GROUPS = ((0, 1), (1, 4), (4, 5), (5, 8), (8, 10), (10, 13))


def pack_kernel(n, two, me_ref, *refs):
    (rho, vel, temp, stress, heat), refs = refs[:5], refs[5:]
    inputs = (rho, vel, temp, stress.at[0:3], stress.at[3:5], heat)
    count = n if two else 0
    outs, (strip, given, arrived), refs = refs[: count + 1], refs[count + 1 : count + 4], refs[count + 4 :]
    held, left_at = refs[:-1], refs[-1]
    rows, cols = given.shape[1:]
    slab = cols // n
    me = me_ref[0]
    copies = []
    for k, (first, end) in enumerate(GROUPS):
        dst = given.at[first] if len(inputs[k].shape) == 2 else given.at[first:end]
        copies.append(pltpu.make_async_copy(inputs[k], dst, arrived.at[k]))
        copies[k].start()
    wide = slab // 2 + 2 * HALO
    lane = min(rows, 128)
    leaving = []
    done = 0
    for at, (first, end) in enumerate(GROUPS):
        copies[at].wait()
        for f in range(first, end):
            strip[f, 0:HALO, :] = jnp.zeros((HALO, rows), jnp.float32)
            strip[f, HALO + cols :, :] = jnp.zeros((HALO, rows), jnp.float32)
            strip[f, HALO : HALO + cols, :] = code(f, given[f]).T
            for s in range(count):
                block = strip[f, pl.ds(message_start(me, s, slab), wide), :][SKIP : wide - SKIP]
                halves = [block[:, p : p + lane] for p in range(0, rows, lane)]
                held[s][f] = jnp.concatenate(halves, axis=0).astype(jnp.bfloat16)
            held[count][f] = strip[f].astype(jnp.bfloat16)
        if at in (1, 3, 4, 5):
            span = pl.ds(done, end - done)
            for k, out in enumerate(outs):
                copy = pltpu.make_async_copy(held[k].at[span], out.at[span], left_at.at[k, at - 1])
                copy.start()
                leaving.append(copy)
            done = end
    for copy in leaving:
        copy.wait()


def edge_kernel(tall, tie, left, right):
    cols = tall.shape[1] - 2 * HALO
    left[...] = tall[:, 0 : 2 * HALO, :]
    right[...] = tall[:, cols : cols + 2 * HALO, :]


def rest_kernel(n, two, me_ref, tall, before, after, *outs):
    me = me_ref[0]
    slab = (tall.shape[1] - 2 * HALO) // n
    count = outs[0].shape[1]
    wide = slab // 2 + 2 * HALO if two else count
    line = lax.broadcasted_iota(jnp.int32, before.shape[1:], 0)
    for s in range(n):
        to = jnp.bitwise_xor(me, s)
        even = to % 2 == 0
        start = to * slab
        if two:
            start += jnp.where(even, 0, slab // 2)
        start = pl.multiple_of(start, 16)
        for f in range(MOMENTS):
            block = tall[f, pl.ds(start, wide), :].astype(jnp.float32)
            first, last = block[: 2 * HALO], block[wide - 2 * HALO :]
            first = jnp.where((line < HALO) & (to == 0), before[f].astype(jnp.float32), first)
            last = jnp.where((line >= HALO) & (to == n - 1), after[f].astype(jnp.float32), last)
            between = [block[2 * HALO : wide - 2 * HALO]] if wide > 4 * HALO else []
            block = jnp.concatenate([first, *between, last], axis=0)
            if two:
                near_end = block[SKIP : SKIP + count]
                far_end = block[wide - SKIP - count : wide - SKIP]
                block = jnp.where(even, near_end, far_end)
            outs[s][f] = block.astype(jnp.bfloat16)


def grid_kernel(n, rows, slots, me_ref, *refs):
    out, sin_col, cos_col, back_col, line_col, total = refs[-6:]
    size = n * rows
    last = size - 1
    half = math.pi / (2.0 * last)
    me = me_ref[0]
    step = 64
    lane = min(rows, 128)

    def table(s):
        line = jnp.bitwise_xor(me, s) * rows + lax.broadcasted_iota(jnp.int32, (8, rows), 1)
        angle = half * line.astype(jnp.float32)
        edge = (line == 0) | (line == last)
        sign = (1 - 2 * (line & 1)).astype(jnp.float32)
        return line.astype(jnp.float32), jnp.sin(angle), jnp.cos(angle), edge, sign

    def column(x):
        return jnp.broadcast_to(x[0:1], (lane, rows)).T

    for s in range(n):
        line, sine, cosine, edge, sign = table(s)
        here = pl.ds(s * rows, rows)
        line_col[here, :] = column(line)
        sin_col[here, :] = column(sine)
        cos_col[here, :] = column(cosine)
        back_col[here, :] = column(jnp.where(edge, 0.5 * sign, sign))

    for index, s in enumerate(slots):
        line, sine, cosine, edge, sign = table(s)
        front = (-math.pi / last) * sine * cosine * jnp.where(edge, 2.0 * sign, sign)
        for p in range(rows // lane):
            here = pl.ds(index * rows + p * lane, lane)
            own = pl.ds(s * rows + p * lane, lane)
            line_i, sin_i, cos_i, front_i = (
                x[0:1, p * lane : (p + 1) * lane] for x in (line, sine, cosine, front)
            )
            total[...] = jnp.zeros_like(total)

            def block(t, carry):
                down = pl.ds(pl.multiple_of(t * step, step), step)
                gap = line_i - line_col[down, :]
                same = gap == 0.0
                x = half * gap
                x2 = x * x
                poly = -1.0 / 39916800.0
                for c in (1 / 362880.0, -1 / 5040.0, 1 / 120.0, -1 / 6.0, 1.0):
                    poly = poly * x2 + c
                plus = sin_i * cos_col[down, :] + cos_i * sin_col[down, :]
                denom = jnp.where(same, 1.0, plus * (x * poly))
                off = jnp.where(same, 0.0, front_i * back_col[down, :] / denom)
                total[...] += jnp.sum(off.reshape(step // 8, 8, lane), axis=0)
                out[down, here] = off.astype(jnp.bfloat16)
                return carry

            lax.fori_loop(0, size // step, block, 0)
            diagonal = -jnp.sum(total[...], axis=0, keepdims=True)
            same = lax.broadcasted_iota(jnp.int32, (lane, lane), 0) == (
                lax.broadcasted_iota(jnp.int32, (lane, lane), 1)
            )
            tile = out[own, here].astype(jnp.float32)
            out[own, here] = jnp.where(same, diagonal, tile).astype(jnp.bfloat16)


def weights_of(parts, grids, s, down=slice(None)):
    for part, grid in zip(parts, grids):
        if s in part:
            rows = grid.shape[1] // len(part)
            at = part.index(s) * rows
            return grid[down, at : at + rows]


def flip_kernel(n, parts, far, *refs):
    grids, out = refs[: len(parts)], refs[-1]
    rows = out.shape[0] // n
    line = lax.broadcasted_iota(jnp.int32, (rows, rows), 0)
    turn = line + lax.broadcasted_iota(jnp.int32, (rows, rows), 1) == rows - 1
    turn = jnp.where(turn, 1.0, 0.0).astype(jnp.bfloat16)
    for k, s in enumerate(far):
        for a in range(n):
            down = (a ^ (n - 1)) * rows
            tile = weights_of(parts, grids, s ^ (n - 1), slice(down, down + rows))
            tile = jnp.dot(turn, tile, preferred_element_type=jnp.float32).astype(jnp.bfloat16)
            tile = -jnp.dot(tile, turn, preferred_element_type=jnp.float32)
            out[a * rows : (a + 1) * rows, k * rows : (k + 1) * rows] = tile.astype(jnp.bfloat16)


def far_first(arrays):
    half = len(arrays) // 2
    return [arrays[0], *arrays[half:], *arrays[1:half]]


def in_slots(arrays):
    half = len(arrays) // 2
    return [arrays[0], *arrays[half + 1 :], *arrays[1 : half + 1]]


def section_kernel(n, two, second, far, parts, me_ref, *refs):
    grids, refs = refs[: len(parts)], refs[len(parts) :]
    firsts, refs = in_slots(refs[:n]), refs[n:]
    if second:
        rests, refs = in_slots(refs[:n]), refs[n + 1 :]
    outs, refs = refs[: len(far)], refs[len(far) :]
    u1, r0, fy1, u0, fy0, product, turned = refs
    wide, size = u0.shape[1:]
    rows = size // n
    core = wide - 2 * HALO
    me = me_ref[0]
    right_first = me % 2 == 0
    lane = min(rows, 128)
    strips = rows // lane

    part = wide - 2 * SKIP
    lap = 2 * NEED
    for s in range(n):
        for f in range(MOMENTS):
            if not two:
                u0[f, :, pl.ds(s * rows, rows)] = decode(f, firsts[s][f].astype(jnp.float32))
                continue
            whole = decode(f, firsts[s][f].astype(jnp.float32))
            for p in range(strips):
                here = pl.ds(s * rows + p * lane, lane)
                first = whole[p * part : (p + 1) * part]
                u0[f, 0:8, here] = jnp.zeros((8, lane), jnp.float32)
                u0[f, wide - 8 :, here] = jnp.zeros((8, lane), jnp.float32)
                if not second:
                    u0[f, SKIP : SKIP + part, here] = first
                    continue
                new = rests[s][f, :, p * lane : (p + 1) * lane].astype(jnp.float32)
                new = decode(f, new)
                left = jnp.concatenate([new, first[:lap]], axis=0)
                right = jnp.concatenate([first[part - lap :], new], axis=0)
                u0[f, SKIP : SKIP + part, here] = jnp.where(right_first, left, right)

    for s in range(n):
        for p in range(strips):
            here = pl.ds(s * rows + p * lane, lane)
            u = [u0[f, :, here] for f in range(MOMENTS)]
            for f in range(MOMENTS):
                fy0[f * wide : (f + 1) * wide, here] = flux(u, 1, f).astype(jnp.bfloat16)

    middle = slice(HALO, HALO + core)
    for s in range(n):
        weights = weights_of(parts, grids, s)
        product[...] = jnp.dot(fy0[...], weights, preferred_element_type=jnp.float32)
        for p in range(strips):
            here = pl.ds(s * rows + p * lane, lane)
            there = pl.ds(p * lane, lane)
            u = [u0[f, :, here] for f in range(MOMENTS)]
            src = sources(u, walls(me, s, p, n, rows, wide))
            new = []
            for f in range(MOMENTS):
                across = product[f * wide : (f + 1) * wide, there]
                rate = -(along_of(flux(u, 0, f), turned, f)[...] + across)
                if src[f] is not None:
                    rate = rate + src[f]
                r0[f, :, here] = rate[middle]
                new.append(u[f] + time_step * rate)
                u1[f, :, here] = new[f]
            inner = [x[middle] for x in new]
            for f in range(MOMENTS):
                fy1[f * core : (f + 1) * core, here] = flux(inner, 1, f).astype(jnp.bfloat16)

    def place(s, f):
        return outs[far.index(s)].at[f]

    finish(n, far, me_ref, parts, grids, u1, r0, fy1, place, product, turned)


THIRDS = ((0, 5), (5, 9), (9, MOMENTS))


def finish_kernel(n, near, parts, chunks, me_ref, *refs):
    grids, refs = refs[: len(parts)], refs[len(parts) :]
    states, product, turned = refs[: 3 * chunks], *refs[-2:]
    outs = refs[-2 - 1 - len(THIRDS) * (len(near) - 1) : -2]
    core = outs[0].shape[1] // chunks

    def place(c, s, f):
        span = slice(c * core, (c + 1) * core)
        if s == 0:
            return outs[0].at[f, span]
        third = [first <= f < end for first, end in THIRDS].index(True)
        return outs[1 + len(THIRDS) * (s - 1) + third].at[f - THIRDS[third][0], span]

    for c in range(chunks):
        part = functools.partial(place, c)
        finish(n, near, me_ref, parts, grids, *states[3 * c : 3 * c + 3], part, product, turned)


def walls(me, s, p, n, rows, count):
    lane = min(rows, 128)
    line = jnp.bitwise_xor(me, s) * rows + p * lane
    line = line + lax.broadcasted_iota(jnp.int32, (count, lane), 1)
    return jnp.where(line == 0, 1.0, jnp.where(line == n * rows - 1, -1.0, 0.0))


def finish(n, slots, me_ref, parts, grids, u1, r0, fy1, outs, product, turned):
    wide, size = u1.shape[1:]
    rows = size // n
    core = wide - 2 * HALO
    lane = min(rows, 128)
    me = me_ref[0]
    middle = slice(HALO, HALO + core)
    for k, s in enumerate(slots):
        weights = weights_of(parts, grids, s)
        product[0 : MOMENTS * core, :] = jnp.dot(
            fy1[...], weights, preferred_element_type=jnp.float32
        )
        for p in range(rows // lane):
            here = pl.ds(s * rows + p * lane, lane)
            there = pl.ds(p * lane, lane)
            u = [u1[f, :, here] for f in range(MOMENTS)]
            inner = [x[middle] for x in u]
            src = sources(inner, walls(me, s, p, n, rows, core))
            for f in range(MOMENTS):
                across = product[f * core : (f + 1) * core, there]
                rate = -(along_of(flux(u, 0, f), turned, f)[middle, :] + across)
                if src[f] is not None:
                    rate = rate + src[f]
                rate = 0.5 * (r0[f, :, here] + rate)
                target = outs(s, f)
                target[:, there] = rate.astype(target.dtype)


def arrived_kernel(*refs):
    refs[-1][...] = jnp.zeros_like(refs[-1])


def unpack_kernel(n, slots, chunks, pieces, token, me_ref, *refs):
    out, tall, held, leaving = *refs[-4 - len(token) : -3 - len(token)], *refs[-3:]
    for ref in refs[-3 - len(token) : -3]:
        ref[...] = jnp.zeros_like(ref)
    rows, cols = held.shape[1:]
    slab = cols // len(slots)
    width = slab // chunks
    me = me_ref[0]
    copies = []
    for f in range(MOMENTS):
        for array, (s, c, first, end) in zip(refs, pieces):
            if not first <= f < end:
                continue
            of = jnp.bitwise_xor(me, s)
            for k in range(chunks) if c is None else (c,):
                start = of % len(slots) * slab
                if chunks == 2:
                    start += jnp.where(of % 2 == 0, width * (1 - k), width * k)
                here = pl.ds(pl.multiple_of(start, 16), width)
                piece = array[f - first, k * width : (k + 1) * width] if c is None else array[f]
                tall[f, here, :] = piece.astype(jnp.float32)
        held[f] = tall[f].T
        side = jnp.bitwise_xor(me, slots[0]) // len(slots) * cols
        there = out.at[f, :, pl.ds(pl.multiple_of(side, 128), cols)]
        copies.append(pltpu.make_async_copy(held.at[f], there, leaving.at[f]))
        copies[f].start()
    for copy in copies:
        copy.wait()


def to_partner(array, n, s):
    return array if s == 0 else lax.ppermute(array, "gy", [(i, i ^ s) for i in range(n)])


def exchange(arrays, n, slots):
    pairs = list(zip(arrays, slots))[::-1]
    return [to_partner(array, n, s) for array, s in pairs][::-1]


def on_device(rho, vel, temp, stress, heat):
    rows, cols = rho.shape
    n = lax.axis_size("gy")
    ring = lax.axis_size("gx")
    size, slab = n * rows, cols // n
    two = slab % 32 == 0
    core = slab // 2 if two else slab
    wide = core + 2 * HALO
    lane = min(rows, 128)
    half = jnp.bfloat16
    me = lax.axis_index("gy").astype(jnp.int32).reshape(1)
    vel, stress, heat = (jnp.swapaxes(a, 0, 1) for a in (vel, stress, heat))

    def message(width, kind=half):
        return jax.ShapeDtypeStruct((MOMENTS, width, rows), kind)

    far, near = (tuple(range(n // 2, n)), tuple(range(n // 2)))
    inputs = (rho, vel, temp, stress, heat)

    def pack(arrays):
        sent = (MOMENTS, (wide - 2 * SKIP) * (rows // lane), lane)
        shapes = [jax.ShapeDtypeStruct(sent, half)] * n if two else []
        shapes += [message(cols + 2 * HALO)]
        return pl.pallas_call(
            functools.partial(pack_kernel, n, two),
            out_shape=shapes,
            in_specs=[SMEM] + [HBM] * len(arrays),
            out_specs=[ANY] * len(shapes),
            scratch_shapes=[
                pltpu.VMEM((MOMENTS, cols + 2 * HALO, rows), jnp.float32),
                pltpu.VMEM((MOMENTS, rows, cols), jnp.float32),
                pltpu.SemaphoreType.DMA((len(GROUPS),)),
            ]
            + [pltpu.VMEM(x.shape, x.dtype) for x in shapes]
            + [pltpu.SemaphoreType.DMA((len(shapes), len(GROUPS)))],
            compiler_params=params(56),
            cost_estimate=cost(2),
            name="pack",
        )(me, *arrays)

    firsts = []
    if two:
        *firsts, tall = pack(inputs)
        firsts = exchange(firsts, n, range(n))
    else:
        (tall,) = pack(inputs)

    def grid_of(slots, *ties):
        return pl.pallas_call(
            functools.partial(grid_kernel, n, rows, slots),
            out_shape=jax.ShapeDtypeStruct((size, len(slots) * rows), half),
            in_specs=[SMEM] + [ANY] * len(ties),
            out_specs=VMEM,
            scratch_shapes=[pltpu.VMEM((size, lane), jnp.float32)] * 4
            + [pltpu.VMEM((8, lane), jnp.float32)],
            compiler_params=params(24),
            cost_estimate=cost(1),
            name="grid",
        )(me, *ties)

    parts = (near[: n // 4], near[n // 4 :])
    grids = [grid_of(part) for part in parts]
    left, right = pl.pallas_call(
        edge_kernel,
        out_shape=[message(2 * HALO)] * 2,
        in_specs=[VMEM, ANY],
        out_specs=[VMEM] * 2,
        compiler_params=params(24),
        cost_estimate=cost(0.2),
        name="edges",
    )(tall, grids[0])
    up = [(i, (i + 1) % ring) for i in range(ring)]
    before = lax.ppermute(right, "gx", up)
    after = lax.ppermute(left, "gx", [(j, i) for i, j in up])
    turned = pl.pallas_call(
        functools.partial(flip_kernel, n, parts, far),
        out_shape=jax.ShapeDtypeStruct((size, len(far) * rows), half),
        in_specs=[VMEM] * 2,
        out_specs=VMEM,
        compiler_params=params(24),
        cost_estimate=cost(0.3),
        name="flip",
    )(*grids)
    all_parts, all_grids = (*parts, far), (*grids, turned)
    rests = pl.pallas_call(
        functools.partial(rest_kernel, n, two),
        out_shape=[message(core if two else wide)] * n,
        in_specs=[SMEM] + [VMEM] * 3,
        out_specs=[VMEM] * n,
        compiler_params=params(),
        cost_estimate=cost(0.2),
        name="rest",
    )(me, tall, before, after)
    rests = exchange(rests, n, range(n))

    def sections(second, *arrays):
        state = [
            jax.ShapeDtypeStruct((MOMENTS, wide, size), jnp.float32),
            jax.ShapeDtypeStruct((MOMENTS, core, size), jnp.float32),
            jax.ShapeDtypeStruct((MOMENTS * core, size), half),
        ]
        *crossing, u1, r0, fy1 = pl.pallas_call(
            functools.partial(section_kernel, n, two, second, far, all_parts),
            out_shape=[message(core)] * len(far) + state,
            in_specs=[SMEM] + [VMEM] * (len(arrays) + 3 - second) + [ANY] * second,
            out_specs=[VMEM] * (len(far) + 3),
            scratch_shapes=[
                pltpu.VMEM((MOMENTS, wide, size), jnp.float32),
                pltpu.VMEM((MOMENTS * wide, size), half),
                pltpu.VMEM((MOMENTS * wide, rows), jnp.float32),
                pltpu.VMEM((2 * MOMENTS, wide, lane), jnp.float32),
            ],
            compiler_params=params(24),
            cost_estimate=cost(6),
            name="sections",
        )(me, *all_grids, *arrays)
        return crossing, [u1, r0, fy1]

    def finished(states, *ties):
        thirds = [jax.ShapeDtypeStruct((end - first, slab, rows), half) for first, end in THIRDS]
        shapes = [message(slab, jnp.float32)] + thirds * (len(near) - 1)
        own, *others = pl.pallas_call(
            functools.partial(finish_kernel, n, near, parts, len(states) // 3),
            out_shape=shapes,
            in_specs=[SMEM] + [VMEM] * (len(states) + 2) + [ANY] * len(ties),
            out_specs=[VMEM] * len(shapes),
            scratch_shapes=[
                pltpu.VMEM((MOMENTS * core, rows), jnp.float32),
                pltpu.VMEM((2 * MOMENTS, wide, lane), jnp.float32),
            ],
            compiler_params=params(24),
            cost_estimate=cost(4),
            name="finish",
        )(me, *grids, *states, *ties)
        slots = [s for s in near[1:] for _ in THIRDS]
        return [own, *exchange(others, n, slots)]

    if two:
        firsts, rests = far_first(firsts), far_first(rests)
        crossing, states = sections(False, *firsts)
        back = exchange(crossing, n, far)
        crossing, more = sections(True, *firsts, *rests, crossing[0])
        staying = finished(states + more, *back)
        back += exchange(crossing, n, far)
    else:
        crossing, states = sections(False, *far_first(rests))
        staying = finished(states)
        back = exchange(crossing, n, far)
    chunks = 2 if two else 1
    token = jax.ShapeDtypeStruct((8, 128), jnp.float32)

    def unpack(slots, arrays, pieces, *before):
        alias = {1 + len(arrays): 0} if before else {}
        tokens = [] if before else [token]
        return pl.pallas_call(
            functools.partial(unpack_kernel, n, slots, chunks, pieces, tokens),
            out_shape=[jax.ShapeDtypeStruct((MOMENTS, rows, cols), jnp.float32), *tokens],
            in_specs=[SMEM] + [VMEM] * len(arrays) + [ANY] * len(before),
            out_specs=[ANY] + [VMEM] * len(tokens),
            scratch_shapes=[
                pltpu.VMEM((MOMENTS, cols // 2, rows), jnp.float32),
                pltpu.VMEM((MOMENTS, rows, cols // 2), jnp.float32),
                pltpu.SemaphoreType.DMA((MOMENTS,)),
            ],
            input_output_aliases=alias,
            compiler_params=params(24),
            cost_estimate=cost(0.01),
            name="unpack",
        )(me, *arrays, *before)

    pieces = [(0, None, 0, MOMENTS)] + [(s, None, *span) for s in near[1:] for span in THIRDS]
    out, turned_near = unpack(near, staying, tuple(pieces))
    arrived = pl.pallas_call(
        arrived_kernel,
        out_shape=token,
        in_specs=[ANY] * (len(back) + 1),
        out_specs=VMEM,
        compiler_params=params(1),
        cost_estimate=cost(6),
        name="arrived",
    )(*back, turned_near)
    pieces = [(s, c, 0, MOMENTS) for c in range(chunks) for s in far]
    (out,) = unpack(far, back, tuple(pieces), out, arrived)
    return jnp.swapaxes(out, 0, 1)


def solution(mesh):
    return jax.shard_map(
        on_device,
        mesh=mesh,
        in_specs=(
            P("gy", "gx"),
            P("gy", None, "gx"),
            P("gy", "gx"),
            P("gy", None, "gx"),
            P("gy", None, "gx"),
        ),
        out_specs=P("gy", None, "gx"),
        check_vma=False,
    )
```

```python
import functools
import math

import jax
import jax.numpy as jnp
from jax import lax
from jax.experimental import pallas as pl
from jax.experimental.pallas import tpu as pltpu
from jax.sharding import PartitionSpec as P

time_step = 0.05
enforcement_weight = 4.0
plate_speed = 0.5
dissipation_speed = 0.25
coeffs = (0.75, -0.15, 1.0 / 60.0)

MOMENTS = 13
HALO = 8
NEED = 6
SKIP = HALO - NEED
RHO, TEMP = 0, 4
VMEM = pl.BlockSpec(memory_space=pltpu.VMEM)
ANY = pl.BlockSpec(memory_space=pl.ANY)
HBM = pl.BlockSpec(memory_space=pltpu.HBM)
SMEM = pl.BlockSpec(memory_space=pltpu.SMEM)


def cost(micros):
    return pl.CostEstimate(
        flops=int(micros * 1e9), bytes_accessed=int(micros * 3e6), transcendentals=0
    )


def params(mib=48):
    return pltpu.CompilerParams(vmem_limit_bytes=mib * 2**20)


def code(f, x):
    if f == RHO:
        return x - 1.25
    if f == TEMP:
        return jnp.exp2(160.0 * (x - 1.25))
    return x


def decode(f, y):
    if f == RHO:
        return y + 1.25
    if f == TEMP:
        return jnp.log2(y) * (1.0 / 160.0) + 1.25
    return y


def flux(u, d, f):
    v = u[1 + d]
    temperature = u[4]
    heat = u[10:13]
    s = [[u[5], u[6], u[8]], [u[6], u[7], u[9]], [u[8], u[9], None]]
    if f == 0:
        return u[0] * v
    if f < 4:
        i = f - 1
        out = u[1 + i] * v + s[i][d]
        return out + temperature if i == d else out
    if f == 4:
        return v * temperature + 2.0 / 3.0 * heat[d]
    if f < 10:
        i, j = ((0, 0), (0, 1), (1, 1), (0, 2), (1, 2))[f - 5]
        out = v * s[i][j]
        weight = {}
        if j == d:
            weight[i] = weight.get(i, 0.0) + 0.4
        if i == d:
            weight[j] = weight.get(j, 0.0) + 0.4
        if i == j:
            weight[d] = weight.get(d, 0.0) - 4.0 / 15.0
        for k, w in weight.items():
            out = out + w * heat[k]
        return out
    i = f - 10
    out = v * heat[i] + temperature * s[i][d]
    return out + 2.5 * temperature * temperature if i == d else out


def sources(u, wall):
    near = jnp.abs(wall)
    nu = u[0] * jnp.sqrt(u[4] * u[4] + 0.25)
    heavy, light = -0.8 * nu, -0.55 * nu
    out = [None] * MOMENTS
    out[1] = -enforcement_weight * near * (u[1] - plate_speed * wall)
    out[4] = -dissipation_speed * nu * u[4] - enforcement_weight * near * (u[4] - 1.0)
    for f in range(5, 10):
        out[f] = heavy * u[f]
    for f in range(10, 13):
        out[f] = light * u[f]
    return out


def along_of(fx, turned, f):
    count = fx.shape[0] // 8
    turned[f] = fx
    x = [turned[f, pl.ds(v, 8, stride=count), :] for v in range(count)]
    x = [pltpu.roll(y, 1, 0) for y in x[-3:]] + x + [pltpu.roll(y, 7, 0) for y in x[:3]]
    for v in range(count):
        total = None
        for k in range(3):
            term = coeffs[k] * (x[3 + v + k + 1] - x[3 + v - k - 1])
            total = term if total is None else total + term
        turned[MOMENTS + f, pl.ds(v, 8, stride=count), :] = total
    return turned.at[MOMENTS + f]


def message_start(me, s, slab):
    to = jnp.bitwise_xor(me, s)
    return pl.multiple_of(to * slab + jnp.where(to % 2 == 0, slab // 2, 0), 16)


GROUPS = ((0, 1), (1, 4), (4, 5), (5, 8), (8, 10), (10, 12), (12, 13))


def pack_kernel(n, two, me_ref, *refs):
    (rho, vel, temp, stress, heat), refs = refs[:5], refs[5:]
    inputs = (rho, vel, temp, stress.at[0:3], stress.at[3:5], heat.at[0:2], heat.at[2:3])
    count = n if two else 0
    outs, (strip, given, arrived), refs = refs[: count + 1], refs[count + 1 : count + 4], refs[count + 4 :]
    held, left_at = refs[:-1], refs[-1]
    rows, cols = given.shape[1:]
    slab = cols // n
    me = me_ref[0]
    copies = []
    for k, (first, end) in enumerate(GROUPS):
        dst = given.at[first] if len(inputs[k].shape) == 2 else given.at[first:end]
        copies.append(pltpu.make_async_copy(inputs[k], dst, arrived.at[k]))
        copies[k].start()
    wide = slab // 2 + 2 * HALO
    lane = min(rows, 128)
    strip[0:HALO, :] = jnp.zeros((HALO, rows), jnp.float32)
    strip[HALO + cols :, :] = jnp.zeros((HALO, rows), jnp.float32)
    leaving = []
    done = 0
    for at, (first, end) in enumerate(GROUPS):
        copies[at].wait()
        for f in range(first, end):
            strip[HALO : HALO + cols, :] = code(f, given[f]).T
            for s in range(count):
                block = strip[pl.ds(message_start(me, s, slab), wide), :][SKIP : wide - SKIP]
                halves = [block[:, p : p + lane] for p in range(0, rows, lane)]
                held[s][f] = jnp.concatenate(halves, axis=0).astype(jnp.bfloat16)
            held[count][f] = strip[...].astype(jnp.bfloat16)
        if at > 0:
            span = pl.ds(done, end - done)
            for k, out in enumerate(outs):
                copy = pltpu.make_async_copy(held[k].at[span], out.at[span], left_at.at[k, at - 1])
                copy.start()
                leaving.append(copy)
            done = end
    for copy in leaving:
        copy.wait()


def edge_kernel(tall, tie, left, right):
    cols = tall.shape[1] - 2 * HALO
    left[...] = tall[:, 0 : 2 * HALO, :]
    right[...] = tall[:, cols : cols + 2 * HALO, :]


def rest_kernel(n, two, me_ref, tall, before, after, *outs):
    me = me_ref[0]
    slab = (tall.shape[1] - 2 * HALO) // n
    count = outs[0].shape[1]
    wide = slab // 2 + 2 * HALO if two else count
    line = lax.broadcasted_iota(jnp.int32, before.shape[1:], 0)
    for s in range(n):
        to = jnp.bitwise_xor(me, s)
        even = to % 2 == 0
        start = to * slab
        if two:
            start += jnp.where(even, 0, slab // 2)
        start = pl.multiple_of(start, 16)
        for f in range(MOMENTS):
            block = tall[f, pl.ds(start, wide), :].astype(jnp.float32)
            first, last = block[: 2 * HALO], block[wide - 2 * HALO :]
            first = jnp.where((line < HALO) & (to == 0), before[f].astype(jnp.float32), first)
            last = jnp.where((line >= HALO) & (to == n - 1), after[f].astype(jnp.float32), last)
            between = [block[2 * HALO : wide - 2 * HALO]] if wide > 4 * HALO else []
            block = jnp.concatenate([first, *between, last], axis=0)
            if two:
                near_end = block[SKIP : SKIP + count]
                far_end = block[wide - SKIP - count : wide - SKIP]
                block = jnp.where(even, near_end, far_end)
            outs[s][f] = block.astype(jnp.bfloat16)


def grid_kernel(n, rows, slots, me_ref, *refs):
    out, sin_col, cos_col, back_col, line_col, total = refs[-6:]
    size = n * rows
    last = size - 1
    half = math.pi / (2.0 * last)
    me = me_ref[0]
    step = 64
    lane = min(rows, 128)

    def table(s):
        line = jnp.bitwise_xor(me, s) * rows + lax.broadcasted_iota(jnp.int32, (8, rows), 1)
        angle = half * line.astype(jnp.float32)
        edge = (line == 0) | (line == last)
        sign = (1 - 2 * (line & 1)).astype(jnp.float32)
        return line.astype(jnp.float32), jnp.sin(angle), jnp.cos(angle), edge, sign

    def column(x):
        return jnp.broadcast_to(x[0:1], (lane, rows)).T

    for s in range(n):
        line, sine, cosine, edge, sign = table(s)
        here = pl.ds(s * rows, rows)
        line_col[here, :] = column(line)
        sin_col[here, :] = column(sine)
        cos_col[here, :] = column(cosine)
        back_col[here, :] = column(jnp.where(edge, 0.5 * sign, sign))

    for index, s in enumerate(slots):
        line, sine, cosine, edge, sign = table(s)
        front = (-math.pi / last) * sine * cosine * jnp.where(edge, 2.0 * sign, sign)
        for p in range(rows // lane):
            here = pl.ds(index * rows + p * lane, lane)
            own = pl.ds(s * rows + p * lane, lane)
            line_i, sin_i, cos_i, front_i = (
                x[0:1, p * lane : (p + 1) * lane] for x in (line, sine, cosine, front)
            )
            total[...] = jnp.zeros_like(total)

            def block(t, carry):
                down = pl.ds(pl.multiple_of(t * step, step), step)
                gap = line_i - line_col[down, :]
                same = gap == 0.0
                x = half * gap
                x2 = x * x
                poly = -1.0 / 39916800.0
                for c in (1 / 362880.0, -1 / 5040.0, 1 / 120.0, -1 / 6.0, 1.0):
                    poly = poly * x2 + c
                plus = sin_i * cos_col[down, :] + cos_i * sin_col[down, :]
                denom = jnp.where(same, 1.0, plus * (x * poly))
                off = jnp.where(same, 0.0, front_i * back_col[down, :] / denom)
                total[...] += jnp.sum(off.reshape(step // 8, 8, lane), axis=0)
                out[down, here] = off.astype(jnp.bfloat16)
                return carry

            lax.fori_loop(0, size // step, block, 0)
            diagonal = -jnp.sum(total[...], axis=0, keepdims=True)
            same = lax.broadcasted_iota(jnp.int32, (lane, lane), 0) == (
                lax.broadcasted_iota(jnp.int32, (lane, lane), 1)
            )
            tile = out[own, here].astype(jnp.float32)
            out[own, here] = jnp.where(same, diagonal, tile).astype(jnp.bfloat16)


def weights_of(parts, grids, s, down=slice(None)):
    for part, grid in zip(parts, grids):
        if s in part:
            rows = grid.shape[1] // len(part)
            at = part.index(s) * rows
            return grid[down, at : at + rows]


def flip_kernel(n, parts, far, *refs):
    grids, out = refs[: len(parts)], refs[-1]
    rows = out.shape[0] // n
    line = lax.broadcasted_iota(jnp.int32, (rows, rows), 0)
    turn = line + lax.broadcasted_iota(jnp.int32, (rows, rows), 1) == rows - 1
    turn = jnp.where(turn, 1.0, 0.0).astype(jnp.bfloat16)
    for k, s in enumerate(far):
        for a in range(n):
            down = (a ^ (n - 1)) * rows
            tile = weights_of(parts, grids, s ^ (n - 1), slice(down, down + rows))
            tile = jnp.dot(turn, tile, preferred_element_type=jnp.float32).astype(jnp.bfloat16)
            tile = -jnp.dot(tile, turn, preferred_element_type=jnp.float32)
            out[a * rows : (a + 1) * rows, k * rows : (k + 1) * rows] = tile.astype(jnp.bfloat16)


def far_first(arrays):
    half = len(arrays) // 2
    return [arrays[0], *arrays[half:], *arrays[1:half]]


def in_slots(arrays):
    half = len(arrays) // 2
    return [arrays[0], *arrays[half + 1 :], *arrays[1 : half + 1]]


def section_kernel(n, two, second, far, parts, me_ref, *refs):
    grids, refs = refs[: len(parts)], refs[len(parts) :]
    firsts, refs = in_slots(refs[:n]), refs[n:]
    if second:
        rests, refs = in_slots(refs[:n]), refs[n + 1 :]
    outs, refs = refs[: len(far)], refs[len(far) :]
    u1, r0, fy1, u0, fy0, product, turned = refs
    wide, size = u0.shape[1:]
    rows = size // n
    core = wide - 2 * HALO
    me = me_ref[0]
    right_first = me % 2 == 0
    lane = min(rows, 128)
    strips = rows // lane

    part = wide - 2 * SKIP
    lap = 2 * NEED
    for s in range(n):
        for f in range(MOMENTS):
            if not two:
                u0[f, :, pl.ds(s * rows, rows)] = decode(f, firsts[s][f].astype(jnp.float32))
                continue
            whole = decode(f, firsts[s][f].astype(jnp.float32))
            for p in range(strips):
                here = pl.ds(s * rows + p * lane, lane)
                first = whole[p * part : (p + 1) * part]
                u0[f, 0:8, here] = jnp.zeros((8, lane), jnp.float32)
                u0[f, wide - 8 :, here] = jnp.zeros((8, lane), jnp.float32)
                if not second:
                    u0[f, SKIP : SKIP + part, here] = first
                    continue
                new = rests[s][f, :, p * lane : (p + 1) * lane].astype(jnp.float32)
                new = decode(f, new)
                left = jnp.concatenate([new, first[:lap]], axis=0)
                right = jnp.concatenate([first[part - lap :], new], axis=0)
                u0[f, SKIP : SKIP + part, here] = jnp.where(right_first, left, right)

    for s in range(n):
        for p in range(strips):
            here = pl.ds(s * rows + p * lane, lane)
            u = [u0[f, :, here] for f in range(MOMENTS)]
            for f in range(MOMENTS):
                fy0[f * wide : (f + 1) * wide, here] = flux(u, 1, f).astype(jnp.bfloat16)

    middle = slice(HALO, HALO + core)
    for s in range(n):
        weights = weights_of(parts, grids, s)
        product[...] = jnp.dot(fy0[...], weights, preferred_element_type=jnp.float32)
        for p in range(strips):
            here = pl.ds(s * rows + p * lane, lane)
            there = pl.ds(p * lane, lane)
            u = [u0[f, :, here] for f in range(MOMENTS)]
            src = sources(u, walls(me, s, p, n, rows, wide))
            new = []
            for f in range(MOMENTS):
                across = product[f * wide : (f + 1) * wide, there]
                rate = -(along_of(flux(u, 0, f), turned, f)[...] + across)
                if src[f] is not None:
                    rate = rate + src[f]
                r0[f, :, here] = rate[middle]
                new.append(u[f] + time_step * rate)
                u1[f, :, here] = new[f]
            inner = [x[middle] for x in new]
            for f in range(MOMENTS):
                fy1[f * core : (f + 1) * core, here] = flux(inner, 1, f).astype(jnp.bfloat16)

    def place(s, f):
        return outs[far.index(s)].at[f]

    finish(n, far, me_ref, parts, grids, u1, r0, fy1, place, product, turned)


THIRDS = ((0, 5), (5, 9), (9, MOMENTS))


def finish_kernel(n, near, parts, chunks, me_ref, *refs):
    grids, refs = refs[: len(parts)], refs[len(parts) :]
    states, product, turned = refs[: 3 * chunks], *refs[-2:]
    outs = refs[-2 - 1 - len(THIRDS) * (len(near) - 1) : -2]
    core = outs[0].shape[1] // chunks

    def place(c, s, f):
        span = slice(c * core, (c + 1) * core)
        if s == 0:
            return outs[0].at[f, span]
        third = [first <= f < end for first, end in THIRDS].index(True)
        return outs[1 + len(THIRDS) * (s - 1) + third].at[f - THIRDS[third][0], span]

    for c in range(chunks):
        part = functools.partial(place, c)
        finish(n, near, me_ref, parts, grids, *states[3 * c : 3 * c + 3], part, product, turned)


def walls(me, s, p, n, rows, count):
    lane = min(rows, 128)
    line = jnp.bitwise_xor(me, s) * rows + p * lane
    line = line + lax.broadcasted_iota(jnp.int32, (count, lane), 1)
    return jnp.where(line == 0, 1.0, jnp.where(line == n * rows - 1, -1.0, 0.0))


def finish(n, slots, me_ref, parts, grids, u1, r0, fy1, outs, product, turned):
    wide, size = u1.shape[1:]
    rows = size // n
    core = wide - 2 * HALO
    lane = min(rows, 128)
    me = me_ref[0]
    middle = slice(HALO, HALO + core)
    for k, s in enumerate(slots):
        weights = weights_of(parts, grids, s)
        product[0 : MOMENTS * core, :] = jnp.dot(
            fy1[...], weights, preferred_element_type=jnp.float32
        )
        for p in range(rows // lane):
            here = pl.ds(s * rows + p * lane, lane)
            there = pl.ds(p * lane, lane)
            u = [u1[f, :, here] for f in range(MOMENTS)]
            inner = [x[middle] for x in u]
            src = sources(inner, walls(me, s, p, n, rows, core))
            for f in range(MOMENTS):
                across = product[f * core : (f + 1) * core, there]
                rate = -(along_of(flux(u, 0, f), turned, f)[middle, :] + across)
                if src[f] is not None:
                    rate = rate + src[f]
                rate = 0.5 * (r0[f, :, here] + rate)
                target = outs(s, f)
                target[:, there] = rate.astype(target.dtype)


def arrived_kernel(*refs):
    refs[-1][...] = jnp.zeros_like(refs[-1])


def unpack_kernel(n, slots, chunks, pieces, token, me_ref, *refs):
    out, tall, held, leaving = *refs[-4 - len(token) : -3 - len(token)], *refs[-3:]
    for ref in refs[-3 - len(token) : -3]:
        ref[...] = jnp.zeros_like(ref)
    rows, cols = held.shape[1:]
    slab = cols // len(slots)
    width = slab // chunks
    me = me_ref[0]
    copies = []
    for f in range(MOMENTS):
        for array, (s, c, first, end) in zip(refs, pieces):
            if not first <= f < end:
                continue
            of = jnp.bitwise_xor(me, s)
            for k in range(chunks) if c is None else (c,):
                start = of % len(slots) * slab
                if chunks == 2:
                    start += jnp.where(of % 2 == 0, width * (1 - k), width * k)
                here = pl.ds(pl.multiple_of(start, 16), width)
                piece = array[f - first, k * width : (k + 1) * width] if c is None else array[f]
                tall[f, here, :] = piece.astype(jnp.float32)
        held[f] = tall[f].T
        side = jnp.bitwise_xor(me, slots[0]) // len(slots) * cols
        there = out.at[f, :, pl.ds(pl.multiple_of(side, 128), cols)]
        copies.append(pltpu.make_async_copy(held.at[f], there, leaving.at[f]))
        copies[f].start()
    for copy in copies:
        copy.wait()


def to_partner(array, n, s):
    return array if s == 0 else lax.ppermute(array, "gy", [(i, i ^ s) for i in range(n)])


def exchange(arrays, n, slots):
    pairs = list(zip(arrays, slots))[::-1]
    return [to_partner(array, n, s) for array, s in pairs][::-1]


def on_device(rho, vel, temp, stress, heat):
    rows, cols = rho.shape
    n = lax.axis_size("gy")
    ring = lax.axis_size("gx")
    size, slab = n * rows, cols // n
    two = slab % 32 == 0
    core = slab // 2 if two else slab
    wide = core + 2 * HALO
    lane = min(rows, 128)
    half = jnp.bfloat16
    me = lax.axis_index("gy").astype(jnp.int32).reshape(1)
    vel, stress, heat = (jnp.swapaxes(a, 0, 1) for a in (vel, stress, heat))

    def message(width, kind=half):
        return jax.ShapeDtypeStruct((MOMENTS, width, rows), kind)

    far, near = (tuple(range(n // 2, n)), tuple(range(n // 2)))
    inputs = (rho, vel, temp, stress, heat)

    def pack(arrays):
        sent = (MOMENTS, (wide - 2 * SKIP) * (rows // lane), lane)
        shapes = [jax.ShapeDtypeStruct(sent, half)] * n if two else []
        shapes += [message(cols + 2 * HALO)]
        return pl.pallas_call(
            functools.partial(pack_kernel, n, two),
            out_shape=shapes,
            in_specs=[SMEM] + [HBM] * len(arrays),
            out_specs=[ANY] * len(shapes),
            scratch_shapes=[
                pltpu.VMEM((cols + 2 * HALO, rows), jnp.float32),
                pltpu.VMEM((MOMENTS, rows, cols), jnp.float32),
                pltpu.SemaphoreType.DMA((len(GROUPS),)),
            ]
            + [pltpu.VMEM(x.shape, x.dtype) for x in shapes]
            + [pltpu.SemaphoreType.DMA((len(shapes), len(GROUPS)))],
            compiler_params=params(56),
            cost_estimate=cost(2),
            name="pack",
        )(me, *arrays)

    firsts = []
    if two:
        *firsts, tall = pack(inputs)
        firsts = exchange(firsts, n, range(n))
    else:
        (tall,) = pack(inputs)

    def grid_of(slots, *ties):
        return pl.pallas_call(
            functools.partial(grid_kernel, n, rows, slots),
            out_shape=jax.ShapeDtypeStruct((size, len(slots) * rows), half),
            in_specs=[SMEM] + [ANY] * len(ties),
            out_specs=VMEM,
            scratch_shapes=[pltpu.VMEM((size, lane), jnp.float32)] * 4
            + [pltpu.VMEM((8, lane), jnp.float32)],
            compiler_params=params(24),
            cost_estimate=cost(1),
            name="grid",
        )(me, *ties)

    parts = (near[: n // 4], near[n // 4 :])
    grids = [grid_of(part) for part in parts]
    left, right = pl.pallas_call(
        edge_kernel,
        out_shape=[message(2 * HALO)] * 2,
        in_specs=[VMEM, ANY],
        out_specs=[VMEM] * 2,
        compiler_params=params(24),
        cost_estimate=cost(0.2),
        name="edges",
    )(tall, grids[0])
    up = [(i, (i + 1) % ring) for i in range(ring)]
    before = lax.ppermute(right, "gx", up)
    after = lax.ppermute(left, "gx", [(j, i) for i, j in up])
    turned = pl.pallas_call(
        functools.partial(flip_kernel, n, parts, far),
        out_shape=jax.ShapeDtypeStruct((size, len(far) * rows), half),
        in_specs=[VMEM] * 2,
        out_specs=VMEM,
        compiler_params=params(24),
        cost_estimate=cost(0.3),
        name="flip",
    )(*grids)
    all_parts, all_grids = (*parts, far), (*grids, turned)
    rests = pl.pallas_call(
        functools.partial(rest_kernel, n, two),
        out_shape=[message(core if two else wide)] * n,
        in_specs=[SMEM] + [VMEM] * 3,
        out_specs=[VMEM] * n,
        compiler_params=params(),
        cost_estimate=cost(0.2),
        name="rest",
    )(me, tall, before, after)
    rests = exchange(rests, n, range(n))

    def sections(second, *arrays):
        state = [
            jax.ShapeDtypeStruct((MOMENTS, wide, size), jnp.float32),
            jax.ShapeDtypeStruct((MOMENTS, core, size), jnp.float32),
            jax.ShapeDtypeStruct((MOMENTS * core, size), half),
        ]
        *crossing, u1, r0, fy1 = pl.pallas_call(
            functools.partial(section_kernel, n, two, second, far, all_parts),
            out_shape=[message(core)] * len(far) + state,
            in_specs=[SMEM] + [VMEM] * (len(arrays) + 3 - second) + [ANY] * second,
            out_specs=[VMEM] * (len(far) + 3),
            scratch_shapes=[
                pltpu.VMEM((MOMENTS, wide, size), jnp.float32),
                pltpu.VMEM((MOMENTS * wide, size), half),
                pltpu.VMEM((MOMENTS * wide, rows), jnp.float32),
                pltpu.VMEM((2 * MOMENTS, wide, lane), jnp.float32),
            ],
            compiler_params=params(24),
            cost_estimate=cost(6),
            name="sections",
        )(me, *all_grids, *arrays)
        return crossing, [u1, r0, fy1]

    def finished(states, *ties):
        thirds = [jax.ShapeDtypeStruct((end - first, slab, rows), half) for first, end in THIRDS]
        shapes = [message(slab, jnp.float32)] + thirds * (len(near) - 1)
        own, *others = pl.pallas_call(
            functools.partial(finish_kernel, n, near, parts, len(states) // 3),
            out_shape=shapes,
            in_specs=[SMEM] + [VMEM] * (len(states) + 2) + [ANY] * len(ties),
            out_specs=[VMEM] * len(shapes),
            scratch_shapes=[
                pltpu.VMEM((MOMENTS * core, rows), jnp.float32),
                pltpu.VMEM((2 * MOMENTS, wide, lane), jnp.float32),
            ],
            compiler_params=params(24),
            cost_estimate=cost(4),
            name="finish",
        )(me, *grids, *states, *ties)
        slots = [s for s in near[1:] for _ in THIRDS]
        return [own, *exchange(others, n, slots)]

    if two:
        firsts, rests = far_first(firsts), far_first(rests)
        crossing, states = sections(False, *firsts)
        back = exchange(crossing, n, far)
        crossing, more = sections(True, *firsts, *rests, crossing[0])
        staying = finished(states + more, *back)
        back += exchange(crossing, n, far)
    else:
        crossing, states = sections(False, *far_first(rests))
        staying = finished(states)
        back = exchange(crossing, n, far)
    chunks = 2 if two else 1
    token = jax.ShapeDtypeStruct((8, 128), jnp.float32)

    def unpack(slots, arrays, pieces, *before):
        alias = {1 + len(arrays): 0} if before else {}
        tokens = [] if before else [token]
        return pl.pallas_call(
            functools.partial(unpack_kernel, n, slots, chunks, pieces, tokens),
            out_shape=[jax.ShapeDtypeStruct((MOMENTS, rows, cols), jnp.float32), *tokens],
            in_specs=[SMEM] + [VMEM] * len(arrays) + [ANY] * len(before),
            out_specs=[ANY] + [VMEM] * len(tokens),
            scratch_shapes=[
                pltpu.VMEM((MOMENTS, cols // 2, rows), jnp.float32),
                pltpu.VMEM((MOMENTS, rows, cols // 2), jnp.float32),
                pltpu.SemaphoreType.DMA((MOMENTS,)),
            ],
            input_output_aliases=alias,
            compiler_params=params(24),
            cost_estimate=cost(0.01),
            name="unpack",
        )(me, *arrays, *before)

    pieces = [(0, None, 0, MOMENTS)] + [(s, None, *span) for s in near[1:] for span in THIRDS]
    out, turned_near = unpack(near, staying, tuple(pieces))
    arrived = pl.pallas_call(
        arrived_kernel,
        out_shape=token,
        in_specs=[ANY] * (len(back) + 1),
        out_specs=VMEM,
        compiler_params=params(1),
        cost_estimate=cost(6),
        name="arrived",
    )(*back, turned_near)
    pieces = [(s, c, 0, MOMENTS) for c in range(chunks) for s in far]
    (out,) = unpack(far, back, tuple(pieces), out, arrived)
    return jnp.swapaxes(out, 0, 1)


def solution(mesh):
    return jax.shard_map(
        on_device,
        mesh=mesh,
        in_specs=(
            P("gy", "gx"),
            P("gy", None, "gx"),
            P("gy", "gx"),
            P("gy", None, "gx"),
            P("gy", None, "gx"),
        ),
        out_specs=P("gy", None, "gx"),
        check_vma=False,
    )
```

```python
import functools
import math

import jax
import jax.numpy as jnp
from jax import lax
from jax.experimental import pallas as pl
from jax.experimental.pallas import tpu as pltpu
from jax.sharding import PartitionSpec as P

time_step = 0.05
enforcement_weight = 4.0
plate_speed = 0.5
dissipation_speed = 0.25
coeffs = (0.75, -0.15, 1.0 / 60.0)

MOMENTS = 13
HALO = 8
NEED = 6
SKIP = HALO - NEED
RHO, TEMP = 0, 4
VMEM = pl.BlockSpec(memory_space=pltpu.VMEM)
ANY = pl.BlockSpec(memory_space=pl.ANY)
HBM = pl.BlockSpec(memory_space=pltpu.HBM)
SMEM = pl.BlockSpec(memory_space=pltpu.SMEM)


def cost(micros):
    return pl.CostEstimate(
        flops=int(micros * 1e9), bytes_accessed=int(micros * 3e6), transcendentals=0
    )


def params(mib=48):
    return pltpu.CompilerParams(vmem_limit_bytes=mib * 2**20)


def code(f, x):
    if f == RHO:
        return x - 1.25
    if f == TEMP:
        return jnp.exp2(160.0 * (x - 1.25))
    return x


def decode(f, y):
    if f == RHO:
        return y + 1.25
    if f == TEMP:
        return jnp.log2(y) * (1.0 / 160.0) + 1.25
    return y


def flux(u, d, f):
    v = u[1 + d]
    temperature = u[4]
    heat = u[10:13]
    s = [[u[5], u[6], u[8]], [u[6], u[7], u[9]], [u[8], u[9], None]]
    if f == 0:
        return u[0] * v
    if f < 4:
        i = f - 1
        out = u[1 + i] * v + s[i][d]
        return out + temperature if i == d else out
    if f == 4:
        return v * temperature + 2.0 / 3.0 * heat[d]
    if f < 10:
        i, j = ((0, 0), (0, 1), (1, 1), (0, 2), (1, 2))[f - 5]
        out = v * s[i][j]
        weight = {}
        if j == d:
            weight[i] = weight.get(i, 0.0) + 0.4
        if i == d:
            weight[j] = weight.get(j, 0.0) + 0.4
        if i == j:
            weight[d] = weight.get(d, 0.0) - 4.0 / 15.0
        for k, w in weight.items():
            out = out + w * heat[k]
        return out
    i = f - 10
    out = v * heat[i] + temperature * s[i][d]
    return out + 2.5 * temperature * temperature if i == d else out


def sources(u, wall):
    near = jnp.abs(wall)
    nu = u[0] * jnp.sqrt(u[4] * u[4] + 0.25)
    heavy, light = -0.8 * nu, -0.55 * nu
    out = [None] * MOMENTS
    out[1] = -enforcement_weight * near * (u[1] - plate_speed * wall)
    out[4] = -dissipation_speed * nu * u[4] - enforcement_weight * near * (u[4] - 1.0)
    for f in range(5, 10):
        out[f] = heavy * u[f]
    for f in range(10, 13):
        out[f] = light * u[f]
    return out


def along_of(fx, turned, f):
    count = fx.shape[0] // 8
    turned[f] = fx
    x = [turned[f, pl.ds(v, 8, stride=count), :] for v in range(count)]
    x = [pltpu.roll(y, 1, 0) for y in x[-3:]] + x + [pltpu.roll(y, 7, 0) for y in x[:3]]
    for v in range(count):
        total = None
        for k in range(3):
            term = coeffs[k] * (x[3 + v + k + 1] - x[3 + v - k - 1])
            total = term if total is None else total + term
        turned[MOMENTS + f, pl.ds(v, 8, stride=count), :] = total
    return turned.at[MOMENTS + f]


def message_start(me, s, slab):
    to = jnp.bitwise_xor(me, s)
    return pl.multiple_of(to * slab + jnp.where(to % 2 == 0, slab // 2, 0), 16)


GROUPS = ((0, 1), (1, 4), (4, 5), (5, 8), (8, 10), (10, 12), (12, 13))


def pack_kernel(n, two, me_ref, *refs):
    (rho, vel, temp, stress, heat), refs = refs[:5], refs[5:]
    inputs = (rho, vel, temp, stress.at[0:3], stress.at[3:5], heat.at[0:2], heat.at[2:3])
    count = n if two else 0
    outs, (strip, given, arrived), refs = refs[: count + 1], refs[count + 1 : count + 4], refs[count + 4 :]
    held, left_at = refs[:-1], refs[-1]
    rows, cols = given.shape[1:]
    slab = cols // n
    me = me_ref[0]
    copies = []
    for k, (first, end) in enumerate(GROUPS):
        dst = given.at[first] if len(inputs[k].shape) == 2 else given.at[first:end]
        copies.append(pltpu.make_async_copy(inputs[k], dst, arrived.at[k]))
        copies[k].start()
    wide = slab // 2 + 2 * HALO
    lane = min(rows, 128)
    strip[0:HALO, :] = jnp.zeros((HALO, rows), jnp.float32)
    strip[HALO + cols :, :] = jnp.zeros((HALO, rows), jnp.float32)
    leaving = []
    done = 0
    for at, (first, end) in enumerate(GROUPS):
        copies[at].wait()
        for f in range(first, end):
            strip[HALO : HALO + cols, :] = code(f, given[f]).T
            for s in range(count):
                block = strip[pl.ds(message_start(me, s, slab), wide), :][SKIP : wide - SKIP]
                halves = [block[:, p : p + lane] for p in range(0, rows, lane)]
                held[s][f] = jnp.concatenate(halves, axis=0).astype(jnp.bfloat16)
            for d in range(n):
                start = d * slab + (slab // 2 if two and d % 2 else 0)
                block = strip[start : start + held[count].shape[2], :]
                held[count][d, f] = block.astype(jnp.bfloat16)
        if at > 0:
            span = pl.ds(done, end - done)
            for k, out in enumerate(outs):
                at_span = (slice(None), span) if k == count else span
                mine, there = held[k].at[at_span], out.at[at_span]
                copy = pltpu.make_async_copy(mine, there, left_at.at[k, at - 1])
                copy.start()
                leaving.append(copy)
            done = end
    for copy in leaving:
        copy.wait()


def edge_kernel(tall, tie, left, right):
    n, _, wide, _ = tall.shape
    left[...] = tall[0, :, 0 : 2 * HALO, :]
    right[...] = tall[n - 1, :, wide - 2 * HALO : wide, :]


def rest_kernel(n, two, me_ref, tall, before, after, *outs):
    me = me_ref[0]
    count, wide = outs[0].shape[1], tall.shape[2]
    line = lax.broadcasted_iota(jnp.int32, before.shape[1:], 0)
    for s in range(n):
        to = jnp.bitwise_xor(me, s)
        even = to % 2 == 0
        for f in range(MOMENTS):
            block = tall[to, f].astype(jnp.float32)
            first, last = block[: 2 * HALO], block[wide - 2 * HALO :]
            first = jnp.where((line < HALO) & (to == 0), before[f].astype(jnp.float32), first)
            last = jnp.where((line >= HALO) & (to == n - 1), after[f].astype(jnp.float32), last)
            between = [block[2 * HALO : wide - 2 * HALO]] if wide > 4 * HALO else []
            block = jnp.concatenate([first, *between, last], axis=0)
            if two:
                near_end = block[SKIP : SKIP + count]
                far_end = block[wide - SKIP - count : wide - SKIP]
                block = jnp.where(even, near_end, far_end)
            outs[s][f] = block.astype(jnp.bfloat16)


def grid_kernel(n, rows, slots, me_ref, *refs):
    out, sin_col, cos_col, back_col, line_col, total = refs[-6:]
    size = n * rows
    last = size - 1
    half = math.pi / (2.0 * last)
    me = me_ref[0]
    step = 64
    lane = min(rows, 128)

    def table(s):
        line = jnp.bitwise_xor(me, s) * rows + lax.broadcasted_iota(jnp.int32, (8, rows), 1)
        angle = half * line.astype(jnp.float32)
        edge = (line == 0) | (line == last)
        sign = (1 - 2 * (line & 1)).astype(jnp.float32)
        return line.astype(jnp.float32), jnp.sin(angle), jnp.cos(angle), edge, sign

    def column(x):
        return jnp.broadcast_to(x[0:1], (lane, rows)).T

    for s in range(n):
        line, sine, cosine, edge, sign = table(s)
        here = pl.ds(s * rows, rows)
        line_col[here, :] = column(line)
        sin_col[here, :] = column(sine)
        cos_col[here, :] = column(cosine)
        back_col[here, :] = column(jnp.where(edge, 0.5 * sign, sign))

    for index, s in enumerate(slots):
        line, sine, cosine, edge, sign = table(s)
        front = (-math.pi / last) * sine * cosine * jnp.where(edge, 2.0 * sign, sign)
        for p in range(rows // lane):
            here = pl.ds(index * rows + p * lane, lane)
            own = pl.ds(s * rows + p * lane, lane)
            line_i, sin_i, cos_i, front_i = (
                x[0:1, p * lane : (p + 1) * lane] for x in (line, sine, cosine, front)
            )
            total[...] = jnp.zeros_like(total)

            def block(t, carry):
                down = pl.ds(pl.multiple_of(t * step, step), step)
                gap = line_i - line_col[down, :]
                same = gap == 0.0
                x = half * gap
                x2 = x * x
                poly = -1.0 / 39916800.0
                for c in (1 / 362880.0, -1 / 5040.0, 1 / 120.0, -1 / 6.0, 1.0):
                    poly = poly * x2 + c
                plus = sin_i * cos_col[down, :] + cos_i * sin_col[down, :]
                denom = jnp.where(same, 1.0, plus * (x * poly))
                off = jnp.where(same, 0.0, front_i * back_col[down, :] / denom)
                total[...] += jnp.sum(off.reshape(step // 8, 8, lane), axis=0)
                out[down, here] = off.astype(jnp.bfloat16)
                return carry

            lax.fori_loop(0, size // step, block, 0)
            diagonal = -jnp.sum(total[...], axis=0, keepdims=True)
            same = lax.broadcasted_iota(jnp.int32, (lane, lane), 0) == (
                lax.broadcasted_iota(jnp.int32, (lane, lane), 1)
            )
            tile = out[own, here].astype(jnp.float32)
            out[own, here] = jnp.where(same, diagonal, tile).astype(jnp.bfloat16)


def weights_of(parts, grids, s, down=slice(None)):
    for part, grid in zip(parts, grids):
        if s in part:
            rows = grid.shape[1] // len(part)
            at = part.index(s) * rows
            return grid[down, at : at + rows]


def flip_kernel(n, parts, far, *refs):
    grids, out = refs[: len(parts)], refs[-1]
    rows = out.shape[0] // n
    line = lax.broadcasted_iota(jnp.int32, (rows, rows), 0)
    turn = line + lax.broadcasted_iota(jnp.int32, (rows, rows), 1) == rows - 1
    turn = jnp.where(turn, 1.0, 0.0).astype(jnp.bfloat16)
    for k, s in enumerate(far):
        for a in range(n):
            down = (a ^ (n - 1)) * rows
            tile = weights_of(parts, grids, s ^ (n - 1), slice(down, down + rows))
            tile = jnp.dot(turn, tile, preferred_element_type=jnp.float32).astype(jnp.bfloat16)
            tile = -jnp.dot(tile, turn, preferred_element_type=jnp.float32)
            out[a * rows : (a + 1) * rows, k * rows : (k + 1) * rows] = tile.astype(jnp.bfloat16)


def far_first(arrays):
    half = len(arrays) // 2
    return [arrays[0], *arrays[half:], *arrays[1:half]]


def in_slots(arrays):
    half = len(arrays) // 2
    return [arrays[0], *arrays[half + 1 :], *arrays[1 : half + 1]]


def section_kernel(n, two, second, far, parts, me_ref, *refs):
    grids, refs = refs[: len(parts)], refs[len(parts) :]
    firsts, refs = in_slots(refs[:n]), refs[n:]
    if second:
        rests, refs = in_slots(refs[:n]), refs[n + 1 :]
    outs, refs = refs[: len(far)], refs[len(far) :]
    u1, r0, fy1, u0, fy0, product, turned = refs
    wide, size = u0.shape[1:]
    rows = size // n
    core = wide - 2 * HALO
    me = me_ref[0]
    right_first = me % 2 == 0
    lane = min(rows, 128)
    strips = rows // lane

    part = wide - 2 * SKIP
    lap = 2 * NEED
    for s in range(n):
        for f in range(MOMENTS):
            if not two:
                u0[f, :, pl.ds(s * rows, rows)] = decode(f, firsts[s][f].astype(jnp.float32))
                continue
            whole = decode(f, firsts[s][f].astype(jnp.float32))
            for p in range(strips):
                here = pl.ds(s * rows + p * lane, lane)
                first = whole[p * part : (p + 1) * part]
                u0[f, 0:8, here] = jnp.zeros((8, lane), jnp.float32)
                u0[f, wide - 8 :, here] = jnp.zeros((8, lane), jnp.float32)
                if not second:
                    u0[f, SKIP : SKIP + part, here] = first
                    continue
                new = rests[s][f, :, p * lane : (p + 1) * lane].astype(jnp.float32)
                new = decode(f, new)
                left = jnp.concatenate([new, first[:lap]], axis=0)
                right = jnp.concatenate([first[part - lap :], new], axis=0)
                u0[f, SKIP : SKIP + part, here] = jnp.where(right_first, left, right)

    for s in range(n):
        for p in range(strips):
            here = pl.ds(s * rows + p * lane, lane)
            u = [u0[f, :, here] for f in range(MOMENTS)]
            for f in range(MOMENTS):
                fy0[f * wide : (f + 1) * wide, here] = flux(u, 1, f).astype(jnp.bfloat16)

    middle = slice(HALO, HALO + core)
    for s in range(n):
        weights = weights_of(parts, grids, s)
        product[...] = jnp.dot(fy0[...], weights, preferred_element_type=jnp.float32)
        for p in range(strips):
            here = pl.ds(s * rows + p * lane, lane)
            there = pl.ds(p * lane, lane)
            u = [u0[f, :, here] for f in range(MOMENTS)]
            src = sources(u, walls(me, s, p, n, rows, wide))
            new = []
            for f in range(MOMENTS):
                across = product[f * wide : (f + 1) * wide, there]
                rate = -(along_of(flux(u, 0, f), turned, f)[...] + across)
                if src[f] is not None:
                    rate = rate + src[f]
                r0[f, :, here] = rate[middle]
                new.append(u[f] + time_step * rate)
                u1[f, :, here] = new[f]
            inner = [x[middle] for x in new]
            for f in range(MOMENTS):
                fy1[f * core : (f + 1) * core, here] = flux(inner, 1, f).astype(jnp.bfloat16)

    def place(s, f):
        return outs[far.index(s)].at[f]

    finish(n, far, me_ref, parts, grids, u1, r0, fy1, place, product, turned)


THIRDS = ((0, 5), (5, 9), (9, MOMENTS))


def finish_kernel(n, near, parts, chunks, me_ref, *refs):
    grids, refs = refs[: len(parts)], refs[len(parts) :]
    states, product, turned = refs[: 3 * chunks], *refs[-2:]
    outs = refs[-2 - 1 - len(THIRDS) * (len(near) - 1) : -2]
    core = outs[0].shape[1] // chunks

    def place(c, s, f):
        span = slice(c * core, (c + 1) * core)
        if s == 0:
            return outs[0].at[f, span]
        third = [first <= f < end for first, end in THIRDS].index(True)
        return outs[1 + len(THIRDS) * (s - 1) + third].at[f - THIRDS[third][0], span]

    for c in range(chunks):
        part = functools.partial(place, c)
        finish(n, near, me_ref, parts, grids, *states[3 * c : 3 * c + 3], part, product, turned)


def walls(me, s, p, n, rows, count):
    lane = min(rows, 128)
    line = jnp.bitwise_xor(me, s) * rows + p * lane
    line = line + lax.broadcasted_iota(jnp.int32, (count, lane), 1)
    return jnp.where(line == 0, 1.0, jnp.where(line == n * rows - 1, -1.0, 0.0))


def finish(n, slots, me_ref, parts, grids, u1, r0, fy1, outs, product, turned):
    wide, size = u1.shape[1:]
    rows = size // n
    core = wide - 2 * HALO
    lane = min(rows, 128)
    me = me_ref[0]
    middle = slice(HALO, HALO + core)
    for k, s in enumerate(slots):
        weights = weights_of(parts, grids, s)
        product[0 : MOMENTS * core, :] = jnp.dot(
            fy1[...], weights, preferred_element_type=jnp.float32
        )
        for p in range(rows // lane):
            here = pl.ds(s * rows + p * lane, lane)
            there = pl.ds(p * lane, lane)
            u = [u1[f, :, here] for f in range(MOMENTS)]
            inner = [x[middle] for x in u]
            src = sources(inner, walls(me, s, p, n, rows, core))
            for f in range(MOMENTS):
                across = product[f * core : (f + 1) * core, there]
                rate = -(along_of(flux(u, 0, f), turned, f)[middle, :] + across)
                if src[f] is not None:
                    rate = rate + src[f]
                rate = 0.5 * (r0[f, :, here] + rate)
                target = outs(s, f)
                target[:, there] = rate.astype(target.dtype)


def arrived_kernel(*refs):
    refs[-1][...] = jnp.zeros_like(refs[-1])


def unpack_kernel(n, slots, chunks, pieces, token, me_ref, *refs):
    out, tall, held, leaving = *refs[-4 - len(token) : -3 - len(token)], *refs[-3:]
    for ref in refs[-3 - len(token) : -3]:
        ref[...] = jnp.zeros_like(ref)
    rows, cols = held.shape[1:]
    slab = cols // len(slots)
    width = slab // chunks
    me = me_ref[0]
    copies = []
    for f in range(MOMENTS):
        for array, (s, c, first, end) in zip(refs, pieces):
            if not first <= f < end:
                continue
            of = jnp.bitwise_xor(me, s)
            for k in range(chunks) if c is None else (c,):
                start = of % len(slots) * slab
                if chunks == 2:
                    start += jnp.where(of % 2 == 0, width * (1 - k), width * k)
                here = pl.ds(pl.multiple_of(start, 16), width)
                piece = array[f - first, k * width : (k + 1) * width] if c is None else array[f]
                tall[f, here, :] = piece.astype(jnp.float32)
        held[f] = tall[f].T
        side = jnp.bitwise_xor(me, slots[0]) // len(slots) * cols
        there = out.at[f, :, pl.ds(pl.multiple_of(side, 128), cols)]
        copies.append(pltpu.make_async_copy(held.at[f], there, leaving.at[f]))
        copies[f].start()
    for copy in copies:
        copy.wait()


def to_partner(array, n, s):
    return array if s == 0 else lax.ppermute(array, "gy", [(i, i ^ s) for i in range(n)])


def exchange(arrays, n, slots):
    pairs = list(zip(arrays, slots))[::-1]
    return [to_partner(array, n, s) for array, s in pairs][::-1]


def on_device(rho, vel, temp, stress, heat):
    rows, cols = rho.shape
    n = lax.axis_size("gy")
    ring = lax.axis_size("gx")
    size, slab = n * rows, cols // n
    two = slab % 32 == 0
    core = slab // 2 if two else slab
    wide = core + 2 * HALO
    lane = min(rows, 128)
    half = jnp.bfloat16
    me = lax.axis_index("gy").astype(jnp.int32).reshape(1)
    vel, stress, heat = (jnp.swapaxes(a, 0, 1) for a in (vel, stress, heat))

    def message(width, kind=half):
        return jax.ShapeDtypeStruct((MOMENTS, width, rows), kind)

    far, near = (tuple(range(n // 2, n)), tuple(range(n // 2)))
    inputs = (rho, vel, temp, stress, heat)

    def pack(arrays):
        sent = (MOMENTS, (wide - 2 * SKIP) * (rows // lane), lane)
        shapes = [jax.ShapeDtypeStruct(sent, half)] * n if two else []
        shapes += [jax.ShapeDtypeStruct((n, MOMENTS, wide, rows), half)]
        return pl.pallas_call(
            functools.partial(pack_kernel, n, two),
            out_shape=shapes,
            in_specs=[SMEM] + [HBM] * len(arrays),
            out_specs=[ANY] * len(shapes),
            scratch_shapes=[
                pltpu.VMEM((cols + 2 * HALO, rows), jnp.float32),
                pltpu.VMEM((MOMENTS, rows, cols), jnp.float32),
                pltpu.SemaphoreType.DMA((len(GROUPS),)),
            ]
            + [pltpu.VMEM(x.shape, x.dtype) for x in shapes]
            + [pltpu.SemaphoreType.DMA((len(shapes), len(GROUPS)))],
            compiler_params=params(56),
            cost_estimate=cost(2),
            name="pack",
        )(me, *arrays)

    firsts = []
    if two:
        *firsts, tall = pack(inputs)
        firsts = exchange(firsts, n, range(n))
    else:
        (tall,) = pack(inputs)

    def grid_of(slots, *ties):
        return pl.pallas_call(
            functools.partial(grid_kernel, n, rows, slots),
            out_shape=jax.ShapeDtypeStruct((size, len(slots) * rows), half),
            in_specs=[SMEM] + [ANY] * len(ties),
            out_specs=VMEM,
            scratch_shapes=[pltpu.VMEM((size, lane), jnp.float32)] * 4
            + [pltpu.VMEM((8, lane), jnp.float32)],
            compiler_params=params(24),
            cost_estimate=cost(1),
            name="grid",
        )(me, *ties)

    parts = (near[: n // 4], near[n // 4 :])
    grids = [grid_of(part) for part in parts]
    left, right = pl.pallas_call(
        edge_kernel,
        out_shape=[message(2 * HALO)] * 2,
        in_specs=[VMEM, ANY],
        out_specs=[VMEM] * 2,
        compiler_params=params(24),
        cost_estimate=cost(0.2),
        name="edges",
    )(tall, grids[0])
    up = [(i, (i + 1) % ring) for i in range(ring)]
    before = lax.ppermute(right, "gx", up)
    after = lax.ppermute(left, "gx", [(j, i) for i, j in up])
    turned = pl.pallas_call(
        functools.partial(flip_kernel, n, parts, far),
        out_shape=jax.ShapeDtypeStruct((size, len(far) * rows), half),
        in_specs=[VMEM] * 2,
        out_specs=VMEM,
        compiler_params=params(24),
        cost_estimate=cost(0.3),
        name="flip",
    )(*grids)
    all_parts, all_grids = (*parts, far), (*grids, turned)
    rests = pl.pallas_call(
        functools.partial(rest_kernel, n, two),
        out_shape=[message(core if two else wide)] * n,
        in_specs=[SMEM] + [VMEM] * 3,
        out_specs=[VMEM] * n,
        compiler_params=params(),
        cost_estimate=cost(0.2),
        name="rest",
    )(me, tall, before, after)
    rests = exchange(rests, n, range(n))

    def sections(second, *arrays):
        state = [
            jax.ShapeDtypeStruct((MOMENTS, wide, size), jnp.float32),
            jax.ShapeDtypeStruct((MOMENTS, core, size), jnp.float32),
            jax.ShapeDtypeStruct((MOMENTS * core, size), half),
        ]
        *crossing, u1, r0, fy1 = pl.pallas_call(
            functools.partial(section_kernel, n, two, second, far, all_parts),
            out_shape=[message(core)] * len(far) + state,
            in_specs=[SMEM] + [VMEM] * (len(arrays) + 3 - second) + [ANY] * second,
            out_specs=[VMEM] * (len(far) + 3),
            scratch_shapes=[
                pltpu.VMEM((MOMENTS, wide, size), jnp.float32),
                pltpu.VMEM((MOMENTS * wide, size), half),
                pltpu.VMEM((MOMENTS * wide, rows), jnp.float32),
                pltpu.VMEM((2 * MOMENTS, wide, lane), jnp.float32),
            ],
            compiler_params=params(24),
            cost_estimate=cost(6),
            name="sections",
        )(me, *all_grids, *arrays)
        return crossing, [u1, r0, fy1]

    def finished(states, *ties):
        thirds = [jax.ShapeDtypeStruct((end - first, slab, rows), half) for first, end in THIRDS]
        shapes = [message(slab, jnp.float32)] + thirds * (len(near) - 1)
        own, *others = pl.pallas_call(
            functools.partial(finish_kernel, n, near, parts, len(states) // 3),
            out_shape=shapes,
            in_specs=[SMEM] + [VMEM] * (len(states) + 2) + [ANY] * len(ties),
            out_specs=[VMEM] * len(shapes),
            scratch_shapes=[
                pltpu.VMEM((MOMENTS * core, rows), jnp.float32),
                pltpu.VMEM((2 * MOMENTS, wide, lane), jnp.float32),
            ],
            compiler_params=params(24),
            cost_estimate=cost(4),
            name="finish",
        )(me, *grids, *states, *ties)
        slots = [s for s in near[1:] for _ in THIRDS]
        return [own, *exchange(others, n, slots)]

    if two:
        firsts, rests = far_first(firsts), far_first(rests)
        crossing, states = sections(False, *firsts)
        back = exchange(crossing, n, far)
        crossing, more = sections(True, *firsts, *rests, crossing[0])
        staying = finished(states + more, *back)
        back += exchange(crossing, n, far)
    else:
        crossing, states = sections(False, *far_first(rests))
        staying = finished(states)
        back = exchange(crossing, n, far)
    chunks = 2 if two else 1
    token = jax.ShapeDtypeStruct((8, 128), jnp.float32)

    def unpack(slots, arrays, pieces, *before):
        alias = {1 + len(arrays): 0} if before else {}
        tokens = [] if before else [token]
        return pl.pallas_call(
            functools.partial(unpack_kernel, n, slots, chunks, pieces, tokens),
            out_shape=[jax.ShapeDtypeStruct((MOMENTS, rows, cols), jnp.float32), *tokens],
            in_specs=[SMEM] + [VMEM] * len(arrays) + [ANY] * len(before),
            out_specs=[ANY] + [VMEM] * len(tokens),
            scratch_shapes=[
                pltpu.VMEM((MOMENTS, cols // 2, rows), jnp.float32),
                pltpu.VMEM((MOMENTS, rows, cols // 2), jnp.float32),
                pltpu.SemaphoreType.DMA((MOMENTS,)),
            ],
            input_output_aliases=alias,
            compiler_params=params(24),
            cost_estimate=cost(0.01),
            name="unpack",
        )(me, *arrays, *before)

    pieces = [(0, None, 0, MOMENTS)] + [(s, None, *span) for s in near[1:] for span in THIRDS]
    out, turned_near = unpack(near, staying, tuple(pieces))
    arrived = pl.pallas_call(
        arrived_kernel,
        out_shape=token,
        in_specs=[ANY] * (len(back) + 1),
        out_specs=VMEM,
        compiler_params=params(1),
        cost_estimate=cost(6),
        name="arrived",
    )(*back, turned_near)
    pieces = [(s, c, 0, MOMENTS) for c in range(chunks) for s in far]
    (out,) = unpack(far, back, tuple(pieces), out, arrived)
    return jnp.swapaxes(out, 0, 1)


def solution(mesh):
    return jax.shard_map(
        on_device,
        mesh=mesh,
        in_specs=(
            P("gy", "gx"),
            P("gy", None, "gx"),
            P("gy", "gx"),
            P("gy", None, "gx"),
            P("gy", None, "gx"),
        ),
        out_specs=P("gy", None, "gx"),
        check_vma=False,
    )
```

```python
import functools
import math

import jax
import jax.numpy as jnp
from jax import lax
from jax.experimental import pallas as pl
from jax.experimental.pallas import tpu as pltpu
from jax.sharding import PartitionSpec as P

time_step = 0.05
enforcement_weight = 4.0
plate_speed = 0.5
dissipation_speed = 0.25
coeffs = (0.75, -0.15, 1.0 / 60.0)

MOMENTS = 13
HALO = 8
NEED = 6
SKIP = HALO - NEED
RHO, TEMP = 0, 4
VMEM = pl.BlockSpec(memory_space=pltpu.VMEM)
ANY = pl.BlockSpec(memory_space=pl.ANY)
HBM = pl.BlockSpec(memory_space=pltpu.HBM)
SMEM = pl.BlockSpec(memory_space=pltpu.SMEM)


def cost(micros):
    return pl.CostEstimate(
        flops=int(micros * 1e9), bytes_accessed=int(micros * 3e6), transcendentals=0
    )


def params(mib=48):
    return pltpu.CompilerParams(vmem_limit_bytes=mib * 2**20)


def code(f, x):
    if f == RHO:
        return x - 1.25
    if f == TEMP:
        return jnp.exp2(160.0 * (x - 1.25))
    return x


def decode(f, y):
    if f == RHO:
        return y + 1.25
    if f == TEMP:
        return jnp.log2(y) * (1.0 / 160.0) + 1.25
    return y


def flux(u, d, f):
    v = u[1 + d]
    temperature = u[4]
    heat = u[10:13]
    s = [[u[5], u[6], u[8]], [u[6], u[7], u[9]], [u[8], u[9], None]]
    if f == 0:
        return u[0] * v
    if f < 4:
        i = f - 1
        out = u[1 + i] * v + s[i][d]
        return out + temperature if i == d else out
    if f == 4:
        return v * temperature + 2.0 / 3.0 * heat[d]
    if f < 10:
        i, j = ((0, 0), (0, 1), (1, 1), (0, 2), (1, 2))[f - 5]
        out = v * s[i][j]
        weight = {}
        if j == d:
            weight[i] = weight.get(i, 0.0) + 0.4
        if i == d:
            weight[j] = weight.get(j, 0.0) + 0.4
        if i == j:
            weight[d] = weight.get(d, 0.0) - 4.0 / 15.0
        for k, w in weight.items():
            out = out + w * heat[k]
        return out
    i = f - 10
    out = v * heat[i] + temperature * s[i][d]
    return out + 2.5 * temperature * temperature if i == d else out


def sources(u, wall):
    near = jnp.abs(wall)
    nu = u[0] * jnp.sqrt(u[4] * u[4] + 0.25)
    heavy, light = -0.8 * nu, -0.55 * nu
    out = [None] * MOMENTS
    out[1] = -enforcement_weight * near * (u[1] - plate_speed * wall)
    out[4] = -dissipation_speed * nu * u[4] - enforcement_weight * near * (u[4] - 1.0)
    for f in range(5, 10):
        out[f] = heavy * u[f]
    for f in range(10, 13):
        out[f] = light * u[f]
    return out


def along_of(fx, turned, f):
    count = fx.shape[0] // 8
    turned[f] = fx
    x = [turned[f, pl.ds(v, 8, stride=count), :] for v in range(count)]
    x = [pltpu.roll(y, 1, 0) for y in x[-3:]] + x + [pltpu.roll(y, 7, 0) for y in x[:3]]
    for v in range(count):
        total = None
        for k in range(3):
            term = coeffs[k] * (x[3 + v + k + 1] - x[3 + v - k - 1])
            total = term if total is None else total + term
        turned[MOMENTS + f, pl.ds(v, 8, stride=count), :] = total
    return turned.at[MOMENTS + f]


def message_start(me, s, slab):
    to = jnp.bitwise_xor(me, s)
    return pl.multiple_of(to * slab + jnp.where(to % 2 == 0, slab // 2, 0), 16)


GROUPS = ((0, 1), (1, 4), (4, 5), (5, 8), (8, 10), (10, 12), (12, 13))


def pack_kernel(n, two, me_ref, *refs):
    (rho, vel, temp, stress, heat), refs = refs[:5], refs[5:]
    inputs = (rho, vel, temp, stress.at[0:3], stress.at[3:5], heat.at[0:2], heat.at[2:3])
    count = n if two else 0
    outs, (strip, given, arrived), refs = refs[: count + 1], refs[count + 1 : count + 4], refs[count + 4 :]
    held, left_at = refs[:-1], refs[-1]
    rows, cols = given.shape[1:]
    slab = cols // n
    me = me_ref[0]
    copies = []
    for k, (first, end) in enumerate(GROUPS):
        dst = given.at[first] if len(inputs[k].shape) == 2 else given.at[first:end]
        copies.append(pltpu.make_async_copy(inputs[k], dst, arrived.at[k]))
        copies[k].start()
    wide = slab // 2 + 2 * HALO
    lane = min(rows, 128)
    strip[0:HALO, :] = jnp.zeros((HALO, rows), jnp.float32)
    strip[HALO + cols :, :] = jnp.zeros((HALO, rows), jnp.float32)
    leaving = []
    done = 0
    for at, (first, end) in enumerate(GROUPS):
        copies[at].wait()
        for f in range(first, end):
            strip[HALO : HALO + cols, :] = code(f, given[f]).T
            for s in range(count):
                block = strip[pl.ds(message_start(me, s, slab), wide), :][SKIP : wide - SKIP]
                halves = [block[:, p : p + lane] for p in range(0, rows, lane)]
                held[s][f] = jnp.concatenate(halves, axis=0).astype(jnp.bfloat16)
            held[count][f] = strip[...].astype(jnp.bfloat16)
        if at > 0:
            span = pl.ds(done, end - done)
            for k, out in enumerate(outs):
                copy = pltpu.make_async_copy(held[k].at[span], out.at[span], left_at.at[k, at - 1])
                copy.start()
                leaving.append(copy)
            done = end
    for copy in leaving:
        copy.wait()


def edge_kernel(tall, tie, left, right):
    cols = tall.shape[1] - 2 * HALO
    left[...] = tall[:, 0 : 2 * HALO, :]
    right[...] = tall[:, cols : cols + 2 * HALO, :]


def rest_kernel(n, two, me_ref, tall, before, after, *outs):
    me = me_ref[0]
    slab = (tall.shape[1] - 2 * HALO) // n
    count = outs[0].shape[1]
    wide = slab // 2 + 2 * HALO if two else count
    line = lax.broadcasted_iota(jnp.int32, before.shape[1:], 0)
    for s in range(n):
        to = jnp.bitwise_xor(me, s)
        even = to % 2 == 0
        start = to * slab
        if two:
            start += jnp.where(even, 0, slab // 2)
        start = pl.multiple_of(start, 16)
        for f in range(MOMENTS):
            block = tall[f, pl.ds(start, wide), :].astype(jnp.float32)
            first, last = block[: 2 * HALO], block[wide - 2 * HALO :]
            first = jnp.where((line < HALO) & (to == 0), before[f].astype(jnp.float32), first)
            last = jnp.where((line >= HALO) & (to == n - 1), after[f].astype(jnp.float32), last)
            between = [block[2 * HALO : wide - 2 * HALO]] if wide > 4 * HALO else []
            block = jnp.concatenate([first, *between, last], axis=0)
            if two:
                near_end = block[SKIP : SKIP + count]
                far_end = block[wide - SKIP - count : wide - SKIP]
                block = jnp.where(even, near_end, far_end)
            outs[s][f] = block.astype(jnp.bfloat16)


def grid_kernel(n, rows, slots, me_ref, *refs):
    out, sin_col, cos_col, back_col, line_col, total = refs[-6:]
    size = n * rows
    last = size - 1
    half = math.pi / (2.0 * last)
    me = me_ref[0]
    step = 64
    lane = min(rows, 128)

    def table(s):
        line = jnp.bitwise_xor(me, s) * rows + lax.broadcasted_iota(jnp.int32, (8, rows), 1)
        angle = half * line.astype(jnp.float32)
        edge = (line == 0) | (line == last)
        sign = (1 - 2 * (line & 1)).astype(jnp.float32)
        return line.astype(jnp.float32), jnp.sin(angle), jnp.cos(angle), edge, sign

    def column(x):
        return jnp.broadcast_to(x[0:1], (lane, rows)).T

    for s in range(n):
        line, sine, cosine, edge, sign = table(s)
        here = pl.ds(s * rows, rows)
        line_col[here, :] = column(line)
        sin_col[here, :] = column(sine)
        cos_col[here, :] = column(cosine)
        back_col[here, :] = column(jnp.where(edge, 0.5 * sign, sign))

    for index, s in enumerate(slots):
        line, sine, cosine, edge, sign = table(s)
        front = (-math.pi / last) * sine * cosine * jnp.where(edge, 2.0 * sign, sign)
        for p in range(rows // lane):
            here = pl.ds(index * rows + p * lane, lane)
            own = pl.ds(s * rows + p * lane, lane)
            line_i, sin_i, cos_i, front_i = (
                x[0:1, p * lane : (p + 1) * lane] for x in (line, sine, cosine, front)
            )
            total[...] = jnp.zeros_like(total)

            def block(t, carry):
                down = pl.ds(pl.multiple_of(t * step, step), step)
                gap = line_i - line_col[down, :]
                same = gap == 0.0
                x = half * gap
                x2 = x * x
                poly = -1.0 / 39916800.0
                for c in (1 / 362880.0, -1 / 5040.0, 1 / 120.0, -1 / 6.0, 1.0):
                    poly = poly * x2 + c
                plus = sin_i * cos_col[down, :] + cos_i * sin_col[down, :]
                denom = jnp.where(same, 1.0, plus * (x * poly))
                off = jnp.where(same, 0.0, front_i * back_col[down, :] / denom)
                total[...] += jnp.sum(off.reshape(step // 8, 8, lane), axis=0)
                out[down, here] = off.astype(jnp.bfloat16)
                return carry

            lax.fori_loop(0, size // step, block, 0)
            diagonal = -jnp.sum(total[...], axis=0, keepdims=True)
            same = lax.broadcasted_iota(jnp.int32, (lane, lane), 0) == (
                lax.broadcasted_iota(jnp.int32, (lane, lane), 1)
            )
            tile = out[own, here].astype(jnp.float32)
            out[own, here] = jnp.where(same, diagonal, tile).astype(jnp.bfloat16)


def weights_of(parts, grids, s, down=slice(None)):
    for part, grid in zip(parts, grids):
        if s in part:
            rows = grid.shape[1] // len(part)
            at = part.index(s) * rows
            return grid[down, at : at + rows]


def flip_kernel(n, parts, far, *refs):
    grids, out = refs[: len(parts)], refs[-1]
    rows = out.shape[0] // n
    line = lax.broadcasted_iota(jnp.int32, (rows, rows), 0)
    turn = line + lax.broadcasted_iota(jnp.int32, (rows, rows), 1) == rows - 1
    turn = jnp.where(turn, 1.0, 0.0).astype(jnp.bfloat16)
    for k, s in enumerate(far):
        for a in range(n):
            down = (a ^ (n - 1)) * rows
            tile = weights_of(parts, grids, s ^ (n - 1), slice(down, down + rows))
            tile = jnp.dot(turn, tile, preferred_element_type=jnp.float32).astype(jnp.bfloat16)
            tile = -jnp.dot(tile, turn, preferred_element_type=jnp.float32)
            out[a * rows : (a + 1) * rows, k * rows : (k + 1) * rows] = tile.astype(jnp.bfloat16)


def far_first(arrays):
    half = len(arrays) // 2
    return [arrays[0], *arrays[half:], *arrays[1:half]]


def in_slots(arrays):
    half = len(arrays) // 2
    return [arrays[0], *arrays[half + 1 :], *arrays[1 : half + 1]]


def section_kernel(n, two, second, far, parts, me_ref, *refs):
    grids, refs = refs[: len(parts)], refs[len(parts) :]
    firsts, refs = in_slots(refs[:n]), refs[n:]
    if second:
        rests, refs = refs[:n], refs[n + 1 :]
    outs, refs = refs[: len(far)], refs[len(far) :]
    u1, r0, fy1, u0, fy0, product, turned = refs
    wide, size = u0.shape[1:]
    rows = size // n
    core = wide - 2 * HALO
    me = me_ref[0]
    right_first = me % 2 == 0
    lane = min(rows, 128)
    strips = rows // lane

    part = wide - 2 * SKIP
    lap = 2 * NEED
    for s in range(n):
        for f in range(MOMENTS):
            if not two:
                u0[f, :, pl.ds(s * rows, rows)] = decode(f, firsts[s][f].astype(jnp.float32))
                continue
            whole = decode(f, firsts[s][f].astype(jnp.float32))
            for p in range(strips):
                here = pl.ds(s * rows + p * lane, lane)
                first = whole[p * part : (p + 1) * part]
                u0[f, 0:8, here] = jnp.zeros((8, lane), jnp.float32)
                u0[f, wide - 8 :, here] = jnp.zeros((8, lane), jnp.float32)
                if not second:
                    u0[f, SKIP : SKIP + part, here] = first
                    continue
                new = rests[s][f, :, p * lane : (p + 1) * lane].astype(jnp.float32)
                new = decode(f, new)
                left = jnp.concatenate([new, first[:lap]], axis=0)
                right = jnp.concatenate([first[part - lap :], new], axis=0)
                u0[f, SKIP : SKIP + part, here] = jnp.where(right_first, left, right)

    for s in range(n):
        for p in range(strips):
            here = pl.ds(s * rows + p * lane, lane)
            u = [u0[f, :, here] for f in range(MOMENTS)]
            for f in range(MOMENTS):
                fy0[f * wide : (f + 1) * wide, here] = flux(u, 1, f).astype(jnp.bfloat16)

    middle = slice(HALO, HALO + core)
    for s in range(n):
        weights = weights_of(parts, grids, s)
        product[...] = jnp.dot(fy0[...], weights, preferred_element_type=jnp.float32)
        for p in range(strips):
            here = pl.ds(s * rows + p * lane, lane)
            there = pl.ds(p * lane, lane)
            u = [u0[f, :, here] for f in range(MOMENTS)]
            src = sources(u, walls(me, s, p, n, rows, wide))
            new = []
            for f in range(MOMENTS):
                across = product[f * wide : (f + 1) * wide, there]
                rate = -(along_of(flux(u, 0, f), turned, f)[...] + across)
                if src[f] is not None:
                    rate = rate + src[f]
                r0[f, :, here] = rate[middle]
                new.append(u[f] + time_step * rate)
                u1[f, :, here] = new[f]
            inner = [x[middle] for x in new]
            for f in range(MOMENTS):
                fy1[f * core : (f + 1) * core, here] = flux(inner, 1, f).astype(jnp.bfloat16)

    def place(s, f):
        return outs[far.index(s)].at[f]

    finish(n, far, me_ref, parts, grids, u1, r0, fy1, place, product, turned)


THIRDS = ((0, 5), (5, 9), (9, MOMENTS))


def finish_kernel(n, near, parts, chunks, me_ref, *refs):
    grids, refs = refs[: len(parts)], refs[len(parts) :]
    states, product, turned = refs[: 3 * chunks], *refs[-2:]
    outs = refs[-2 - 1 - len(THIRDS) * (len(near) - 1) : -2]
    core = outs[0].shape[1] // chunks

    def place(c, s, f):
        span = slice(c * core, (c + 1) * core)
        if s == 0:
            return outs[0].at[f, span]
        third = [first <= f < end for first, end in THIRDS].index(True)
        return outs[1 + len(THIRDS) * (s - 1) + third].at[f - THIRDS[third][0], span]

    for c in range(chunks):
        part = functools.partial(place, c)
        finish(n, near, me_ref, parts, grids, *states[3 * c : 3 * c + 3], part, product, turned)


def walls(me, s, p, n, rows, count):
    lane = min(rows, 128)
    line = jnp.bitwise_xor(me, s) * rows + p * lane
    line = line + lax.broadcasted_iota(jnp.int32, (count, lane), 1)
    return jnp.where(line == 0, 1.0, jnp.where(line == n * rows - 1, -1.0, 0.0))


def finish(n, slots, me_ref, parts, grids, u1, r0, fy1, outs, product, turned):
    wide, size = u1.shape[1:]
    rows = size // n
    core = wide - 2 * HALO
    lane = min(rows, 128)
    me = me_ref[0]
    middle = slice(HALO, HALO + core)
    for k, s in enumerate(slots):
        weights = weights_of(parts, grids, s)
        product[0 : MOMENTS * core, :] = jnp.dot(
            fy1[...], weights, preferred_element_type=jnp.float32
        )
        for p in range(rows // lane):
            here = pl.ds(s * rows + p * lane, lane)
            there = pl.ds(p * lane, lane)
            u = [u1[f, :, here] for f in range(MOMENTS)]
            inner = [x[middle] for x in u]
            src = sources(inner, walls(me, s, p, n, rows, core))
            for f in range(MOMENTS):
                across = product[f * core : (f + 1) * core, there]
                rate = -(along_of(flux(u, 0, f), turned, f)[middle, :] + across)
                if src[f] is not None:
                    rate = rate + src[f]
                rate = 0.5 * (r0[f, :, here] + rate)
                target = outs(s, f)
                target[:, there] = rate.astype(target.dtype)


def arrived_kernel(*refs):
    refs[-1][...] = jnp.zeros_like(refs[-1])


def unpack_kernel(n, slots, chunks, pieces, token, me_ref, *refs):
    out, tall, held, leaving = *refs[-4 - len(token) : -3 - len(token)], *refs[-3:]
    for ref in refs[-3 - len(token) : -3]:
        ref[...] = jnp.zeros_like(ref)
    rows, cols = held.shape[1:]
    slab = cols // len(slots)
    width = slab // chunks
    me = me_ref[0]
    copies = []
    for f in range(MOMENTS):
        for array, (s, c, first, end) in zip(refs, pieces):
            if not first <= f < end:
                continue
            of = jnp.bitwise_xor(me, s)
            for k in range(chunks) if c is None else (c,):
                start = of % len(slots) * slab
                if chunks == 2:
                    start += jnp.where(of % 2 == 0, width * (1 - k), width * k)
                here = pl.ds(pl.multiple_of(start, 16), width)
                piece = array[f - first, k * width : (k + 1) * width] if c is None else array[f]
                tall[f, here, :] = piece.astype(jnp.float32)
        held[f] = tall[f].T
        side = jnp.bitwise_xor(me, slots[0]) // len(slots) * cols
        there = out.at[f, :, pl.ds(pl.multiple_of(side, 128), cols)]
        copies.append(pltpu.make_async_copy(held.at[f], there, leaving.at[f]))
        copies[f].start()
    for copy in copies:
        copy.wait()


def to_partner(array, n, s):
    return array if s == 0 else lax.ppermute(array, "gy", [(i, i ^ s) for i in range(n)])


def exchange(arrays, n, slots):
    pairs = list(zip(arrays, slots))[::-1]
    return [to_partner(array, n, s) for array, s in pairs][::-1]


def on_device(rho, vel, temp, stress, heat):
    rows, cols = rho.shape
    n = lax.axis_size("gy")
    ring = lax.axis_size("gx")
    size, slab = n * rows, cols // n
    two = slab % 32 == 0
    core = slab // 2 if two else slab
    wide = core + 2 * HALO
    lane = min(rows, 128)
    half = jnp.bfloat16
    me = lax.axis_index("gy").astype(jnp.int32).reshape(1)
    vel, stress, heat = (jnp.swapaxes(a, 0, 1) for a in (vel, stress, heat))

    def message(width, kind=half):
        return jax.ShapeDtypeStruct((MOMENTS, width, rows), kind)

    far, near = (tuple(range(n // 2, n)), tuple(range(n // 2)))
    inputs = (rho, vel, temp, stress, heat)

    def pack(arrays):
        sent = (MOMENTS, (wide - 2 * SKIP) * (rows // lane), lane)
        shapes = [jax.ShapeDtypeStruct(sent, half)] * n if two else []
        shapes += [message(cols + 2 * HALO)]
        return pl.pallas_call(
            functools.partial(pack_kernel, n, two),
            out_shape=shapes,
            in_specs=[SMEM] + [HBM] * len(arrays),
            out_specs=[ANY] * len(shapes),
            scratch_shapes=[
                pltpu.VMEM((cols + 2 * HALO, rows), jnp.float32),
                pltpu.VMEM((MOMENTS, rows, cols), jnp.float32),
                pltpu.SemaphoreType.DMA((len(GROUPS),)),
            ]
            + [pltpu.VMEM(x.shape, x.dtype) for x in shapes]
            + [pltpu.SemaphoreType.DMA((len(shapes), len(GROUPS)))],
            compiler_params=params(56),
            cost_estimate=cost(2),
            name="pack",
        )(me, *arrays)

    firsts = []
    if two:
        *firsts, tall = pack(inputs)
        firsts = exchange(firsts, n, range(n))
    else:
        (tall,) = pack(inputs)

    def grid_of(slots, *ties):
        return pl.pallas_call(
            functools.partial(grid_kernel, n, rows, slots),
            out_shape=jax.ShapeDtypeStruct((size, len(slots) * rows), half),
            in_specs=[SMEM] + [ANY] * len(ties),
            out_specs=VMEM,
            scratch_shapes=[pltpu.VMEM((size, lane), jnp.float32)] * 4
            + [pltpu.VMEM((8, lane), jnp.float32)],
            compiler_params=params(24),
            cost_estimate=cost(1),
            name="grid",
        )(me, *ties)

    parts = (near[: n // 4], near[n // 4 :])
    grids = [grid_of(part) for part in parts]
    left, right = pl.pallas_call(
        edge_kernel,
        out_shape=[message(2 * HALO)] * 2,
        in_specs=[VMEM, ANY],
        out_specs=[VMEM] * 2,
        compiler_params=params(24),
        cost_estimate=cost(0.2),
        name="edges",
    )(tall, grids[0])
    up = [(i, (i + 1) % ring) for i in range(ring)]
    before = lax.ppermute(right, "gx", up)
    after = lax.ppermute(left, "gx", [(j, i) for i, j in up])
    turned = pl.pallas_call(
        functools.partial(flip_kernel, n, parts, far),
        out_shape=jax.ShapeDtypeStruct((size, len(far) * rows), half),
        in_specs=[VMEM] * 2,
        out_specs=VMEM,
        compiler_params=params(24),
        cost_estimate=cost(0.3),
        name="flip",
    )(*grids)
    all_parts, all_grids = (*parts, far), (*grids, turned)
    rests = pl.pallas_call(
        functools.partial(rest_kernel, n, two),
        out_shape=[message(core if two else wide)] * n,
        in_specs=[SMEM] + [VMEM] * 3,
        out_specs=[VMEM] * n,
        compiler_params=params(),
        cost_estimate=cost(0.2),
        name="rest",
    )(me, tall, before, after)
    rests = exchange(rests, n, range(n))

    def sections(second, *arrays):
        state = [
            jax.ShapeDtypeStruct((MOMENTS, wide, size), jnp.float32),
            jax.ShapeDtypeStruct((MOMENTS, core, size), jnp.float32),
            jax.ShapeDtypeStruct((MOMENTS * core, size), half),
        ]
        *crossing, u1, r0, fy1 = pl.pallas_call(
            functools.partial(section_kernel, n, two, second, far, all_parts),
            out_shape=[message(core)] * len(far) + state,
            in_specs=[SMEM] + [VMEM] * (len(arrays) + 3 - second) + [ANY] * second,
            out_specs=[VMEM] * (len(far) + 3),
            scratch_shapes=[
                pltpu.VMEM((MOMENTS, wide, size), jnp.float32),
                pltpu.VMEM((MOMENTS * wide, size), half),
                pltpu.VMEM((MOMENTS * wide, rows), jnp.float32),
                pltpu.VMEM((2 * MOMENTS, wide, lane), jnp.float32),
            ],
            compiler_params=params(24),
            cost_estimate=cost(6),
            name="sections",
        )(me, *all_grids, *arrays)
        return crossing, [u1, r0, fy1]

    def finished(states, *ties):
        thirds = [jax.ShapeDtypeStruct((end - first, slab, rows), half) for first, end in THIRDS]
        shapes = [message(slab, jnp.float32)] + thirds * (len(near) - 1)
        own, *others = pl.pallas_call(
            functools.partial(finish_kernel, n, near, parts, len(states) // 3),
            out_shape=shapes,
            in_specs=[SMEM] + [VMEM] * (len(states) + 2) + [ANY] * len(ties),
            out_specs=[VMEM] * len(shapes),
            scratch_shapes=[
                pltpu.VMEM((MOMENTS * core, rows), jnp.float32),
                pltpu.VMEM((2 * MOMENTS, wide, lane), jnp.float32),
            ],
            compiler_params=params(24),
            cost_estimate=cost(4),
            name="finish",
        )(me, *grids, *states, *ties)
        slots = [s for s in near[1:] for _ in THIRDS]
        return [own, *exchange(others, n, slots)]

    if two:
        firsts = far_first(firsts)
        crossing, states = sections(False, *firsts)
        back = exchange(crossing, n, far)
        crossing, more = sections(True, *firsts, *rests, crossing[0])
        staying = finished(states + more, *back)
        back += exchange(crossing, n, far)
    else:
        crossing, states = sections(False, *far_first(rests))
        staying = finished(states)
        back = exchange(crossing, n, far)
    chunks = 2 if two else 1
    token = jax.ShapeDtypeStruct((8, 128), jnp.float32)

    def unpack(slots, arrays, pieces, *before):
        alias = {1 + len(arrays): 0} if before else {}
        tokens = [] if before else [token]
        return pl.pallas_call(
            functools.partial(unpack_kernel, n, slots, chunks, pieces, tokens),
            out_shape=[jax.ShapeDtypeStruct((MOMENTS, rows, cols), jnp.float32), *tokens],
            in_specs=[SMEM] + [VMEM] * len(arrays) + [ANY] * len(before),
            out_specs=[ANY] + [VMEM] * len(tokens),
            scratch_shapes=[
                pltpu.VMEM((MOMENTS, cols // 2, rows), jnp.float32),
                pltpu.VMEM((MOMENTS, rows, cols // 2), jnp.float32),
                pltpu.SemaphoreType.DMA((MOMENTS,)),
            ],
            input_output_aliases=alias,
            compiler_params=params(24),
            cost_estimate=cost(0.01),
            name="unpack",
        )(me, *arrays, *before)

    pieces = [(0, None, 0, MOMENTS)] + [(s, None, *span) for s in near[1:] for span in THIRDS]
    out, turned_near = unpack(near, staying, tuple(pieces))
    arrived = pl.pallas_call(
        arrived_kernel,
        out_shape=token,
        in_specs=[ANY] * (len(back) + 1),
        out_specs=VMEM,
        compiler_params=params(1),
        cost_estimate=cost(6),
        name="arrived",
    )(*back, turned_near)
    pieces = [(s, c, 0, MOMENTS) for c in range(chunks) for s in far]
    (out,) = unpack(far, back, tuple(pieces), out, arrived)
    return jnp.swapaxes(out, 0, 1)


def solution(mesh):
    return jax.shard_map(
        on_device,
        mesh=mesh,
        in_specs=(
            P("gy", "gx"),
            P("gy", None, "gx"),
            P("gy", "gx"),
            P("gy", None, "gx"),
            P("gy", None, "gx"),
        ),
        out_specs=P("gy", None, "gx"),
        check_vma=False,
    )
```

```python
import functools
import math

import jax
import jax.numpy as jnp
from jax import lax
from jax.experimental import pallas as pl
from jax.experimental.pallas import tpu as pltpu
from jax.sharding import PartitionSpec as P

time_step = 0.05
enforcement_weight = 4.0
plate_speed = 0.5
dissipation_speed = 0.25
coeffs = (0.75, -0.15, 1.0 / 60.0)

MOMENTS = 13
HALO = 8
NEED = 6
SKIP = HALO - NEED
RHO, TEMP = 0, 4
VMEM = pl.BlockSpec(memory_space=pltpu.VMEM)
ANY = pl.BlockSpec(memory_space=pl.ANY)
HBM = pl.BlockSpec(memory_space=pltpu.HBM)
SMEM = pl.BlockSpec(memory_space=pltpu.SMEM)


def cost(micros):
    return pl.CostEstimate(
        flops=int(micros * 1e9), bytes_accessed=int(micros * 3e6), transcendentals=0
    )


def params(mib=48):
    return pltpu.CompilerParams(vmem_limit_bytes=mib * 2**20)


def code(f, x):
    if f == RHO:
        return x - 1.25
    if f == TEMP:
        return jnp.exp2(160.0 * (x - 1.25))
    return x


def decode(f, y):
    if f == RHO:
        return y + 1.25
    if f == TEMP:
        return jnp.log2(y) * (1.0 / 160.0) + 1.25
    return y


def flux(u, d, f):
    v = u[1 + d]
    temperature = u[4]
    heat = u[10:13]
    s = [[u[5], u[6], u[8]], [u[6], u[7], u[9]], [u[8], u[9], None]]
    if f == 0:
        return u[0] * v
    if f < 4:
        i = f - 1
        out = u[1 + i] * v + s[i][d]
        return out + temperature if i == d else out
    if f == 4:
        return v * temperature + 2.0 / 3.0 * heat[d]
    if f < 10:
        i, j = ((0, 0), (0, 1), (1, 1), (0, 2), (1, 2))[f - 5]
        out = v * s[i][j]
        weight = {}
        if j == d:
            weight[i] = weight.get(i, 0.0) + 0.4
        if i == d:
            weight[j] = weight.get(j, 0.0) + 0.4
        if i == j:
            weight[d] = weight.get(d, 0.0) - 4.0 / 15.0
        for k, w in weight.items():
            out = out + w * heat[k]
        return out
    i = f - 10
    out = v * heat[i] + temperature * s[i][d]
    return out + 2.5 * temperature * temperature if i == d else out


def sources(u, wall):
    near = jnp.abs(wall)
    nu = u[0] * jnp.sqrt(u[4] * u[4] + 0.25)
    heavy, light = -0.8 * nu, -0.55 * nu
    out = [None] * MOMENTS
    out[1] = -enforcement_weight * near * (u[1] - plate_speed * wall)
    out[4] = -dissipation_speed * nu * u[4] - enforcement_weight * near * (u[4] - 1.0)
    for f in range(5, 10):
        out[f] = heavy * u[f]
    for f in range(10, 13):
        out[f] = light * u[f]
    return out


def along_of(fx, turned, f):
    count = fx.shape[0] // 8
    turned[f] = fx
    x = [turned[f, pl.ds(v, 8, stride=count), :] for v in range(count)]
    x = [pltpu.roll(y, 1, 0) for y in x[-3:]] + x + [pltpu.roll(y, 7, 0) for y in x[:3]]
    for v in range(count):
        total = None
        for k in range(3):
            term = coeffs[k] * (x[3 + v + k + 1] - x[3 + v - k - 1])
            total = term if total is None else total + term
        turned[MOMENTS + f, pl.ds(v, 8, stride=count), :] = total
    return turned.at[MOMENTS + f]


def message_start(me, s, slab):
    to = jnp.bitwise_xor(me, s)
    return pl.multiple_of(to * slab + jnp.where(to % 2 == 0, slab // 2, 0), 16)


GROUPS = ((0, 1), (1, 4), (4, 5), (5, 8), (8, 10), (10, 12), (12, 13))


def pack_kernel(n, two, me_ref, *refs):
    (rho, vel, temp, stress, heat), refs = refs[:5], refs[5:]
    inputs = (rho, vel, temp, stress.at[0:3], stress.at[3:5], heat.at[0:2], heat.at[2:3])
    count = n if two else 0
    outs, (strip, given, arrived), refs = refs[: count + 1], refs[count + 1 : count + 4], refs[count + 4 :]
    held, left_at = refs[:-1], refs[-1]
    rows, cols = given.shape[1:]
    slab = cols // n
    me = me_ref[0]
    copies = []
    for k, (first, end) in enumerate(GROUPS):
        dst = given.at[first] if len(inputs[k].shape) == 2 else given.at[first:end]
        copies.append(pltpu.make_async_copy(inputs[k], dst, arrived.at[k]))
        copies[k].start()
    wide = slab // 2 + 2 * HALO
    lane = min(rows, 128)
    strip[0:HALO, :] = jnp.zeros((HALO, rows), jnp.float32)
    strip[HALO + cols :, :] = jnp.zeros((HALO, rows), jnp.float32)
    leaving = []
    done = 0
    for at, (first, end) in enumerate(GROUPS):
        copies[at].wait()
        for f in range(first, end):
            strip[HALO : HALO + cols, :] = code(f, given[f]).T
            for s in range(count):
                block = strip[pl.ds(message_start(me, s, slab), wide), :][SKIP : wide - SKIP]
                halves = [block[:, p : p + lane] for p in range(0, rows, lane)]
                held[s][f] = jnp.concatenate(halves, axis=0).astype(jnp.bfloat16)
            held[count][f] = strip[...].astype(jnp.bfloat16)
        if at > 0:
            span = pl.ds(done, end - done)
            for k, out in enumerate(outs):
                copy = pltpu.make_async_copy(held[k].at[span], out.at[span], left_at.at[k, at - 1])
                copy.start()
                leaving.append(copy)
            done = end
    for copy in leaving:
        copy.wait()


def edge_kernel(tall, tie, left, right):
    cols = tall.shape[1] - 2 * HALO
    left[...] = tall[:, 0 : 2 * HALO, :]
    right[...] = tall[:, cols : cols + 2 * HALO, :]


def rest_kernel(n, two, me_ref, tall, before, after, *outs):
    me = me_ref[0]
    slab = (tall.shape[1] - 2 * HALO) // n
    count = outs[0].shape[1]
    wide = slab // 2 + 2 * HALO if two else count
    line = lax.broadcasted_iota(jnp.int32, before.shape[1:], 0)
    for s in range(n):
        to = jnp.bitwise_xor(me, s)
        even = to % 2 == 0
        start = to * slab
        if two:
            start += jnp.where(even, 0, slab // 2)
        start = pl.multiple_of(start, 16)
        for f in range(MOMENTS):
            block = tall[f, pl.ds(start, wide), :].astype(jnp.float32)
            first, last = block[: 2 * HALO], block[wide - 2 * HALO :]
            first = jnp.where((line < HALO) & (to == 0), before[f].astype(jnp.float32), first)
            last = jnp.where((line >= HALO) & (to == n - 1), after[f].astype(jnp.float32), last)
            between = [block[2 * HALO : wide - 2 * HALO]] if wide > 4 * HALO else []
            block = jnp.concatenate([first, *between, last], axis=0)
            if two:
                near_end = block[SKIP : SKIP + count]
                far_end = block[wide - SKIP - count : wide - SKIP]
                block = jnp.where(even, near_end, far_end)
            outs[s][f] = block.astype(jnp.bfloat16)


def grid_kernel(n, rows, slots, me_ref, *refs):
    out, sin_col, cos_col, back_col, line_col, total = refs[-6:]
    size = n * rows
    last = size - 1
    half = math.pi / (2.0 * last)
    me = me_ref[0]
    step = 64
    lane = min(rows, 128)

    def table(s):
        line = jnp.bitwise_xor(me, s) * rows + lax.broadcasted_iota(jnp.int32, (8, rows), 1)
        angle = half * line.astype(jnp.float32)
        edge = (line == 0) | (line == last)
        sign = (1 - 2 * (line & 1)).astype(jnp.float32)
        return line.astype(jnp.float32), jnp.sin(angle), jnp.cos(angle), edge, sign

    def column(x):
        return jnp.broadcast_to(x[0:1], (lane, rows)).T

    for s in range(n):
        line, sine, cosine, edge, sign = table(s)
        here = pl.ds(s * rows, rows)
        line_col[here, :] = column(line)
        sin_col[here, :] = column(sine)
        cos_col[here, :] = column(cosine)
        back_col[here, :] = column(jnp.where(edge, 0.5 * sign, sign))

    for index, s in enumerate(slots):
        line, sine, cosine, edge, sign = table(s)
        front = (-math.pi / last) * sine * cosine * jnp.where(edge, 2.0 * sign, sign)
        for p in range(rows // lane):
            here = pl.ds(index * rows + p * lane, lane)
            own = pl.ds(s * rows + p * lane, lane)
            line_i, sin_i, cos_i, front_i = (
                x[0:1, p * lane : (p + 1) * lane] for x in (line, sine, cosine, front)
            )
            total[...] = jnp.zeros_like(total)

            def block(t, carry):
                down = pl.ds(pl.multiple_of(t * step, step), step)
                gap = line_i - line_col[down, :]
                same = gap == 0.0
                x = half * gap
                x2 = x * x
                poly = -1.0 / 39916800.0
                for c in (1 / 362880.0, -1 / 5040.0, 1 / 120.0, -1 / 6.0, 1.0):
                    poly = poly * x2 + c
                plus = sin_i * cos_col[down, :] + cos_i * sin_col[down, :]
                denom = jnp.where(same, 1.0, plus * (x * poly))
                off = jnp.where(same, 0.0, front_i * back_col[down, :] / denom)
                total[...] += jnp.sum(off.reshape(step // 8, 8, lane), axis=0)
                out[down, here] = off.astype(jnp.bfloat16)
                return carry

            lax.fori_loop(0, size // step, block, 0)
            diagonal = -jnp.sum(total[...], axis=0, keepdims=True)
            same = lax.broadcasted_iota(jnp.int32, (lane, lane), 0) == (
                lax.broadcasted_iota(jnp.int32, (lane, lane), 1)
            )
            tile = out[own, here].astype(jnp.float32)
            out[own, here] = jnp.where(same, diagonal, tile).astype(jnp.bfloat16)


def weights_of(parts, grids, s, down=slice(None)):
    for part, grid in zip(parts, grids):
        if s in part:
            rows = grid.shape[1] // len(part)
            at = part.index(s) * rows
            return grid[down, at : at + rows]


def flip_kernel(n, parts, far, *refs):
    grids, out = refs[: len(parts)], refs[-1]
    rows = out.shape[0] // n
    line = lax.broadcasted_iota(jnp.int32, (rows, rows), 0)
    turn = line + lax.broadcasted_iota(jnp.int32, (rows, rows), 1) == rows - 1
    turn = jnp.where(turn, 1.0, 0.0).astype(jnp.bfloat16)
    for k, s in enumerate(far):
        for a in range(n):
            down = (a ^ (n - 1)) * rows
            tile = weights_of(parts, grids, s ^ (n - 1), slice(down, down + rows))
            tile = jnp.dot(turn, tile, preferred_element_type=jnp.float32).astype(jnp.bfloat16)
            tile = -jnp.dot(tile, turn, preferred_element_type=jnp.float32)
            out[a * rows : (a + 1) * rows, k * rows : (k + 1) * rows] = tile.astype(jnp.bfloat16)


def far_first(arrays):
    half = len(arrays) // 2
    return [arrays[0], *arrays[half:][::-1], *arrays[1:half]]


def in_slots(arrays):
    half = len(arrays) // 2
    return [arrays[0], *arrays[half + 1 :], *arrays[1 : half + 1][::-1]]


def section_kernel(n, two, second, far, parts, me_ref, *refs):
    grids, refs = refs[: len(parts)], refs[len(parts) :]
    firsts, refs = in_slots(refs[:n]), refs[n:]
    if second:
        rests, refs = in_slots(refs[:n]), refs[n + 1 :]
    outs, refs = refs[: len(far)], refs[len(far) :]
    u1, r0, fy1, u0, fy0, product, turned = refs
    wide, size = u0.shape[1:]
    rows = size // n
    core = wide - 2 * HALO
    me = me_ref[0]
    right_first = me % 2 == 0
    lane = min(rows, 128)
    strips = rows // lane

    part = wide - 2 * SKIP
    lap = 2 * NEED
    for s in range(n):
        for f in range(MOMENTS):
            if not two:
                u0[f, :, pl.ds(s * rows, rows)] = decode(f, firsts[s][f].astype(jnp.float32))
                continue
            whole = decode(f, firsts[s][f].astype(jnp.float32))
            for p in range(strips):
                here = pl.ds(s * rows + p * lane, lane)
                first = whole[p * part : (p + 1) * part]
                u0[f, 0:8, here] = jnp.zeros((8, lane), jnp.float32)
                u0[f, wide - 8 :, here] = jnp.zeros((8, lane), jnp.float32)
                if not second:
                    u0[f, SKIP : SKIP + part, here] = first
                    continue
                new = rests[s][f, :, p * lane : (p + 1) * lane].astype(jnp.float32)
                new = decode(f, new)
                left = jnp.concatenate([new, first[:lap]], axis=0)
                right = jnp.concatenate([first[part - lap :], new], axis=0)
                u0[f, SKIP : SKIP + part, here] = jnp.where(right_first, left, right)

    for s in range(n):
        for p in range(strips):
            here = pl.ds(s * rows + p * lane, lane)
            u = [u0[f, :, here] for f in range(MOMENTS)]
            for f in range(MOMENTS):
                fy0[f * wide : (f + 1) * wide, here] = flux(u, 1, f).astype(jnp.bfloat16)

    middle = slice(HALO, HALO + core)
    for s in range(n):
        weights = weights_of(parts, grids, s)
        product[...] = jnp.dot(fy0[...], weights, preferred_element_type=jnp.float32)
        for p in range(strips):
            here = pl.ds(s * rows + p * lane, lane)
            there = pl.ds(p * lane, lane)
            u = [u0[f, :, here] for f in range(MOMENTS)]
            src = sources(u, walls(me, s, p, n, rows, wide))
            new = []
            for f in range(MOMENTS):
                across = product[f * wide : (f + 1) * wide, there]
                rate = -(along_of(flux(u, 0, f), turned, f)[...] + across)
                if src[f] is not None:
                    rate = rate + src[f]
                r0[f, :, here] = rate[middle]
                new.append(u[f] + time_step * rate)
                u1[f, :, here] = new[f]
            inner = [x[middle] for x in new]
            for f in range(MOMENTS):
                fy1[f * core : (f + 1) * core, here] = flux(inner, 1, f).astype(jnp.bfloat16)

    def place(s, f):
        return outs[far.index(s)].at[f]

    finish(n, far, me_ref, parts, grids, u1, r0, fy1, place, product, turned)


THIRDS = ((0, 5), (5, 9), (9, MOMENTS))


def finish_kernel(n, near, parts, chunks, me_ref, *refs):
    grids, refs = refs[: len(parts)], refs[len(parts) :]
    states, product, turned = refs[: 3 * chunks], *refs[-2:]
    outs = refs[-2 - 1 - len(THIRDS) * (len(near) - 1) : -2]
    core = outs[0].shape[1] // chunks

    def place(c, s, f):
        span = slice(c * core, (c + 1) * core)
        if s == 0:
            return outs[0].at[f, span]
        third = [first <= f < end for first, end in THIRDS].index(True)
        return outs[1 + len(THIRDS) * (s - 1) + third].at[f - THIRDS[third][0], span]

    for c in range(chunks):
        part = functools.partial(place, c)
        finish(n, near, me_ref, parts, grids, *states[3 * c : 3 * c + 3], part, product, turned)


def walls(me, s, p, n, rows, count):
    lane = min(rows, 128)
    line = jnp.bitwise_xor(me, s) * rows + p * lane
    line = line + lax.broadcasted_iota(jnp.int32, (count, lane), 1)
    return jnp.where(line == 0, 1.0, jnp.where(line == n * rows - 1, -1.0, 0.0))


def finish(n, slots, me_ref, parts, grids, u1, r0, fy1, outs, product, turned):
    wide, size = u1.shape[1:]
    rows = size // n
    core = wide - 2 * HALO
    lane = min(rows, 128)
    me = me_ref[0]
    middle = slice(HALO, HALO + core)
    for k, s in enumerate(slots):
        weights = weights_of(parts, grids, s)
        product[0 : MOMENTS * core, :] = jnp.dot(
            fy1[...], weights, preferred_element_type=jnp.float32
        )
        for p in range(rows // lane):
            here = pl.ds(s * rows + p * lane, lane)
            there = pl.ds(p * lane, lane)
            u = [u1[f, :, here] for f in range(MOMENTS)]
            inner = [x[middle] for x in u]
            src = sources(inner, walls(me, s, p, n, rows, core))
            for f in range(MOMENTS):
                across = product[f * core : (f + 1) * core, there]
                rate = -(along_of(flux(u, 0, f), turned, f)[middle, :] + across)
                if src[f] is not None:
                    rate = rate + src[f]
                rate = 0.5 * (r0[f, :, here] + rate)
                target = outs(s, f)
                target[:, there] = rate.astype(target.dtype)


def arrived_kernel(*refs):
    refs[-1][...] = jnp.zeros_like(refs[-1])


def unpack_kernel(n, slots, chunks, pieces, token, me_ref, *refs):
    out, tall, held, leaving = *refs[-4 - len(token) : -3 - len(token)], *refs[-3:]
    for ref in refs[-3 - len(token) : -3]:
        ref[...] = jnp.zeros_like(ref)
    rows, cols = held.shape[1:]
    slab = cols // len(slots)
    width = slab // chunks
    me = me_ref[0]
    copies = []
    for f in range(MOMENTS):
        for array, (s, c, first, end) in zip(refs, pieces):
            if not first <= f < end:
                continue
            of = jnp.bitwise_xor(me, s)
            for k in range(chunks) if c is None else (c,):
                start = of % len(slots) * slab
                if chunks == 2:
                    start += jnp.where(of % 2 == 0, width * (1 - k), width * k)
                here = pl.ds(pl.multiple_of(start, 16), width)
                piece = array[f - first, k * width : (k + 1) * width] if c is None else array[f]
                tall[f, here, :] = piece.astype(jnp.float32)
        held[f] = tall[f].T
        side = jnp.bitwise_xor(me, slots[0]) // len(slots) * cols
        there = out.at[f, :, pl.ds(pl.multiple_of(side, 128), cols)]
        copies.append(pltpu.make_async_copy(held.at[f], there, leaving.at[f]))
        copies[f].start()
    for copy in copies:
        copy.wait()


def to_partner(array, n, s):
    return array if s == 0 else lax.ppermute(array, "gy", [(i, i ^ s) for i in range(n)])


def exchange(arrays, n, slots):
    pairs = list(zip(arrays, slots))[::-1]
    return [to_partner(array, n, s) for array, s in pairs][::-1]


def on_device(rho, vel, temp, stress, heat):
    rows, cols = rho.shape
    n = lax.axis_size("gy")
    ring = lax.axis_size("gx")
    size, slab = n * rows, cols // n
    two = slab % 32 == 0
    core = slab // 2 if two else slab
    wide = core + 2 * HALO
    lane = min(rows, 128)
    half = jnp.bfloat16
    me = lax.axis_index("gy").astype(jnp.int32).reshape(1)
    vel, stress, heat = (jnp.swapaxes(a, 0, 1) for a in (vel, stress, heat))

    def message(width, kind=half):
        return jax.ShapeDtypeStruct((MOMENTS, width, rows), kind)

    far, near = (tuple(range(n // 2, n)), tuple(range(n // 2)))
    inputs = (rho, vel, temp, stress, heat)

    def pack(arrays):
        sent = (MOMENTS, (wide - 2 * SKIP) * (rows // lane), lane)
        shapes = [jax.ShapeDtypeStruct(sent, half)] * n if two else []
        shapes += [message(cols + 2 * HALO)]
        return pl.pallas_call(
            functools.partial(pack_kernel, n, two),
            out_shape=shapes,
            in_specs=[SMEM] + [HBM] * len(arrays),
            out_specs=[ANY] * len(shapes),
            scratch_shapes=[
                pltpu.VMEM((cols + 2 * HALO, rows), jnp.float32),
                pltpu.VMEM((MOMENTS, rows, cols), jnp.float32),
                pltpu.SemaphoreType.DMA((len(GROUPS),)),
            ]
            + [pltpu.VMEM(x.shape, x.dtype) for x in shapes]
            + [pltpu.SemaphoreType.DMA((len(shapes), len(GROUPS)))],
            compiler_params=params(56),
            cost_estimate=cost(2),
            name="pack",
        )(me, *arrays)

    firsts = []
    if two:
        *firsts, tall = pack(inputs)
        firsts = exchange(firsts, n, range(n))
    else:
        (tall,) = pack(inputs)

    def grid_of(slots, *ties):
        return pl.pallas_call(
            functools.partial(grid_kernel, n, rows, slots),
            out_shape=jax.ShapeDtypeStruct((size, len(slots) * rows), half),
            in_specs=[SMEM] + [ANY] * len(ties),
            out_specs=VMEM,
            scratch_shapes=[pltpu.VMEM((size, lane), jnp.float32)] * 4
            + [pltpu.VMEM((8, lane), jnp.float32)],
            compiler_params=params(24),
            cost_estimate=cost(1),
            name="grid",
        )(me, *ties)

    parts = (near[: n // 4], near[n // 4 :])
    grids = [grid_of(part) for part in parts]
    left, right = pl.pallas_call(
        edge_kernel,
        out_shape=[message(2 * HALO)] * 2,
        in_specs=[VMEM, ANY],
        out_specs=[VMEM] * 2,
        compiler_params=params(24),
        cost_estimate=cost(0.2),
        name="edges",
    )(tall, grids[0])
    up = [(i, (i + 1) % ring) for i in range(ring)]
    before = lax.ppermute(right, "gx", up)
    after = lax.ppermute(left, "gx", [(j, i) for i, j in up])
    turned = pl.pallas_call(
        functools.partial(flip_kernel, n, parts, far),
        out_shape=jax.ShapeDtypeStruct((size, len(far) * rows), half),
        in_specs=[VMEM] * 2,
        out_specs=VMEM,
        compiler_params=params(24),
        cost_estimate=cost(0.3),
        name="flip",
    )(*grids)
    all_parts, all_grids = (*parts, far), (*grids, turned)
    rests = pl.pallas_call(
        functools.partial(rest_kernel, n, two),
        out_shape=[message(core if two else wide)] * n,
        in_specs=[SMEM] + [VMEM] * 3,
        out_specs=[VMEM] * n,
        compiler_params=params(),
        cost_estimate=cost(0.2),
        name="rest",
    )(me, tall, before, after)
    rests = exchange(rests, n, range(n))

    def sections(second, *arrays):
        state = [
            jax.ShapeDtypeStruct((MOMENTS, wide, size), jnp.float32),
            jax.ShapeDtypeStruct((MOMENTS, core, size), jnp.float32),
            jax.ShapeDtypeStruct((MOMENTS * core, size), half),
        ]
        *crossing, u1, r0, fy1 = pl.pallas_call(
            functools.partial(section_kernel, n, two, second, far, all_parts),
            out_shape=[message(core)] * len(far) + state,
            in_specs=[SMEM] + [VMEM] * (len(arrays) + 3 - second) + [ANY] * second,
            out_specs=[VMEM] * (len(far) + 3),
            scratch_shapes=[
                pltpu.VMEM((MOMENTS, wide, size), jnp.float32),
                pltpu.VMEM((MOMENTS * wide, size), half),
                pltpu.VMEM((MOMENTS * wide, rows), jnp.float32),
                pltpu.VMEM((2 * MOMENTS, wide, lane), jnp.float32),
            ],
            compiler_params=params(24),
            cost_estimate=cost(6),
            name="sections",
        )(me, *all_grids, *arrays)
        return crossing, [u1, r0, fy1]

    def finished(states, *ties):
        thirds = [jax.ShapeDtypeStruct((end - first, slab, rows), half) for first, end in THIRDS]
        shapes = [message(slab, jnp.float32)] + thirds * (len(near) - 1)
        own, *others = pl.pallas_call(
            functools.partial(finish_kernel, n, near, parts, len(states) // 3),
            out_shape=shapes,
            in_specs=[SMEM] + [VMEM] * (len(states) + 2) + [ANY] * len(ties),
            out_specs=[VMEM] * len(shapes),
            scratch_shapes=[
                pltpu.VMEM((MOMENTS * core, rows), jnp.float32),
                pltpu.VMEM((2 * MOMENTS, wide, lane), jnp.float32),
            ],
            compiler_params=params(24),
            cost_estimate=cost(4),
            name="finish",
        )(me, *grids, *states, *ties)
        slots = [s for s in near[1:] for _ in THIRDS]
        return [own, *exchange(others, n, slots)]

    if two:
        firsts, rests = far_first(firsts), far_first(rests)
        crossing, states = sections(False, *firsts)
        back = exchange(crossing, n, far)
        crossing, more = sections(True, *firsts, *rests, crossing[0])
        staying = finished(states + more, *back)
        back += exchange(crossing, n, far)
    else:
        crossing, states = sections(False, *far_first(rests))
        staying = finished(states)
        back = exchange(crossing, n, far)
    chunks = 2 if two else 1
    token = jax.ShapeDtypeStruct((8, 128), jnp.float32)

    def unpack(slots, arrays, pieces, *before):
        alias = {1 + len(arrays): 0} if before else {}
        tokens = [] if before else [token]
        return pl.pallas_call(
            functools.partial(unpack_kernel, n, slots, chunks, pieces, tokens),
            out_shape=[jax.ShapeDtypeStruct((MOMENTS, rows, cols), jnp.float32), *tokens],
            in_specs=[SMEM] + [VMEM] * len(arrays) + [ANY] * len(before),
            out_specs=[ANY] + [VMEM] * len(tokens),
            scratch_shapes=[
                pltpu.VMEM((MOMENTS, cols // 2, rows), jnp.float32),
                pltpu.VMEM((MOMENTS, rows, cols // 2), jnp.float32),
                pltpu.SemaphoreType.DMA((MOMENTS,)),
            ],
            input_output_aliases=alias,
            compiler_params=params(24),
            cost_estimate=cost(0.01),
            name="unpack",
        )(me, *arrays, *before)

    pieces = [(0, None, 0, MOMENTS)] + [(s, None, *span) for s in near[1:] for span in THIRDS]
    out, turned_near = unpack(near, staying, tuple(pieces))
    arrived = pl.pallas_call(
        arrived_kernel,
        out_shape=token,
        in_specs=[ANY] * (len(back) + 1),
        out_specs=VMEM,
        compiler_params=params(1),
        cost_estimate=cost(6),
        name="arrived",
    )(*back, turned_near)
    pieces = [(s, c, 0, MOMENTS) for c in range(chunks) for s in far]
    (out,) = unpack(far, back, tuple(pieces), out, arrived)
    return jnp.swapaxes(out, 0, 1)


def solution(mesh):
    return jax.shard_map(
        on_device,
        mesh=mesh,
        in_specs=(
            P("gy", "gx"),
            P("gy", None, "gx"),
            P("gy", "gx"),
            P("gy", None, "gx"),
            P("gy", None, "gx"),
        ),
        out_specs=P("gy", None, "gx"),
        check_vma=False,
    )
```
